32 devices in a mesh: groups: 2 (over y), dp: 8 (over z, x), tensor: 2 (over core).
Axes of the slice: x: 2, y: 2, z: 4, core: 2. Of those that a mesh axis runs over, the one named last changes fastest.
Arguments:
- hidden_in: bfloat16 [4096, 12288], P(('groups', 'dp'), 'tensor'), parts along dimension 0
- norm_gain: bfloat16 [12288], P('tensor')
- projection: bfloat16 [2, 6144, 1024], P('tensor', 'dp')
- lengths: int32 [16, 2], P(('groups', 'dp')), parts along dimension 0, may hold values from 16 to 240, as said below
Outputs:
- context: bfloat16 [4096, 768], P(('groups', 'dp'), 'tensor'), parts along dimension 0
The draws below stay inside these ranges and needn't reach their ends.
There are 2 independent parts, one for each index of `groups`. The reference program is written for one: setup_inputs(seed, part) draws one part's arguments, and reference() takes and returns one part's arrays. A program takes and returns all parts, laid end to end along the dimension named above; an argument that names none is the same for every part. Nothing has to cross between parts.
Inputs may be any that keep to these rules, and one draw needn't show every extreme that they name: `lengths`: column 0 is the prompt length, at least 16 and at most 128; column 1 the response length; their sum is at most 256, and equals 256 in every rollout of even index.
All inputs are finite; a program needn't handle non-finite values.
Results may differ from the reference program's by a relative error of at most 0.017.
Values may be sent and summed in bfloat16 or wider, within the bound.
No kernel may reach another device: no remote copies, remote signals or barrier semaphores. Data moves between devices by JAX's collectives and lax.ppermute only.
A program may use at most 64 MiB of HBM per device.

```python
import math
import jax
import jax.numpy as jnp
from jax import lax

D = 12288
HEAD = 128
QHEADS = 6
LEN = 256
QKV = 1024
PAIR = 2
HALF_D = 6144
ROLLOUTS = 8
TOKENS = 2048


def draw_hidden_in(key, part):
    key = jax.random.fold_in(key, 11)
    first, second, third = jax.random.split(key, 3)
    row_scale = jnp.exp(jax.random.uniform(second, (TOKENS, 1), minval=0.0, maxval=math.log(10.0)))
    col_scale = jnp.exp(jax.random.uniform(third, (1, D), minval=0.0, maxval=math.log(4.0)))
    base = jax.random.normal(first, (TOKENS, D))
    return (base * row_scale * col_scale).astype(jnp.bfloat16)


def draw_norm_gain(key, part):
    key = jax.random.fold_in(key, 12)
    value = jnp.exp(jax.random.uniform(key, (D,), minval=-0.7, maxval=0.7))
    return value.astype(jnp.bfloat16)


def draw_projection(key, part):
    key = jax.random.fold_in(key, 14)
    first = jax.random.fold_in(key, 0)
    whole = jax.random.truncated_normal(first, -6.0, 6.0, (D, QKV)) / math.sqrt(D)
    return whole.reshape(PAIR, HALF_D, QKV).astype(jnp.bfloat16)


def draw_lengths(key, part):
    key = jax.random.fold_in(key, 13)
    first, second = jax.random.split(key)
    prompt = jax.random.randint(first, (ROLLOUTS,), LEN // 16, LEN // 2 + 1)
    index = jnp.arange(ROLLOUTS, dtype=jnp.int32)
    prompt = jnp.where(index == 0, LEN // 16, prompt)
    padding = jax.random.randint(second, (ROLLOUTS,), 0, LEN // 4 + 1)
    parity = index % 2
    padding = jnp.where(parity == 0, 0, padding)
    response = LEN - prompt - padding
    return jnp.stack([prompt, response], axis=1).astype(jnp.int32)


def setup_inputs(seed: int = 0, part: int = 0) -> dict:
    key_list = jax.random.split(jax.random.key(seed), 5)
    part_keys = jax.random.split(jax.random.fold_in(key_list[4], part), 5)
    hidden_in = draw_hidden_in(jax.random.fold_in(jax.random.fold_in(key_list[4], part), 71), part)
    norm_gain = draw_norm_gain(jax.random.fold_in(key_list[4], 71), part)
    projection = draw_projection(jax.random.fold_in(key_list[4], 71), part)
    lengths = draw_lengths(jax.random.fold_in(jax.random.fold_in(key_list[4], part), 71), part)
    return {"hidden_in": hidden_in, "norm_gain": norm_gain, "projection": projection, "lengths": lengths}


ROPE_BASE = 1000000.0
EPSILON = 1e-05

def rotate(block, positions):
    half = block.shape[-1] // 2
    freq = ROPE_BASE ** (-(jnp.arange(half, dtype=jnp.float32) * 2.0 / block.shape[-1]))
    angle = positions.astype(jnp.float32)[:, None] * freq[None, :]
    cosine = jnp.cos(angle)[:, None, :]
    sine = jnp.sin(angle)[:, None, :]
    first = block[..., :half]
    second = block[..., half:]
    return jnp.concatenate([first * cosine - second * sine, second * cosine + first * sine], axis=-1)

def attend(query_cols, key_value, length_pair, head_count):
    seq_len = query_cols.shape[0]
    positions = jnp.arange(seq_len, dtype=jnp.int32)
    queries = rotate(query_cols.reshape(seq_len, head_count, HEAD), positions).astype(jnp.bfloat16)
    keys = rotate(key_value[:, None, :HEAD], positions)[:, 0, :].astype(jnp.bfloat16)
    values = key_value[:, HEAD:].astype(jnp.bfloat16)
    scores = jnp.einsum('qhd,kd->hqk', queries.astype(jnp.float32), keys.astype(jnp.float32)) * HEAD ** (-0.5)
    total_len = length_pair[0] + length_pair[1]
    allowed = (positions[None, :] <= positions[:, None]) & (positions[None, :] < total_len)
    scores = jnp.where(allowed[None, :, :], scores, -1e+30)
    largest = lax.optimization_barrier(jnp.max(scores, axis=-1, keepdims=True))
    expo = jnp.exp(scores - largest)
    attn = (expo / lax.optimization_barrier(jnp.sum(expo, axis=-1, keepdims=True))).astype(jnp.bfloat16)
    mixed = jnp.einsum('hqk,kd->qhd', attn.astype(jnp.float32), values.astype(jnp.float32))
    keep = ((positions >= length_pair[0] - 1) & (positions < total_len - 1)).astype(jnp.float32)
    mixed = mixed * keep[:, None, None]
    return mixed.reshape(seq_len, head_count * HEAD).astype(jnp.bfloat16)

def reference(hidden_in, norm_gain, projection, lengths):
    gain32 = norm_gain.astype(jnp.float32)
    weight = projection.reshape(D, QKV)

    def one_rollout(item):
        hidden, length_pair = item
        wide32 = hidden.astype(jnp.float32)
        gated = (wide32 * gain32[None, :]).astype(jnp.bfloat16)
        inv_rms = lax.rsqrt(lax.optimization_barrier(jnp.mean(wide32 * wide32, axis=1)) + EPSILON)
        projected = jnp.dot(gated, weight, preferred_element_type=jnp.float32) * inv_rms[:, None]
        return attend(projected[:, :QHEADS * HEAD], projected[:, QHEADS * HEAD:], length_pair, QHEADS)
    stacked = hidden_in.reshape(ROLLOUTS, LEN, D)
    result = lax.map(one_rollout, (stacked, lengths))
    return result.reshape(TOKENS, QHEADS * HEAD)
```

```python
import jax
import jax.numpy as jnp
from jax import lax
from jax.sharding import PartitionSpec as P

D = 12288
HEAD = 128
QHEADS = 6
ROPE_BASE = 1000000.0
EPSILON = 1e-05


def tables(seq_len):
    half = HEAD // 2
    positions = jnp.arange(seq_len, dtype=jnp.int32)
    freq = ROPE_BASE ** (-(jnp.arange(half, dtype=jnp.float32) * 2.0 / HEAD))
    angle = positions.astype(jnp.float32)[:, None] * freq[None, :]
    return jnp.cos(angle), jnp.sin(angle)


def rotate(block, cosine, sine):
    half = HEAD // 2
    first = block[:, :half]
    second = block[:, half:]
    return jnp.concatenate([first * cosine - second * sine, second * cosine + first * sine], axis=-1)


def attend_head(query, keys, values, allowed, keep):
    scores = lax.dot_general(
        query, keys, (((1,), (1,)), ((), ())), preferred_element_type=jnp.float32
    ) * HEAD ** (-0.5)
    scores = jnp.where(allowed, scores, -1e30)
    largest = jnp.max(scores, axis=-1, keepdims=True)
    expo = jnp.exp(scores - largest)
    attn = (expo / jnp.sum(expo, axis=-1, keepdims=True)).astype(jnp.bfloat16)
    mixed = jnp.dot(attn, values, preferred_element_type=jnp.float32)
    return (mixed * keep).astype(jnp.bfloat16)


def swap(size):
    return [(i, i ^ 1) for i in range(size)]


def local(hidden_in, norm_gain, projection, lengths):
    groups = lax.axis_size("groups")
    dp = lax.axis_size("dp")
    tensor = lax.axis_size("tensor")
    y = lax.axis_index("groups")
    place = lax.axis_index("dp")
    core = lax.axis_index("tensor")
    x = place % 2
    z = place // 2
    depth = dp // 2
    tokens = hidden_in.shape[0]
    rows = projection.shape[1]
    part = rows // groups
    heads_local = QHEADS // tensor

    ring = [(i, (i + 2) % dp) for i in range(dp)]
    over_x = swap(dp)
    over_y = swap(groups)
    over_core = swap(tensor)
    across = [(g * dp + i, (g ^ 1) * dp + (i ^ 1)) for g in range(groups) for i in range(dp)]

    mine = lax.dynamic_slice_in_dim(projection[0], y * part, part, 0)

    def column(owner, index):
        start = (QHEADS + owner) * HEAD if index == 0 else (owner * heads_local + index - 1) * HEAD
        return lax.dynamic_slice_in_dim(mine, start, HEAD, 1)

    n_cols = heads_local + 1
    theirs = jnp.concatenate([column(1 - core, i) for i in range(n_cols)], axis=1)
    other = lax.ppermute(theirs, "tensor", over_core)
    weights = []
    for i in range(n_cols):
        slot = jnp.concatenate([column(core, i), other[:, i * HEAD:(i + 1) * HEAD]], axis=0)
        weights.append([slot])
    for _ in range(depth - 1):
        for i in range(n_cols):
            weights[i].append(lax.ppermute(weights[i][-1], "dp", ring))

    wide32 = hidden_in.astype(jnp.float32)
    gated = (wide32 * norm_gain.astype(jnp.float32)[None, :]).astype(jnp.bfloat16)
    local_sq = jnp.sum(wide32 * wide32, axis=1)
    total_sq = local_sq + lax.ppermute(local_sq, "tensor", over_core)
    inv_rms = lax.rsqrt(total_sq / D + EPSILON)[:, None]

    def piece(dx, dy):
        slabs = []
        for k in range(depth):
            shard = ((z - k + depth) % depth) * 2 + (x ^ dx)
            slabs.append(lax.dynamic_slice_in_dim(gated, shard * rows + (y ^ dy) * part, part, 1))
        return jnp.stack(slabs)

    sent = [piece(1, 1), piece(1, 0), piece(0, 1)]
    held = [
        lax.ppermute(sent[0], ("groups", "dp"), across),
        lax.ppermute(sent[1], "dp", over_x),
        lax.ppermute(sent[2], "groups", over_y),
        piece(0, 0),
    ]
    acts = []
    for h in held:
        acts.append(jnp.concatenate([h, lax.ppermute(h, "tensor", over_core)], axis=2))
    acts = jnp.concatenate(acts, axis=1)

    cosine, sine = tables(tokens)
    positions = jnp.arange(tokens, dtype=jnp.int32)
    prompt = lengths[0, 0]
    total_len = prompt + lengths[0, 1]
    allowed = (positions[None, :] <= positions[:, None]) & (positions[None, :] < total_len)
    keep = ((positions >= prompt - 1) & (positions < total_len - 1)).astype(jnp.float32)[:, None]

    outs = []
    keys = values = None
    for i in range(n_cols):
        partial = sum(
            jnp.dot(acts[k], weights[i][k], preferred_element_type=jnp.float32) for k in range(depth)
        )
        blocks = partial.reshape(4, tokens, HEAD)
        low = blocks[:3].astype(jnp.bfloat16)
        summed = blocks[3]
        summed = summed + lax.ppermute(low[0], ("groups", "dp"), across).astype(jnp.float32)
        summed = summed + lax.ppermute(low[1], "dp", over_x).astype(jnp.float32)
        summed = summed + lax.ppermute(low[2], "groups", over_y).astype(jnp.float32)
        scaled = summed * inv_rms
        if i == 0:
            turned = rotate(scaled, cosine, sine)
            kv = jnp.where(core == 0, turned, scaled).astype(jnp.bfloat16)
            vk = lax.ppermute(kv, "tensor", over_core)
            keys = jnp.where(core == 0, kv, vk)
            values = jnp.where(core == 0, vk, kv)
        else:
            query = rotate(scaled, cosine, sine).astype(jnp.bfloat16)
            outs.append(attend_head(query, keys, values, allowed, keep))
    return jnp.concatenate(outs, axis=1)


def solution(mesh):
    in_specs = (
        P(("groups", "dp"), "tensor"),
        P("tensor"),
        P("tensor", "dp", None),
        P(("groups", "dp"), None),
    )
    out_specs = P(("groups", "dp"), "tensor")
    return jax.shard_map(local, mesh=mesh, in_specs=in_specs, out_specs=out_specs, check_vma=False)
```

```python
import functools

import jax
import jax.numpy as jnp
from jax import lax
from jax.experimental import pallas as pl
from jax.experimental.pallas import tpu as pltpu
from jax.sharding import PartitionSpec as P

D = 12288
HEAD = 128
QHEADS = 6
ROPE_BASE = 1000000.0
EPSILON = 1e-05


def tables(seq_len):
    half = HEAD // 2
    positions = jnp.arange(seq_len, dtype=jnp.int32)
    freq = ROPE_BASE ** (-(jnp.arange(half, dtype=jnp.float32) * 2.0 / HEAD))
    angle = positions.astype(jnp.float32)[:, None] * freq[None, :]
    return jnp.cos(angle), jnp.sin(angle)


def rotate(block, cosine, sine):
    half = HEAD // 2
    first = block[:, :half]
    second = block[:, half:]
    return jnp.concatenate([first * cosine - second * sine, second * cosine + first * sine], axis=-1)


def attend_head(query, keys, values, allowed, keep):
    scores = lax.dot_general(
        query, keys, (((1,), (1,)), ((), ())), preferred_element_type=jnp.float32
    ) * HEAD ** (-0.5)
    scores = jnp.where(allowed, scores, -1e30)
    largest = jnp.max(scores, axis=-1, keepdims=True)
    expo = jnp.exp(scores - largest)
    attn = (expo / jnp.sum(expo, axis=-1, keepdims=True)).astype(jnp.bfloat16)
    mixed = jnp.dot(attn, values, preferred_element_type=jnp.float32)
    return (mixed * keep).astype(jnp.bfloat16)


def swap(size):
    return [(i, i ^ 1) for i in range(size)]


def general(hidden_in, norm_gain, projection, lengths):
    groups = lax.axis_size("groups")
    dp = lax.axis_size("dp")
    tensor = lax.axis_size("tensor")
    y = lax.axis_index("groups")
    place = lax.axis_index("dp")
    core = lax.axis_index("tensor")
    x = place % 2
    z = place // 2
    depth = dp // 2
    tokens = hidden_in.shape[0]
    rows = projection.shape[1]
    part = rows // groups
    heads_local = QHEADS // tensor

    ring = [(i, (i + 2) % dp) for i in range(dp)]
    over_x = swap(dp)
    over_y = swap(groups)
    over_core = swap(tensor)
    across = [(g * dp + i, (g ^ 1) * dp + (i ^ 1)) for g in range(groups) for i in range(dp)]

    mine = lax.dynamic_slice_in_dim(projection[0], y * part, part, 0)

    def column(owner, index):
        start = (QHEADS + owner) * HEAD if index == 0 else (owner * heads_local + index - 1) * HEAD
        return lax.dynamic_slice_in_dim(mine, start, HEAD, 1)

    n_cols = heads_local + 1
    theirs = jnp.concatenate([column(1 - core, i) for i in range(n_cols)], axis=1)
    other = lax.ppermute(theirs, "tensor", over_core)
    weights = []
    for i in range(n_cols):
        slot = jnp.concatenate([column(core, i), other[:, i * HEAD:(i + 1) * HEAD]], axis=0)
        weights.append([slot])
    for _ in range(depth - 1):
        for i in range(n_cols):
            weights[i].append(lax.ppermute(weights[i][-1], "dp", ring))

    wide32 = hidden_in.astype(jnp.float32)
    gated = (wide32 * norm_gain.astype(jnp.float32)[None, :]).astype(jnp.bfloat16)
    local_sq = jnp.sum(wide32 * wide32, axis=1)
    total_sq = local_sq + lax.ppermute(local_sq, "tensor", over_core)
    inv_rms = lax.rsqrt(total_sq / D + EPSILON)[:, None]

    def piece(dx, dy):
        slabs = []
        for k in range(depth):
            shard = ((z - k + depth) % depth) * 2 + (x ^ dx)
            slabs.append(lax.dynamic_slice_in_dim(gated, shard * rows + (y ^ dy) * part, part, 1))
        return jnp.stack(slabs)

    sent = [piece(1, 1), piece(1, 0), piece(0, 1)]
    held = [
        lax.ppermute(sent[0], ("groups", "dp"), across),
        lax.ppermute(sent[1], "dp", over_x),
        lax.ppermute(sent[2], "groups", over_y),
        piece(0, 0),
    ]
    acts = []
    for h in held:
        acts.append(jnp.concatenate([h, lax.ppermute(h, "tensor", over_core)], axis=2))
    acts = jnp.concatenate(acts, axis=1)

    cosine, sine = tables(tokens)
    positions = jnp.arange(tokens, dtype=jnp.int32)
    prompt = lengths[0, 0]
    total_len = prompt + lengths[0, 1]
    allowed = (positions[None, :] <= positions[:, None]) & (positions[None, :] < total_len)
    keep = ((positions >= prompt - 1) & (positions < total_len - 1)).astype(jnp.float32)[:, None]

    outs = []
    keys = values = None
    for i in range(n_cols):
        partial = sum(
            jnp.dot(acts[k], weights[i][k], preferred_element_type=jnp.float32) for k in range(depth)
        )
        blocks = partial.reshape(4, tokens, HEAD)
        low = blocks[:3].astype(jnp.bfloat16)
        summed = blocks[3]
        summed = summed + lax.ppermute(low[0], ("groups", "dp"), across).astype(jnp.float32)
        summed = summed + lax.ppermute(low[1], "dp", over_x).astype(jnp.float32)
        summed = summed + lax.ppermute(low[2], "groups", over_y).astype(jnp.float32)
        scaled = summed * inv_rms
        if i == 0:
            turned = rotate(scaled, cosine, sine)
            kv = jnp.where(core == 0, turned, scaled).astype(jnp.bfloat16)
            vk = lax.ppermute(kv, "tensor", over_core)
            keys = jnp.where(core == 0, kv, vk)
            values = jnp.where(core == 0, vk, kv)
        else:
            query = rotate(scaled, cosine, sine).astype(jnp.bfloat16)
            outs.append(attend_head(query, keys, values, allowed, keep))
    return jnp.concatenate(outs, axis=1)


VMEM = pltpu.VMEM
PLANE = ((1, 1), (1, 0), (0, 1), (0, 0))
WHOLE = pl.BlockSpec(memory_space=VMEM)
SCALARS = pl.BlockSpec(memory_space=pltpu.SMEM)


def call(kernel, out_shape, limit=12, **kwargs):
    return pl.pallas_call(
        kernel,
        out_shape=out_shape,
        compiler_params=pltpu.CompilerParams(vmem_limit_bytes=limit * 2**20),
        cost_estimate=pl.CostEstimate(flops=1, bytes_accessed=1, transcendentals=0),
        **kwargs,
    )


def select_kernel(columns, part, place_ref, rows_ref, *refs):
    out_refs, sems = refs[:len(columns)], refs[len(columns)]
    rows = pl.ds(pl.multiple_of(place_ref[2] * part, HEAD), part)
    copies = []
    for starts, out_ref in zip(columns, out_refs):
        for i, start in enumerate(starts):
            copies.append(pltpu.make_async_copy(
                rows_ref.at[0, rows, pl.ds(start, HEAD)],
                out_ref.at[:, pl.ds(i * HEAD, HEAD)],
                sems.at[len(copies)],
            ))
    for copy in copies:
        copy.start()
    for copy in copies:
        copy.wait()


def select(place, projection, part, columns):
    chunk = jax.ShapeDtypeStruct((part, len(columns[0]) * HEAD), projection.dtype)
    return call(
        functools.partial(select_kernel, columns, part),
        (chunk,) * len(columns),
        in_specs=[SCALARS, pl.BlockSpec(memory_space=pltpu.HBM)],
        out_specs=[pl.BlockSpec(memory_space=pl.ANY)] * len(columns),
        scratch_shapes=[pltpu.SemaphoreType.DMA((len(columns) * len(columns[0]),))],
    )(place, pltpu.with_memory_space_constraint(projection, pltpu.HBM))


def gate_kernel(part, depth, place_ref, hidden_ref, gain_ref, *out_refs):
    piece_refs, sq_ref, row_ref = out_refs[:4], out_refs[4], out_refs[5]
    x, y = place_ref[1], place_ref[2]
    base = lax.rem(place_ref[0] - pl.program_id(0) + depth, depth) * 4 * part

    @pl.when(pl.program_id(0) == 0)
    def _():
        row_ref[0, :] = gain_ref[...].astype(jnp.float32)

    total = jnp.zeros(sq_ref.shape, jnp.float32)
    for piece_ref, (dx, dy) in zip(piece_refs, PLANE):
        start = pl.multiple_of(((x ^ dx) * 2 + (y ^ dy)) * part, HEAD)
        wide = hidden_ref[:, pl.ds(start, part)].astype(jnp.float32)
        gain = row_ref[:, pl.ds(pl.multiple_of(base + start, HEAD), part)]
        piece_ref[0] = (wide * gain).astype(jnp.bfloat16)
        square = wide * wide
        for j in range(0, part, HEAD):
            total += square[:, j:j + HEAD]

    @pl.when(pl.program_id(0) == 0)
    def _():
        sq_ref[...] = total

    @pl.when(pl.program_id(0) > 0)
    def _():
        sq_ref[...] += total


def gate(place, hidden_in, norm_gain, part, depth):
    tokens = hidden_in.shape[0]
    wide = 4 * part
    piece = jax.ShapeDtypeStruct((depth, tokens, part), jnp.bfloat16)

    def shard(k, place):
        return (0, lax.rem(place[0] - k + depth, depth))

    outs = call(
        functools.partial(gate_kernel, part, depth),
        (piece,) * 4 + (jax.ShapeDtypeStruct((tokens, HEAD), jnp.float32),),
        grid_spec=pltpu.PrefetchScalarGridSpec(
            num_scalar_prefetch=1,
            grid=(depth,),
            in_specs=[pl.BlockSpec((tokens, wide), shard), pl.BlockSpec(norm_gain.shape, lambda k, place: (0,))],
            out_specs=[pl.BlockSpec((1, tokens, part), lambda k, place: (k, 0, 0))] * 4
            + [pl.BlockSpec((tokens, HEAD), lambda k, place: (0, 0))],
            scratch_shapes=[pltpu.VMEM((1, norm_gain.shape[0]), jnp.float32)],
        ),
    )(place, hidden_in, norm_gain)
    return outs[:4], outs[4]


def matmul_kernel(firsts, n_blocks, more, sent, place_ref, *refs):
    n_slots = len(firsts)
    acts, refs = refs[:4], refs[4:]
    slots, refs = refs[:n_slots], refs[n_slots:]
    right = [slot[...] for slot in slots]
    wide = 2 * HEAD
    for p in range(4):
        total = jnp.dot(acts[p][firsts[0]], right[0], preferred_element_type=jnp.float32)
        for k in range(1, n_slots):
            total += jnp.dot(acts[p][firsts[k]], right[k], preferred_element_type=jnp.float32)
        if more:
            total += refs[0][p]
        if not sent:
            refs[-1][p] = total
            continue
        mine_ref = refs[-1]
        theirs_refs = refs[-1 - sent:-1]
        per = 4 * n_blocks // sent
        for g in range(n_blocks):
            low = total[:, g * wide:g * wide + HEAD]
            high = total[:, g * wide + HEAD:(g + 1) * wide]
            spot = g * 4 + p
            theirs_refs[spot // per][spot % per] = jnp.where(place_ref[3] == 0, high, low).astype(jnp.bfloat16)
            mine_ref[p, g] = jnp.where(place_ref[3] == 0, low, high)


def matmul(place, acts, slots, firsts, so_far=None, sent=0):
    n_slots, n_blocks = len(slots), slots[0].shape[1] // (2 * HEAD)
    tokens = acts[0].shape[1]
    args = [place, *acts, *slots]
    if so_far is not None:
        args.append(so_far)
    if sent:
        out_shape = (jax.ShapeDtypeStruct((4 * n_blocks // sent, tokens, HEAD), jnp.bfloat16),) * sent
        out_shape += (jax.ShapeDtypeStruct((4, n_blocks, tokens, HEAD), jnp.float32),)
    else:
        out_shape = (jax.ShapeDtypeStruct((4, tokens, n_blocks * 2 * HEAD), jnp.float32),)
    outs = call(
        functools.partial(matmul_kernel, firsts, n_blocks, so_far is not None, sent),
        out_shape,
        in_specs=[SCALARS] + [WHOLE] * (len(args) - 1),
        out_specs=[WHOLE] * len(out_shape),
    )(*args)
    return outs if sent else outs[0]


def join_kernel(mine_ref, *refs):
    n_blocks = mine_ref.shape[1]
    came_refs, out_refs = refs[:-4], refs[-4:]
    per = 4 * n_blocks // len(came_refs)
    for p in range(4):
        for g in range(n_blocks):
            spot = g * 4 + p
            came = came_refs[spot // per][spot % per].astype(jnp.float32)
            out_refs[p][g] = (mine_ref[p, g] + came).astype(out_refs[p].dtype)


def join(mine, *came):
    shape = mine.shape[1:]
    return call(
        join_kernel,
        (jax.ShapeDtypeStruct(shape, jnp.bfloat16),) * 3 + (jax.ShapeDtypeStruct(shape, jnp.float32),),
        in_specs=[WHOLE] * (1 + len(came)),
        out_specs=[WHOLE] * 4,
    )(mine, *came)


def summed(refs, index, scale_ref):
    total = refs[0][index]
    for ref in refs[1:]:
        total += ref[index].astype(jnp.float32)
    return total * scale_ref[...]


def turned(block, cosine_ref, sine_ref):
    half = HEAD // 2
    other = jnp.concatenate([block[:, half:], block[:, :half]], axis=1)
    return block * cosine_ref[...] + other * sine_ref[...]


def kv_kernel(place_ref, own, r0, r1, r2, scale_ref, cosine_ref, sine_ref, out_ref):
    block = summed((own, r0, r1, r2), 0, scale_ref)
    spun = turned(block, cosine_ref, sine_ref)
    out_ref[...] = jnp.where(place_ref[3] == 0, spun, block).astype(jnp.bfloat16)


def heads_kernel(first, n_parts, place_ref, lengths_ref, *refs):
    parts, refs = refs[:n_parts], refs[n_parts:]
    scale_ref, cosine_ref, sine_ref, mine_ref, other_ref, *rest = refs
    out_ref = rest[-1]
    tokens = mine_ref.shape[0]
    is_key = place_ref[3] == 0
    mine, other = mine_ref[...], other_ref[...]
    keys = jnp.where(is_key, mine, other)
    values = jnp.where(is_key, other, mine)
    prompt = lengths_ref[0, 0]
    total_len = prompt + lengths_ref[0, 1]
    at = lax.broadcasted_iota(jnp.int32, (tokens, tokens), 0)
    key_at = lax.broadcasted_iota(jnp.int32, (tokens, tokens), 1)
    allowed = (key_at <= at) & (key_at < total_len)
    row = lax.broadcasted_iota(jnp.int32, (tokens, HEAD), 0)
    keep = ((row >= prompt - 1) & (row < total_len - 1)).astype(jnp.float32)
    before = 0
    if len(rest) > 1:
        before = rest[0].shape[1]
        out_ref[:, :before] = rest[0][...]
    for i in range(first, parts[0].shape[0]):
        query = turned(summed(parts, i, scale_ref), cosine_ref, sine_ref).astype(jnp.bfloat16)
        scores = lax.dot_general(
            query, keys, (((1,), (1,)), ((), ())), preferred_element_type=jnp.float32
        ) * HEAD ** (-0.5)
        scores = jnp.where(allowed, scores, -1e30)
        expo = jnp.exp(scores - jnp.max(scores, axis=-1, keepdims=True))
        attn = (expo / jnp.sum(expo, axis=-1, keepdims=True)).astype(jnp.bfloat16)
        mixed = jnp.dot(attn, values, preferred_element_type=jnp.float32)
        out_ref[:, before + (i - first) * HEAD:before + (i - first + 1) * HEAD] = (mixed * keep).astype(jnp.bfloat16)


def heads(place, lengths, parts, first, scale, cosine, sine, mine, other, *earlier):
    tokens = mine.shape[0]
    args = [place, lengths, *parts, scale, cosine, sine, mine, other, *earlier]
    width = (parts[0].shape[0] - first) * HEAD + sum(e.shape[1] for e in earlier)
    return call(
        functools.partial(heads_kernel, first, len(parts)),
        jax.ShapeDtypeStruct((tokens, width), jnp.bfloat16),
        in_specs=[SCALARS] * 2 + [WHOLE] * (len(args) - 2),
        out_specs=WHOLE,
    )(*args)


def staged(hidden_in, norm_gain, projection, lengths):
    groups = lax.axis_size("groups")
    dp = lax.axis_size("dp")
    tensor = lax.axis_size("tensor")
    y = lax.axis_index("groups")
    spot = lax.axis_index("dp")
    core = lax.axis_index("tensor")
    place = jnp.stack([spot // 2, spot % 2, y, core]).astype(jnp.int32)
    depth = dp // 2
    tokens = hidden_in.shape[0]
    part = projection.shape[1] // groups
    heads_local = QHEADS // tensor

    ring = [(i, (i + 2) % dp) for i in range(dp)]
    over_x = swap(dp)
    over_y = swap(groups)
    over_core = swap(tensor)
    across = [(g * dp + i, (g ^ 1) * dp + (i ^ 1)) for g in range(groups) for i in range(dp)]

    def to_core(a):
        return lax.ppermute(a, "tensor", over_core)

    def on_ring(a):
        return lax.ppermute(a, "dp", ring)

    def back(a):
        return lax.ppermute(a, "dp", [(j, i) for i, j in ring])

    def to_plane(three):
        return [
            lax.ppermute(three[0], ("groups", "dp"), across),
            lax.ppermute(three[1], "dp", over_x),
            lax.ppermute(three[2], "groups", over_y),
        ]

    last = []

    def after(*values):
        held = lax.optimization_barrier(tuple(values) + tuple(last))[:len(values)]
        last[:] = held[:1]
        return held[0] if len(values) == 1 else held

    blocks = [[(QHEADS + c) * HEAD for c in range(tensor)]]
    blocks += [[(c * heads_local + i) * HEAD for c in range(tensor)] for i in range(heads_local)]
    columns = [blocks[0] + blocks[1], blocks[2] + blocks[3]]
    own_a, own_b = after(*select(place, projection, part, columns))
    a1 = on_ring(own_a)
    a3 = back(own_a)
    pieces, squares = gate(place, after(hidden_in), norm_gain, part, depth)
    pieces, squares = list(after(*pieces)), after(squares)
    came = to_plane(pieces[:3])

    a1 = after(a1)
    a2 = on_ring(a1)
    a3, own_b = after(a3, own_b)
    b1 = on_ring(own_b)
    a2, own_b = after(a2, own_b)
    b3 = back(own_b)
    b1 = after(b1)
    b2 = on_ring(b1)
    acts = list(after(*came)) + [pieces[3]]
    b3 = after(b3)
    *theirs, mine = after(*matmul(place, acts, (own_a, a1, a2, a3), (0, 1, 2, 3), sent=4))
    swapped = after(*[to_core(t) for t in theirs])
    *sent, own = after(*join(mine, *swapped))
    first_parts = [own] + to_plane(sent)
    front = after(matmul(place, acts, (own_b, b1, b3), (0, 1, 3)))

    b2 = after(b2)
    *theirs, mine = after(*matmul(place, acts, (b2,), (2,), so_far=front, sent=2))
    swapped = [to_core(t) for t in theirs]
    first_parts = after(*first_parts)
    squares = after(squares)
    squares = squares + to_core(squares)
    scale = lax.rsqrt(jnp.sum(squares, axis=1, keepdims=True) / D + EPSILON)
    cosine, sine = tables(tokens)
    cosine = jnp.concatenate([cosine, cosine], axis=1)
    sine = jnp.concatenate([-sine, sine], axis=1)
    scale, cosine, sine = after(scale, cosine, sine)
    kv = after(call(
        kv_kernel,
        jax.ShapeDtypeStruct((tokens, HEAD), jnp.bfloat16),
        in_specs=[SCALARS] + [WHOLE] * 7,
        out_specs=WHOLE,
    )(place, *first_parts, scale, cosine, sine))
    vk = to_core(kv)
    *sent, own = after(*join(mine, *after(*swapped)))
    parts = [own] + to_plane(sent)
    vk = after(vk)
    one = after(heads(place, lengths, first_parts, 1, scale, cosine, sine, kv, vk))
    return heads(place, lengths, after(*parts), 0, scale, cosine, sine, kv, vk, one)


def local(hidden_in, norm_gain, projection, lengths):
    part = projection.shape[1] // lax.axis_size("groups")
    if lax.axis_size("dp") == 8 and part % HEAD == 0:
        return staged(hidden_in, norm_gain, projection, lengths)
    return general(hidden_in, norm_gain, projection, lengths)


def solution(mesh):
    in_specs = (
        P(("groups", "dp"), "tensor"),
        P("tensor"),
        P("tensor", "dp", None),
        P(("groups", "dp"), None),
    )
    out_specs = P(("groups", "dp"), "tensor")
    return jax.shard_map(local, mesh=mesh, in_specs=in_specs, out_specs=out_specs, check_vma=False)
```

```python
import functools
import math

import jax
import jax.numpy as jnp
from jax import lax
from jax.experimental import pallas as pl
from jax.experimental.pallas import tpu as pltpu
from jax.sharding import PartitionSpec as P

D = 12288
HEAD = 128
QHEADS = 6
ROPE_BASE = 1000000.0
EPSILON = 1e-05


def angles(seq_len):
    half = HEAD // 2
    positions = jnp.arange(seq_len, dtype=jnp.int32)
    freq = ROPE_BASE ** (-(jnp.arange(half, dtype=jnp.float32) * 2.0 / HEAD))
    angle = positions.astype(jnp.float32)[:, None] * freq[None, :]
    return jnp.cos(angle), jnp.sin(angle)


def rotate(block, cosine, sine):
    half = HEAD // 2
    first = block[:, :half]
    second = block[:, half:]
    return jnp.concatenate([first * cosine - second * sine, second * cosine + first * sine], axis=-1)


def attend_head(query, keys, values, allowed, keep):
    scores = lax.dot_general(
        query, keys, (((1,), (1,)), ((), ())), preferred_element_type=jnp.float32
    ) * HEAD ** (-0.5)
    scores = jnp.where(allowed, scores, -1e30)
    largest = jnp.max(scores, axis=-1, keepdims=True)
    expo = jnp.exp(scores - largest)
    attn = (expo / jnp.sum(expo, axis=-1, keepdims=True)).astype(jnp.bfloat16)
    mixed = jnp.dot(attn, values, preferred_element_type=jnp.float32)
    return (mixed * keep).astype(jnp.bfloat16)


def swap(size):
    return [(i, i ^ 1) for i in range(size)]


def general(hidden_in, norm_gain, projection, lengths):
    groups = lax.axis_size("groups")
    dp = lax.axis_size("dp")
    tensor = lax.axis_size("tensor")
    y = lax.axis_index("groups")
    place = lax.axis_index("dp")
    core = lax.axis_index("tensor")
    x = place % 2
    z = place // 2
    depth = dp // 2
    tokens = hidden_in.shape[0]
    rows = projection.shape[1]
    part = rows // groups
    heads_local = QHEADS // tensor

    ring = [(i, (i + 2) % dp) for i in range(dp)]
    over_x = swap(dp)
    over_y = swap(groups)
    over_core = swap(tensor)
    across = [(g * dp + i, (g ^ 1) * dp + (i ^ 1)) for g in range(groups) for i in range(dp)]

    mine = lax.dynamic_slice_in_dim(projection[0], y * part, part, 0)

    def column(owner, index):
        start = (QHEADS + owner) * HEAD if index == 0 else (owner * heads_local + index - 1) * HEAD
        return lax.dynamic_slice_in_dim(mine, start, HEAD, 1)

    n_cols = heads_local + 1
    theirs = jnp.concatenate([column(1 - core, i) for i in range(n_cols)], axis=1)
    other = lax.ppermute(theirs, "tensor", over_core)
    weights = []
    for i in range(n_cols):
        slot = jnp.concatenate([column(core, i), other[:, i * HEAD:(i + 1) * HEAD]], axis=0)
        weights.append([slot])
    for _ in range(depth - 1):
        for i in range(n_cols):
            weights[i].append(lax.ppermute(weights[i][-1], "dp", ring))

    wide32 = hidden_in.astype(jnp.float32)
    gated = (wide32 * norm_gain.astype(jnp.float32)[None, :]).astype(jnp.bfloat16)
    local_sq = jnp.sum(wide32 * wide32, axis=1)
    total_sq = local_sq + lax.ppermute(local_sq, "tensor", over_core)
    inv_rms = lax.rsqrt(total_sq / D + EPSILON)[:, None]

    def piece(dx, dy):
        slabs = []
        for k in range(depth):
            shard = ((z - k + depth) % depth) * 2 + (x ^ dx)
            slabs.append(lax.dynamic_slice_in_dim(gated, shard * rows + (y ^ dy) * part, part, 1))
        return jnp.stack(slabs)

    sent = [piece(1, 1), piece(1, 0), piece(0, 1)]
    held = [
        lax.ppermute(sent[0], ("groups", "dp"), across),
        lax.ppermute(sent[1], "dp", over_x),
        lax.ppermute(sent[2], "groups", over_y),
        piece(0, 0),
    ]
    acts = []
    for h in held:
        acts.append(jnp.concatenate([h, lax.ppermute(h, "tensor", over_core)], axis=2))
    acts = jnp.concatenate(acts, axis=1)

    cosine, sine = angles(tokens)
    positions = jnp.arange(tokens, dtype=jnp.int32)
    prompt = lengths[0, 0]
    total_len = prompt + lengths[0, 1]
    allowed = (positions[None, :] <= positions[:, None]) & (positions[None, :] < total_len)
    keep = ((positions >= prompt - 1) & (positions < total_len - 1)).astype(jnp.float32)[:, None]

    outs = []
    keys = values = None
    for i in range(n_cols):
        partial = sum(
            jnp.dot(acts[k], weights[i][k], preferred_element_type=jnp.float32) for k in range(depth)
        )
        blocks = partial.reshape(4, tokens, HEAD)
        low = blocks[:3].astype(jnp.bfloat16)
        summed = blocks[3]
        summed = summed + lax.ppermute(low[0], ("groups", "dp"), across).astype(jnp.float32)
        summed = summed + lax.ppermute(low[1], "dp", over_x).astype(jnp.float32)
        summed = summed + lax.ppermute(low[2], "groups", over_y).astype(jnp.float32)
        scaled = summed * inv_rms
        if i == 0:
            turned = rotate(scaled, cosine, sine)
            kv = jnp.where(core == 0, turned, scaled).astype(jnp.bfloat16)
            vk = lax.ppermute(kv, "tensor", over_core)
            keys = jnp.where(core == 0, kv, vk)
            values = jnp.where(core == 0, vk, kv)
        else:
            query = rotate(scaled, cosine, sine).astype(jnp.bfloat16)
            outs.append(attend_head(query, keys, values, allowed, keep))
    return jnp.concatenate(outs, axis=1)


VMEM = pltpu.VMEM
PLANE = ((1, 1), (1, 0), (0, 1), (0, 0))
WHOLE = pl.BlockSpec(memory_space=VMEM)
SCALARS = pl.BlockSpec(memory_space=pltpu.SMEM)


def call(kernel, out_shape, limit=12, result=False, **kwargs):
    if not result:
        out_shape = jax.tree.map(lambda s: pltpu.VMEM(s.shape, s.dtype), out_shape)
    return pl.pallas_call(
        kernel,
        out_shape=out_shape,
        compiler_params=pltpu.CompilerParams(vmem_limit_bytes=limit * 2**20),
        cost_estimate=pl.CostEstimate(flops=1, bytes_accessed=1, transcendentals=0),
        **kwargs,
    )


def select_kernel(columns, part, rows_ref, *refs):
    out_refs, sems = refs[:len(columns)], refs[-1]
    rows = pl.ds(pl.multiple_of(lax.axis_index("groups") * part, HEAD), part)
    copies = []
    for starts, out_ref in zip(columns, out_refs):
        at = 0
        while at < len(starts):
            more = 1
            while at + more < len(starts) and starts[at + more] == starts[at] + more * HEAD:
                more += 1
            copies.append(pltpu.make_async_copy(
                rows_ref.at[0, rows, pl.ds(starts[at], more * HEAD)],
                out_ref.at[:, pl.ds(at * HEAD, more * HEAD)],
                sems.at[len(copies)],
            ))
            at += more
    for copy in copies:
        copy.start()
    for copy in copies:
        copy.wait()


def select(projection, part, columns):
    chunk = jax.ShapeDtypeStruct((part, len(columns[0]) * HEAD), projection.dtype)
    out_shape = (chunk,) * len(columns)
    return call(
        functools.partial(select_kernel, columns, part),
        out_shape,
        in_specs=[pl.BlockSpec(memory_space=pltpu.HBM)],
        out_specs=[WHOLE] * len(out_shape),
        scratch_shapes=[pltpu.SemaphoreType.DMA((len(columns) * len(columns[0]),))],
    )(pltpu.with_memory_space_constraint(projection, pltpu.HBM))


def gate_kernel(part, depth, plane, squares, place_ref, hidden_ref, gain_ref, *refs):
    piece_refs, row_ref = refs[:len(plane)], refs[-1]
    x, y = place_ref[1], place_ref[2]
    base = lax.rem(place_ref[0] - pl.program_id(0) + depth, depth) * 4 * part

    @pl.when(pl.program_id(0) == 0)
    def _():
        row_ref[0, :] = gain_ref[...].astype(jnp.float32)

    for piece_ref, (dx, dy) in zip(piece_refs, plane):
        start = pl.multiple_of(((x ^ dx) * 2 + (y ^ dy)) * part, HEAD)
        wide = hidden_ref[:, pl.ds(start, part)].astype(jnp.float32)
        gain = row_ref[:, pl.ds(pl.multiple_of(base + start, HEAD), part)]
        piece_ref[0] = (wide * gain).astype(jnp.bfloat16)
    if not squares:
        return
    sq_ref = refs[len(plane)]
    total = jnp.zeros(sq_ref.shape, jnp.float32)
    for j in range(0, hidden_ref.shape[1], HEAD):
        wide = hidden_ref[:, j:j + HEAD].astype(jnp.float32)
        total += wide * wide

    @pl.when(pl.program_id(0) == 0)
    def _():
        sq_ref[...] = total

    @pl.when(pl.program_id(0) > 0)
    def _():
        sq_ref[...] += total


def gate(place, hidden_in, norm_gain, part, depth, plane=PLANE, squares=True):
    tokens = hidden_in.shape[0]
    wide = 4 * part
    out_shape = (jax.ShapeDtypeStruct((depth, tokens, part), jnp.bfloat16),) * len(plane)
    out_specs = [pl.BlockSpec((1, tokens, part), lambda k, place: (k, 0, 0))] * len(plane)
    if squares:
        out_shape += (jax.ShapeDtypeStruct((tokens, HEAD), jnp.float32),)
        out_specs.append(pl.BlockSpec((tokens, HEAD), lambda k, place: (0, 0)))

    def shard(k, place):
        return (0, lax.rem(place[0] - k + depth, depth))

    return call(
        functools.partial(gate_kernel, part, depth, plane, squares),
        out_shape,
        grid_spec=pltpu.PrefetchScalarGridSpec(
            num_scalar_prefetch=1,
            grid=(depth,),
            in_specs=[
                pl.BlockSpec((tokens, wide), shard),
                pl.BlockSpec(norm_gain.shape, lambda k, place: (0,)),
            ],
            out_specs=out_specs,
            scratch_shapes=[pltpu.VMEM((1, norm_gain.shape[0]), jnp.float32)],
        ),
    )(place, *(pltpu.with_memory_space_constraint(a, pltpu.HBM) for a in (hidden_in, norm_gain)))


def matmul_kernel(firsts, n_acts, n_more, sent, *refs):
    is_first = lax.axis_index("tensor") == 0
    acts, refs = refs[:n_acts], refs[n_acts:]
    slots, refs = refs[:len(firsts)], refs[len(firsts):]
    more, out_refs = refs[:n_more], refs[n_more:]
    more = [(ref, i) for ref in more for i in range(ref.shape[0])]
    right = [slot[...] for slot in slots]
    wide = 2 * HEAD
    for p in range(n_acts):
        total = jnp.dot(acts[p][firsts[0]], right[0], preferred_element_type=jnp.float32)
        for k in range(1, len(firsts)):
            total += jnp.dot(acts[p][firsts[k]], right[k], preferred_element_type=jnp.float32)
        if more:
            ref, i = more[p]
            total += ref[i]
        if not sent:
            out_refs[0][p] = total
            continue
        theirs_refs, mine_ref = out_refs[:-1], out_refs[-1]
        n_blocks = mine_ref.shape[1]
        per = n_acts * n_blocks // sent
        for g in range(n_blocks):
            low = total[:, g * wide:g * wide + HEAD]
            high = total[:, g * wide + HEAD:(g + 1) * wide]
            spot = p * n_blocks + g
            theirs_refs[spot // per][spot % per] = jnp.where(is_first, high, low).astype(jnp.bfloat16)
            mine_ref[p, g] = jnp.where(is_first, low, high)


def matmul(acts, slots, firsts, so_far=(), sent=0):
    n_blocks = slots[0].shape[1] // (2 * HEAD)
    tokens = acts[0].shape[1]
    args = [*acts, *slots, *so_far]
    if sent:
        out_shape = (jax.ShapeDtypeStruct((len(acts) * n_blocks // sent, tokens, HEAD), jnp.bfloat16),) * sent
        out_shape += (jax.ShapeDtypeStruct((len(acts), n_blocks, tokens, HEAD), jnp.float32),)
    else:
        out_shape = (jax.ShapeDtypeStruct((len(acts), tokens, n_blocks * 2 * HEAD), jnp.float32),)
    outs = call(
        functools.partial(matmul_kernel, firsts, len(acts), len(so_far), sent),
        out_shape,
        in_specs=[WHOLE] * len(args),
        out_specs=[WHOLE] * len(out_shape),
    )(*args)
    return outs if sent else outs[0]


def join_kernel(n_came, mine_ref, *refs):
    came_refs, out_refs = refs[:n_came], refs[n_came:]
    n_blocks = mine_ref.shape[1]
    per = len(out_refs) * n_blocks // n_came
    for p, out_ref in enumerate(out_refs):
        for g in range(n_blocks):
            spot = p * n_blocks + g
            came = came_refs[spot // per][spot % per].astype(jnp.float32)
            out_ref[g] = (mine_ref[p, g] + came).astype(out_ref.dtype)


def join(mine, came, types):
    return call(
        functools.partial(join_kernel, len(came)),
        tuple(jax.ShapeDtypeStruct(mine.shape[1:], t) for t in types),
        in_specs=[WHOLE] * (1 + len(came)),
        out_specs=[WHOLE] * len(types),
    )(mine, *came)


def tables_kernel(lengths_ref, _, cosine_ref, sine_ref, allowed_ref, keep_ref):
    at = lax.broadcasted_iota(jnp.int32, cosine_ref.shape, 0)
    lane = lax.broadcasted_iota(jnp.int32, cosine_ref.shape, 1)
    pair = lax.rem(lane, HEAD // 2).astype(jnp.float32)
    angle = at.astype(jnp.float32) * jnp.exp(pair * (-2.0 * math.log(ROPE_BASE) / HEAD))
    cosine_ref[...] = jnp.cos(angle)
    sine_ref[...] = jnp.where(lane < HEAD // 2, -jnp.sin(angle), jnp.sin(angle))
    prompt = lengths_ref[0, 0]
    total_len = prompt + lengths_ref[0, 1]
    keep_ref[...] = ((at >= prompt - 1) & (at < total_len - 1)).astype(jnp.float32)
    query_at = lax.broadcasted_iota(jnp.int32, allowed_ref.shape, 0)
    key_at = lax.broadcasted_iota(jnp.int32, allowed_ref.shape, 1)
    allowed_ref[...] = ((key_at <= query_at) & (key_at < total_len)).astype(jnp.float32)


def tables(tokens, lengths, later_than):
    table = jax.ShapeDtypeStruct((tokens, HEAD), jnp.float32)
    allowed = jax.ShapeDtypeStruct((tokens, tokens), jnp.float32)
    return call(
        tables_kernel,
        (table, table, allowed, table),
        in_specs=[SCALARS, pl.BlockSpec(memory_space=pl.ANY)],
        out_specs=[WHOLE] * 4,
    )(lengths, later_than)


def scale_kernel(own_ref, other_ref, out_ref):
    squares = jnp.sum(own_ref[...] + other_ref[...], axis=1, keepdims=True)
    out_ref[...] = jnp.broadcast_to(lax.rsqrt(squares / D + EPSILON), out_ref.shape)


def inv_rms(own, other):
    return call(
        scale_kernel,
        jax.ShapeDtypeStruct(own.shape, jnp.float32),
        in_specs=[WHOLE] * 2,
        out_specs=WHOLE,
    )(own, other)


def summed(refs, index, scale_ref):
    total = refs[0][index]
    for ref in refs[1:]:
        total += ref[index].astype(jnp.float32)
    return total * scale_ref[...]


def turned(block, cosine_ref, sine_ref):
    half = HEAD // 2
    other = jnp.concatenate([block[:, half:], block[:, :half]], axis=1)
    return block * cosine_ref[...] + other * sine_ref[...]


def kv_kernel(own, r0, r1, r2, scale_ref, cosine_ref, sine_ref, out_ref):
    block = summed((own, r0, r1, r2), 0, scale_ref)
    spun = turned(block, cosine_ref, sine_ref)
    out_ref[...] = jnp.where(lax.axis_index("tensor") == 0, spun, block).astype(jnp.bfloat16)


def heads_kernel(first, n_parts, *refs):
    parts, refs = refs[:n_parts], refs[n_parts:]
    scale_ref, cosine_ref, sine_ref, allowed_ref, keep_ref, mine_ref, other_ref, *rest = refs
    out_ref = rest[-1]
    is_key = lax.axis_index("tensor") == 0
    mine, other = mine_ref[...], other_ref[...]
    keys = jnp.where(is_key, mine, other)
    values = jnp.where(is_key, other, mine)
    before = 0
    if len(rest) > 1:
        before = rest[0].shape[1]
        out_ref[:, :before] = rest[0][...]
    for i in range(first, parts[0].shape[0]):
        query = turned(summed(parts, i, scale_ref), cosine_ref, sine_ref).astype(jnp.bfloat16)
        scores = lax.dot_general(
            query, keys, (((1,), (1,)), ((), ())), preferred_element_type=jnp.float32
        ) * HEAD ** (-0.5)
        scores = jnp.where(allowed_ref[...] > 0.0, scores, -1e30)
        expo = jnp.exp(scores - jnp.max(scores, axis=-1, keepdims=True))
        attn = (expo / jnp.sum(expo, axis=-1, keepdims=True)).astype(jnp.bfloat16)
        mixed = jnp.dot(attn, values, preferred_element_type=jnp.float32)
        at = before + (i - first) * HEAD
        out_ref[:, at:at + HEAD] = (mixed * keep_ref[...]).astype(jnp.bfloat16)


def heads(parts, first, scale, tabled, mine, other, *earlier):
    args = [*parts, scale, *tabled, mine, other, *earlier]
    width = (parts[0].shape[0] - first) * HEAD + sum(e.shape[1] for e in earlier)
    return call(
        functools.partial(heads_kernel, first, len(parts)),
        jax.ShapeDtypeStruct((mine.shape[0], width), jnp.bfloat16),
        result=bool(earlier),
        in_specs=[WHOLE] * len(args),
        out_specs=WHOLE,
    )(*args)


def staged(hidden_in, norm_gain, projection, lengths):
    groups = lax.axis_size("groups")
    dp = lax.axis_size("dp")
    tensor = lax.axis_size("tensor")
    y = lax.axis_index("groups")
    spot = lax.axis_index("dp")
    core = lax.axis_index("tensor")
    place = jnp.stack([spot // 2, spot % 2, y, core]).astype(jnp.int32)
    depth = dp // 2
    tokens = hidden_in.shape[0]
    part = projection.shape[1] // groups
    heads_local = QHEADS // tensor

    ring = [(i, (i + 2) % dp) for i in range(dp)]
    over_x = swap(dp)
    over_y = swap(groups)
    over_core = swap(tensor)
    across = [(g * dp + i, (g ^ 1) * dp + (i ^ 1)) for g in range(groups) for i in range(dp)]

    def to_core(a):
        return lax.ppermute(a, "tensor", over_core)

    def on_ring(a):
        return lax.ppermute(a, "dp", ring)

    def back(a):
        return lax.ppermute(a, "dp", [(j, i) for i, j in ring])

    def to_far(a):
        return lax.ppermute(a, ("groups", "dp"), across)

    def to_x(a):
        return lax.ppermute(a, "dp", over_x)

    def to_y(a):
        return lax.ppermute(a, "groups", over_y)

    def to_plane(three):
        return [to_far(three[0]), to_x(three[1]), to_y(three[2])]

    last = []

    def after(*values):
        held = lax.optimization_barrier(tuple(values) + tuple(last))[:len(values)]
        last[:] = held[:1]
        return held[0] if len(values) == 1 else held

    blocks = [[(QHEADS + c) * HEAD for c in range(tensor)]]
    blocks += [[(c * heads_local + i) * HEAD for c in range(tensor)] for i in range(heads_local)]
    columns = [blocks[0] + blocks[1], blocks[2] + blocks[3]]
    a0, = select(projection, part, columns[:1])
    a0 = after(a0)
    a1 = on_ring(a0)
    a3 = back(a0)
    far, near_x, near_y, own, squares = after(*gate(place, after(hidden_in), norm_gain, part, depth))
    far = to_far(far)
    near_x = to_x(near_x)
    near_y = to_y(near_y)
    b0, = select(after(projection), part, columns[1:])
    tabled = after(*tables(tokens, lengths, after(squares)))

    a1 = after(a1)
    a2 = on_ring(a1)
    a3, b0 = after(a3, b0)
    b1 = on_ring(b0)
    a2, b0 = after(a2, b0)
    b3 = back(b0)
    set_a = (a0, a1, a2, a3)

    far = after(far)
    *theirs, mine = after(*matmul((far, own), set_a, (0, 1, 2, 3), sent=2))
    swapped = [to_core(t) for t in theirs]
    b1 = after(b1)
    b2 = on_ring(b1)
    sums_far, sums = after(*join(mine, after(*swapped), (jnp.bfloat16, jnp.float32)))
    sums_far = to_far(sums_far)
    near_x, near_y = after(near_x, near_y)
    acts = (far, own, near_x, near_y)
    *theirs, mine = after(*matmul((near_x, near_y), set_a, (0, 1, 2, 3), sent=2))
    swapped = [to_core(t) for t in theirs]
    squares = after(squares)
    other_norm = to_core(squares)
    b3 = after(b3)
    *swapped, other_norm = after(*swapped, other_norm)
    scale = inv_rms(squares, other_norm)
    sums_x, sums_y = after(*join(mine, swapped, (jnp.bfloat16, jnp.bfloat16)))
    sums_x = to_x(sums_x)
    sums_y = to_y(sums_y)
    front = after(matmul(acts, (b0, b1, b3), (0, 1, 3)))

    b2 = after(b2)
    parts_a = after(sums, sums_far, sums_x, sums_y)
    *theirs, mine = after(*matmul(acts, (b2,), (2,), (front,), sent=2))
    swapped = [to_core(t) for t in theirs]
    kv = after(call(
        kv_kernel,
        jax.ShapeDtypeStruct((tokens, HEAD), jnp.bfloat16),
        in_specs=[WHOLE] * 7,
        out_specs=WHOLE,
    )(*parts_a, scale, *tabled[:2]))
    vk = to_core(kv)
    types = (jnp.bfloat16, jnp.float32, jnp.bfloat16, jnp.bfloat16)
    sums_far, sums, sums_x, sums_y = after(*join(mine, after(*swapped), types))
    parts_b = (sums, to_far(sums_far), to_x(sums_x), to_y(sums_y))
    vk = after(vk)
    one = after(heads(parts_a, 1, scale, tabled, kv, vk))
    return heads(after(*parts_b), 0, scale, tabled, kv, vk, one)


def local(hidden_in, norm_gain, projection, lengths):
    part = projection.shape[1] // lax.axis_size("groups")
    if lax.axis_size("dp") == 8 and part % HEAD == 0:
        return staged(hidden_in, norm_gain, projection, lengths)
    return general(hidden_in, norm_gain, projection, lengths)


def solution(mesh):
    in_specs = (
        P(("groups", "dp"), "tensor"),
        P("tensor"),
        P("tensor", "dp", None),
        P(("groups", "dp"), None),
    )
    out_specs = P(("groups", "dp"), "tensor")
    return jax.shard_map(local, mesh=mesh, in_specs=in_specs, out_specs=out_specs, check_vma=False)
```

```python
import functools
import math

import jax
import jax.numpy as jnp
from jax import lax
from jax.experimental import pallas as pl
from jax.experimental.pallas import tpu as pltpu
from jax.sharding import PartitionSpec as P

D = 12288
HEAD = 128
QHEADS = 6
ROPE_BASE = 1000000.0
EPSILON = 1e-05


def angles(seq_len):
    half = HEAD // 2
    positions = jnp.arange(seq_len, dtype=jnp.int32)
    freq = ROPE_BASE ** (-(jnp.arange(half, dtype=jnp.float32) * 2.0 / HEAD))
    angle = positions.astype(jnp.float32)[:, None] * freq[None, :]
    return jnp.cos(angle), jnp.sin(angle)


def rotate(block, cosine, sine):
    half = HEAD // 2
    first = block[:, :half]
    second = block[:, half:]
    return jnp.concatenate([first * cosine - second * sine, second * cosine + first * sine], axis=-1)


def attend_head(query, keys, values, allowed, keep):
    scores = lax.dot_general(
        query, keys, (((1,), (1,)), ((), ())), preferred_element_type=jnp.float32
    ) * HEAD ** (-0.5)
    scores = jnp.where(allowed, scores, -1e30)
    largest = jnp.max(scores, axis=-1, keepdims=True)
    expo = jnp.exp(scores - largest)
    attn = (expo / jnp.sum(expo, axis=-1, keepdims=True)).astype(jnp.bfloat16)
    mixed = jnp.dot(attn, values, preferred_element_type=jnp.float32)
    return (mixed * keep).astype(jnp.bfloat16)


def swap(size):
    return [(i, i ^ 1) for i in range(size)]


def general(hidden_in, norm_gain, projection, lengths):
    groups = lax.axis_size("groups")
    dp = lax.axis_size("dp")
    tensor = lax.axis_size("tensor")
    y = lax.axis_index("groups")
    place = lax.axis_index("dp")
    core = lax.axis_index("tensor")
    x = place % 2
    z = place // 2
    depth = dp // 2
    tokens = hidden_in.shape[0]
    rows = projection.shape[1]
    part = rows // groups
    heads_local = QHEADS // tensor

    ring = [(i, (i + 2) % dp) for i in range(dp)]
    over_x = swap(dp)
    over_y = swap(groups)
    over_core = swap(tensor)
    across = [(g * dp + i, (g ^ 1) * dp + (i ^ 1)) for g in range(groups) for i in range(dp)]

    mine = lax.dynamic_slice_in_dim(projection[0], y * part, part, 0)

    def column(owner, index):
        start = (QHEADS + owner) * HEAD if index == 0 else (owner * heads_local + index - 1) * HEAD
        return lax.dynamic_slice_in_dim(mine, start, HEAD, 1)

    n_cols = heads_local + 1
    theirs = jnp.concatenate([column(1 - core, i) for i in range(n_cols)], axis=1)
    other = lax.ppermute(theirs, "tensor", over_core)
    weights = []
    for i in range(n_cols):
        slot = jnp.concatenate([column(core, i), other[:, i * HEAD:(i + 1) * HEAD]], axis=0)
        weights.append([slot])
    for _ in range(depth - 1):
        for i in range(n_cols):
            weights[i].append(lax.ppermute(weights[i][-1], "dp", ring))

    wide32 = hidden_in.astype(jnp.float32)
    gated = (wide32 * norm_gain.astype(jnp.float32)[None, :]).astype(jnp.bfloat16)
    local_sq = jnp.sum(wide32 * wide32, axis=1)
    total_sq = local_sq + lax.ppermute(local_sq, "tensor", over_core)
    inv_rms = lax.rsqrt(total_sq / D + EPSILON)[:, None]

    def piece(dx, dy):
        slabs = []
        for k in range(depth):
            shard = ((z - k + depth) % depth) * 2 + (x ^ dx)
            slabs.append(lax.dynamic_slice_in_dim(gated, shard * rows + (y ^ dy) * part, part, 1))
        return jnp.stack(slabs)

    sent = [piece(1, 1), piece(1, 0), piece(0, 1)]
    held = [
        lax.ppermute(sent[0], ("groups", "dp"), across),
        lax.ppermute(sent[1], "dp", over_x),
        lax.ppermute(sent[2], "groups", over_y),
        piece(0, 0),
    ]
    acts = []
    for h in held:
        acts.append(jnp.concatenate([h, lax.ppermute(h, "tensor", over_core)], axis=2))
    acts = jnp.concatenate(acts, axis=1)

    cosine, sine = angles(tokens)
    positions = jnp.arange(tokens, dtype=jnp.int32)
    prompt = lengths[0, 0]
    total_len = prompt + lengths[0, 1]
    allowed = (positions[None, :] <= positions[:, None]) & (positions[None, :] < total_len)
    keep = ((positions >= prompt - 1) & (positions < total_len - 1)).astype(jnp.float32)[:, None]

    outs = []
    keys = values = None
    for i in range(n_cols):
        partial = sum(
            jnp.dot(acts[k], weights[i][k], preferred_element_type=jnp.float32) for k in range(depth)
        )
        blocks = partial.reshape(4, tokens, HEAD)
        low = blocks[:3].astype(jnp.bfloat16)
        summed = blocks[3]
        summed = summed + lax.ppermute(low[0], ("groups", "dp"), across).astype(jnp.float32)
        summed = summed + lax.ppermute(low[1], "dp", over_x).astype(jnp.float32)
        summed = summed + lax.ppermute(low[2], "groups", over_y).astype(jnp.float32)
        scaled = summed * inv_rms
        if i == 0:
            turned = rotate(scaled, cosine, sine)
            kv = jnp.where(core == 0, turned, scaled).astype(jnp.bfloat16)
            vk = lax.ppermute(kv, "tensor", over_core)
            keys = jnp.where(core == 0, kv, vk)
            values = jnp.where(core == 0, vk, kv)
        else:
            query = rotate(scaled, cosine, sine).astype(jnp.bfloat16)
            outs.append(attend_head(query, keys, values, allowed, keep))
    return jnp.concatenate(outs, axis=1)


VMEM = pltpu.VMEM
PLANE = ((1, 1), (1, 0), (0, 1), (0, 0))
WHOLE = pl.BlockSpec(memory_space=VMEM)
SCALARS = pl.BlockSpec(memory_space=pltpu.SMEM)


def call(kernel, out_shape, limit=12, result=False, **kwargs):
    if not result:
        out_shape = jax.tree.map(lambda s: pltpu.VMEM(s.shape, s.dtype), out_shape)
    return pl.pallas_call(
        kernel,
        out_shape=out_shape,
        compiler_params=pltpu.CompilerParams(vmem_limit_bytes=limit * 2**20),
        cost_estimate=pl.CostEstimate(flops=1, bytes_accessed=1, transcendentals=0),
        **kwargs,
    )


def select_kernel(columns, part, rows_ref, *refs):
    out_refs, sems = refs[:len(columns)], refs[-1]
    rows = pl.ds(pl.multiple_of(lax.axis_index("groups") * part, HEAD), part)
    copies = []
    for starts, out_ref in zip(columns, out_refs):
        at = 0
        while at < len(starts):
            more = 1
            while at + more < len(starts) and starts[at + more] == starts[at] + more * HEAD:
                more += 1
            copies.append(pltpu.make_async_copy(
                rows_ref.at[0, rows, pl.ds(starts[at], more * HEAD)],
                out_ref.at[:, pl.ds(at * HEAD, more * HEAD)],
                sems.at[len(copies)],
            ))
            at += more
    for copy in copies:
        copy.start()
    for copy in copies:
        copy.wait()


def select(projection, part, columns):
    chunk = jax.ShapeDtypeStruct((part, len(columns[0]) * HEAD), projection.dtype)
    out_shape = (chunk,) * len(columns)
    return call(
        functools.partial(select_kernel, columns, part),
        out_shape,
        in_specs=[pl.BlockSpec(memory_space=pltpu.HBM)],
        out_specs=[WHOLE] * len(out_shape),
        scratch_shapes=[pltpu.SemaphoreType.DMA((len(columns) * len(columns[0]),))],
    )(pltpu.with_memory_space_constraint(projection, pltpu.HBM))


def gate_kernel(part, depth, hidden_ref, gain_ref, *refs):
    piece_refs, (sq_ref, slab_ref, row_ref, sems) = refs[:4], refs[4:]
    place = lax.axis_index("dp")
    x, z, y = place % 2, place // 2, lax.axis_index("groups")
    wide = 4 * part
    columns = [pl.ds(pl.multiple_of(lax.rem(z - k + depth, depth) * wide, HEAD), wide) for k in range(depth)]
    copies = [pltpu.make_async_copy(hidden_ref.at[:, c], slab_ref.at[k], sems.at[k]) for k, c in enumerate(columns)]
    for copy in copies:
        copy.start()
    row_ref[0, :] = gain_ref[...].astype(jnp.float32)
    tokens = hidden_ref.shape[0]
    height = 64
    for k, copy in enumerate(copies):
        copy.wait()
        for top in range(0, tokens, height):
            rows = slice(top, top + height)
            total = jnp.zeros((height, HEAD), jnp.float32)
            for piece_ref, (dx, dy) in zip(piece_refs, PLANE):
                start = ((x ^ dx) * 2 + (y ^ dy)) * part
                whole = slab_ref[k, rows, pl.ds(pl.multiple_of(start, HEAD), part)].astype(jnp.float32)
                at = lax.rem(z - k + depth, depth) * wide + start
                gain = row_ref[:, pl.ds(pl.multiple_of(at, HEAD), part)]
                piece_ref[k, rows] = (whole * gain).astype(jnp.bfloat16)
                square = whole * whole
                for j in range(0, part, HEAD):
                    total += square[:, j:j + HEAD]
            sq_ref[rows] = total if k == 0 else sq_ref[rows] + total


def gate(hidden_in, norm_gain, part, depth):
    tokens = hidden_in.shape[0]
    piece = jax.ShapeDtypeStruct((depth, tokens, part), jnp.bfloat16)
    return call(
        functools.partial(gate_kernel, part, depth),
        (piece,) * 4 + (jax.ShapeDtypeStruct((tokens, HEAD), jnp.float32),),
        in_specs=[pl.BlockSpec(memory_space=pltpu.HBM), WHOLE],
        out_specs=[WHOLE] * 5,
        scratch_shapes=[
            pltpu.VMEM((depth, tokens, 4 * part), jnp.bfloat16),
            pltpu.VMEM((1, norm_gain.shape[0]), jnp.float32),
            pltpu.SemaphoreType.DMA((depth,)),
        ],
    )(pltpu.with_memory_space_constraint(hidden_in, pltpu.HBM), norm_gain)


def matmul_kernel(firsts, n_acts, n_more, sent, *refs):
    is_first = lax.axis_index("tensor") == 0
    acts, refs = refs[:n_acts], refs[n_acts:]
    slots, refs = refs[:len(firsts)], refs[len(firsts):]
    more, out_refs = refs[:n_more], refs[n_more:]
    more = [(ref, i) for ref in more for i in range(ref.shape[0])]
    right = [slot[...] for slot in slots]
    wide = 2 * HEAD
    for p in range(n_acts):
        total = jnp.dot(acts[p][firsts[0]], right[0], preferred_element_type=jnp.float32)
        for k in range(1, len(firsts)):
            total += jnp.dot(acts[p][firsts[k]], right[k], preferred_element_type=jnp.float32)
        if more:
            ref, i = more[p]
            total += ref[i]
        if not sent:
            out_refs[0][p] = total
            continue
        theirs_refs, mine_ref = out_refs[:-1], out_refs[-1]
        n_blocks = mine_ref.shape[1]
        per = n_acts * n_blocks // sent
        for g in range(n_blocks):
            low = total[:, g * wide:g * wide + HEAD]
            high = total[:, g * wide + HEAD:(g + 1) * wide]
            spot = p * n_blocks + g
            theirs_refs[spot // per][spot % per] = jnp.where(is_first, high, low).astype(jnp.bfloat16)
            mine_ref[p, g] = jnp.where(is_first, low, high)


def matmul(acts, slots, firsts, so_far=(), sent=0):
    n_blocks = slots[0].shape[1] // (2 * HEAD)
    tokens = acts[0].shape[1]
    args = [*acts, *slots, *so_far]
    if sent:
        out_shape = (jax.ShapeDtypeStruct((len(acts) * n_blocks // sent, tokens, HEAD), jnp.bfloat16),) * sent
        out_shape += (jax.ShapeDtypeStruct((len(acts), n_blocks, tokens, HEAD), jnp.float32),)
    else:
        out_shape = (jax.ShapeDtypeStruct((len(acts), tokens, n_blocks * 2 * HEAD), jnp.float32),)
    outs = call(
        functools.partial(matmul_kernel, firsts, len(acts), len(so_far), sent),
        out_shape,
        in_specs=[WHOLE] * len(args),
        out_specs=[WHOLE] * len(out_shape),
    )(*args)
    return outs if sent else outs[0]


def join_kernel(n_came, first, mine_ref, *refs):
    came_refs, out_refs = refs[:n_came], refs[n_came:]
    n_blocks = mine_ref.shape[1]
    per = len(out_refs) * n_blocks // n_came
    for p, out_ref in enumerate(out_refs):
        for g in range(n_blocks):
            spot = p * n_blocks + g
            came = came_refs[spot // per][spot % per].astype(jnp.float32)
            out_ref[g] = (mine_ref[first + p, g] + came).astype(out_ref.dtype)


def join(mine, came, types, first=0):
    return call(
        functools.partial(join_kernel, len(came), first),
        tuple(jax.ShapeDtypeStruct(mine.shape[1:], t) for t in types),
        in_specs=[WHOLE] * (1 + len(came)),
        out_specs=[WHOLE] * len(types),
    )(mine, *came)


def tables_kernel(lengths_ref, _, cosine_ref, sine_ref, allowed_ref, keep_ref):
    at = lax.broadcasted_iota(jnp.int32, cosine_ref.shape, 0)
    lane = lax.broadcasted_iota(jnp.int32, cosine_ref.shape, 1)
    pair = lax.rem(lane, HEAD // 2).astype(jnp.float32)
    angle = at.astype(jnp.float32) * jnp.exp(pair * (-2.0 * math.log(ROPE_BASE) / HEAD))
    cosine_ref[...] = jnp.cos(angle)
    sine_ref[...] = jnp.where(lane < HEAD // 2, -jnp.sin(angle), jnp.sin(angle))
    prompt = lengths_ref[0, 0]
    total_len = prompt + lengths_ref[0, 1]
    keep_ref[...] = ((at >= prompt - 1) & (at < total_len - 1)).astype(jnp.float32)
    query_at = lax.broadcasted_iota(jnp.int32, allowed_ref.shape, 0)
    key_at = lax.broadcasted_iota(jnp.int32, allowed_ref.shape, 1)
    allowed_ref[...] = ((key_at <= query_at) & (key_at < total_len)).astype(jnp.float32)


def tables(tokens, lengths, later_than):
    table = jax.ShapeDtypeStruct((tokens, HEAD), jnp.float32)
    allowed = jax.ShapeDtypeStruct((tokens, tokens), jnp.float32)
    return call(
        tables_kernel,
        (table, table, allowed, table),
        in_specs=[SCALARS, pl.BlockSpec(memory_space=pl.ANY)],
        out_specs=[WHOLE] * 4,
    )(lengths, later_than)


def scale_kernel(own_ref, other_ref, out_ref):
    squares = jnp.sum(own_ref[...] + other_ref[...], axis=1, keepdims=True)
    out_ref[...] = jnp.broadcast_to(lax.rsqrt(squares / D + EPSILON), out_ref.shape)


def inv_rms(own, other):
    return call(
        scale_kernel,
        jax.ShapeDtypeStruct(own.shape, jnp.float32),
        in_specs=[WHOLE] * 2,
        out_specs=WHOLE,
    )(own, other)


def summed(refs, index, scale_ref):
    total = refs[0][index]
    for ref in refs[1:]:
        total += ref[index].astype(jnp.float32)
    return total * scale_ref[...]


def turned(block, cosine_ref, sine_ref):
    half = HEAD // 2
    other = jnp.concatenate([block[:, half:], block[:, :half]], axis=1)
    return block * cosine_ref[...] + other * sine_ref[...]


def kv_kernel(own, r0, r1, r2, scale_ref, cosine_ref, sine_ref, out_ref):
    block = summed((own, r0, r1, r2), 0, scale_ref)
    spun = turned(block, cosine_ref, sine_ref)
    out_ref[...] = jnp.where(lax.axis_index("tensor") == 0, spun, block).astype(jnp.bfloat16)


def heads_kernel(first, n_parts, *refs):
    parts, refs = refs[:n_parts], refs[n_parts:]
    scale_ref, cosine_ref, sine_ref, allowed_ref, keep_ref, mine_ref, other_ref, *rest = refs
    out_ref = rest[-1]
    is_key = lax.axis_index("tensor") == 0
    mine, other = mine_ref[...], other_ref[...]
    keys = jnp.where(is_key, mine, other)
    values = jnp.where(is_key, other, mine)
    before = 0
    if len(rest) > 1:
        before = rest[0].shape[1]
        out_ref[:, :before] = rest[0][...]
    for i in range(first, parts[0].shape[0]):
        query = turned(summed(parts, i, scale_ref), cosine_ref, sine_ref).astype(jnp.bfloat16)
        scores = lax.dot_general(
            query, keys, (((1,), (1,)), ((), ())), preferred_element_type=jnp.float32
        ) * HEAD ** (-0.5)
        scores = jnp.where(allowed_ref[...] > 0.0, scores, -1e30)
        expo = jnp.exp(scores - jnp.max(scores, axis=-1, keepdims=True))
        attn = (expo / jnp.sum(expo, axis=-1, keepdims=True)).astype(jnp.bfloat16)
        mixed = jnp.dot(attn, values, preferred_element_type=jnp.float32)
        at = before + (i - first) * HEAD
        out_ref[:, at:at + HEAD] = (mixed * keep_ref[...]).astype(jnp.bfloat16)


def heads(parts, first, scale, tabled, mine, other, *earlier):
    args = [*parts, scale, *tabled, mine, other, *earlier]
    width = (parts[0].shape[0] - first) * HEAD + sum(e.shape[1] for e in earlier)
    return call(
        functools.partial(heads_kernel, first, len(parts)),
        jax.ShapeDtypeStruct((mine.shape[0], width), jnp.bfloat16),
        result=bool(earlier),
        in_specs=[WHOLE] * len(args),
        out_specs=WHOLE,
    )(*args)


def staged(hidden_in, norm_gain, projection, lengths):
    groups = lax.axis_size("groups")
    dp = lax.axis_size("dp")
    tensor = lax.axis_size("tensor")
    depth = dp // 2
    tokens = hidden_in.shape[0]
    part = projection.shape[1] // groups
    heads_local = QHEADS // tensor

    ring = [(i, (i + 2) % dp) for i in range(dp)]
    over_x = swap(dp)
    over_y = swap(groups)
    over_core = swap(tensor)
    across = [(g * dp + i, (g ^ 1) * dp + (i ^ 1)) for g in range(groups) for i in range(dp)]

    def to_core(a):
        return lax.ppermute(a, "tensor", over_core)

    def on_ring(a):
        return lax.ppermute(a, "dp", ring)

    def back(a):
        return lax.ppermute(a, "dp", [(j, i) for i, j in ring])

    def to_far(a):
        return lax.ppermute(a, ("groups", "dp"), across)

    def to_x(a):
        return lax.ppermute(a, "dp", over_x)

    def to_y(a):
        return lax.ppermute(a, "groups", over_y)

    def to_plane(three):
        return [to_far(three[0]), to_x(three[1]), to_y(three[2])]

    last = []

    def after(*values):
        held = lax.optimization_barrier(tuple(values) + tuple(last))[:len(values)]
        last[:] = held[:1]
        return held[0] if len(values) == 1 else held

    blocks = [[(QHEADS + c) * HEAD for c in range(tensor)]]
    blocks += [[(c * heads_local + i) * HEAD for c in range(tensor)] for i in range(heads_local)]
    columns = [blocks[0] + blocks[1], blocks[2] + blocks[3]]
    a0, = select(projection, part, columns[:1])
    a0 = after(a0)
    a1 = on_ring(a0)
    far, near_x, near_y, own, squares = after(*gate(after(hidden_in), norm_gain, part, depth))
    near_x = to_x(near_x)
    near_y = to_y(near_y)
    b0, = select(after(projection), part, columns[1:])
    b0, a0 = after(b0, a0)
    a3 = back(a0)
    tabled = after(*tables(tokens, lengths, after(squares)))

    a1, b0, far = after(a1, b0, far)
    b1 = on_ring(b0)
    far = to_far(far)
    a3, a1 = after(a3, a1)
    a2 = on_ring(a1)
    b1 = after(b1)
    b2 = on_ring(b1)
    near_y = after(near_y)
    near_x = after(near_x)
    a2, b0 = after(a2, b0)
    b3 = back(b0)
    set_a = (a0, a1, a2, a3)

    early = (near_x, near_y, own)
    *theirs, mine = after(*matmul(early, set_a, (0, 1, 2, 3), sent=2))
    swapped = [to_core(t) for t in theirs]
    far = after(far)
    sums_x, sums_y, sums = after(*join(mine, after(*swapped), (jnp.bfloat16, jnp.bfloat16, jnp.float32)))
    sums_x = to_x(sums_x)
    sums_y = to_y(sums_y)
    acts = (far, own, near_x, near_y)
    *theirs, mine = after(*matmul((far,), set_a, (0, 1, 2, 3), sent=1))
    swapped = [to_core(t) for t in theirs]
    squares = after(squares)
    other_norm = to_core(squares)
    b2 = after(b2)
    *swapped, other_norm = after(*swapped, other_norm)
    scale = inv_rms(squares, other_norm)
    sums_far = after(*join(mine, swapped, (jnp.bfloat16,)))
    sums_far = to_far(sums_far)
    sums_y = after(sums_y)
    sums_x = after(sums_x)
    front = after(matmul(acts, (b0, b1, b2), (0, 1, 2)))

    b3 = after(b3)
    parts_a = after(sums, sums_far, sums_x, sums_y)
    *theirs, mine = after(*matmul(acts, (b3,), (3,), (front,), sent=2))
    swapped = [to_core(t) for t in theirs]
    kv = after(call(
        kv_kernel,
        jax.ShapeDtypeStruct((tokens, HEAD), jnp.bfloat16),
        in_specs=[WHOLE] * 7,
        out_specs=WHOLE,
    )(*parts_a, scale, *tabled[:2]))
    vk = to_core(kv)
    sums_far, sums = after(*join(mine, (after(swapped[0]),), (jnp.bfloat16, jnp.float32)))
    sums_far = to_far(sums_far)
    sums_x, sums_y = after(*join(mine, (after(swapped[1]),), (jnp.bfloat16, jnp.bfloat16), first=2))
    sums_x = to_x(sums_x)
    sums_y = to_y(sums_y)
    vk = after(vk)
    one = after(heads(parts_a, 1, scale, tabled, kv, vk))
    sums_far = after(sums_far)
    sums_x, sums_y = after(sums_x, sums_y)
    return heads((sums, sums_far, sums_x, sums_y), 0, scale, tabled, kv, vk, one)


def local(hidden_in, norm_gain, projection, lengths):
    part = projection.shape[1] // lax.axis_size("groups")
    if lax.axis_size("dp") == 8 and part % HEAD == 0:
        return staged(hidden_in, norm_gain, projection, lengths)
    return general(hidden_in, norm_gain, projection, lengths)


def solution(mesh):
    in_specs = (
        P(("groups", "dp"), "tensor"),
        P("tensor"),
        P("tensor", "dp", None),
        P(("groups", "dp"), None),
    )
    out_specs = P(("groups", "dp"), "tensor")
    return jax.shard_map(local, mesh=mesh, in_specs=in_specs, out_specs=out_specs, check_vma=False)
```

```python
import functools
import math

import jax
import jax.numpy as jnp
from jax import lax
from jax.experimental import pallas as pl
from jax.experimental.pallas import tpu as pltpu
from jax.sharding import PartitionSpec as P

D = 12288
HEAD = 128
QHEADS = 6
ROPE_BASE = 1000000.0
EPSILON = 1e-05


def angles(seq_len):
    half = HEAD // 2
    positions = jnp.arange(seq_len, dtype=jnp.int32)
    freq = ROPE_BASE ** (-(jnp.arange(half, dtype=jnp.float32) * 2.0 / HEAD))
    angle = positions.astype(jnp.float32)[:, None] * freq[None, :]
    return jnp.cos(angle), jnp.sin(angle)


def rotate(block, cosine, sine):
    half = HEAD // 2
    first = block[:, :half]
    second = block[:, half:]
    return jnp.concatenate([first * cosine - second * sine, second * cosine + first * sine], axis=-1)


def attend_head(query, keys, values, allowed, keep):
    scores = lax.dot_general(
        query, keys, (((1,), (1,)), ((), ())), preferred_element_type=jnp.float32
    ) * HEAD ** (-0.5)
    scores = jnp.where(allowed, scores, -1e30)
    largest = jnp.max(scores, axis=-1, keepdims=True)
    expo = jnp.exp(scores - largest)
    attn = (expo / jnp.sum(expo, axis=-1, keepdims=True)).astype(jnp.bfloat16)
    mixed = jnp.dot(attn, values, preferred_element_type=jnp.float32)
    return (mixed * keep).astype(jnp.bfloat16)


def swap(size):
    return [(i, i ^ 1) for i in range(size)]


def general(hidden_in, norm_gain, projection, lengths):
    groups = lax.axis_size("groups")
    dp = lax.axis_size("dp")
    tensor = lax.axis_size("tensor")
    y = lax.axis_index("groups")
    place = lax.axis_index("dp")
    core = lax.axis_index("tensor")
    x = place % 2
    z = place // 2
    depth = dp // 2
    tokens = hidden_in.shape[0]
    rows = projection.shape[1]
    part = rows // groups
    heads_local = QHEADS // tensor

    ring = [(i, (i + 2) % dp) for i in range(dp)]
    over_x = swap(dp)
    over_y = swap(groups)
    over_core = swap(tensor)
    across = [(g * dp + i, (g ^ 1) * dp + (i ^ 1)) for g in range(groups) for i in range(dp)]

    mine = lax.dynamic_slice_in_dim(projection[0], y * part, part, 0)

    def column(owner, index):
        start = (QHEADS + owner) * HEAD if index == 0 else (owner * heads_local + index - 1) * HEAD
        return lax.dynamic_slice_in_dim(mine, start, HEAD, 1)

    n_cols = heads_local + 1
    theirs = jnp.concatenate([column(1 - core, i) for i in range(n_cols)], axis=1)
    other = lax.ppermute(theirs, "tensor", over_core)
    weights = []
    for i in range(n_cols):
        slot = jnp.concatenate([column(core, i), other[:, i * HEAD:(i + 1) * HEAD]], axis=0)
        weights.append([slot])
    for _ in range(depth - 1):
        for i in range(n_cols):
            weights[i].append(lax.ppermute(weights[i][-1], "dp", ring))

    wide32 = hidden_in.astype(jnp.float32)
    gated = (wide32 * norm_gain.astype(jnp.float32)[None, :]).astype(jnp.bfloat16)
    local_sq = jnp.sum(wide32 * wide32, axis=1)
    total_sq = local_sq + lax.ppermute(local_sq, "tensor", over_core)
    inv_rms = lax.rsqrt(total_sq / D + EPSILON)[:, None]

    def piece(dx, dy):
        slabs = []
        for k in range(depth):
            shard = ((z - k + depth) % depth) * 2 + (x ^ dx)
            slabs.append(lax.dynamic_slice_in_dim(gated, shard * rows + (y ^ dy) * part, part, 1))
        return jnp.stack(slabs)

    sent = [piece(1, 1), piece(1, 0), piece(0, 1)]
    held = [
        lax.ppermute(sent[0], ("groups", "dp"), across),
        lax.ppermute(sent[1], "dp", over_x),
        lax.ppermute(sent[2], "groups", over_y),
        piece(0, 0),
    ]
    acts = []
    for h in held:
        acts.append(jnp.concatenate([h, lax.ppermute(h, "tensor", over_core)], axis=2))
    acts = jnp.concatenate(acts, axis=1)

    cosine, sine = angles(tokens)
    positions = jnp.arange(tokens, dtype=jnp.int32)
    prompt = lengths[0, 0]
    total_len = prompt + lengths[0, 1]
    allowed = (positions[None, :] <= positions[:, None]) & (positions[None, :] < total_len)
    keep = ((positions >= prompt - 1) & (positions < total_len - 1)).astype(jnp.float32)[:, None]

    outs = []
    keys = values = None
    for i in range(n_cols):
        partial = sum(
            jnp.dot(acts[k], weights[i][k], preferred_element_type=jnp.float32) for k in range(depth)
        )
        blocks = partial.reshape(4, tokens, HEAD)
        low = blocks[:3].astype(jnp.bfloat16)
        summed = blocks[3]
        summed = summed + lax.ppermute(low[0], ("groups", "dp"), across).astype(jnp.float32)
        summed = summed + lax.ppermute(low[1], "dp", over_x).astype(jnp.float32)
        summed = summed + lax.ppermute(low[2], "groups", over_y).astype(jnp.float32)
        scaled = summed * inv_rms
        if i == 0:
            turned = rotate(scaled, cosine, sine)
            kv = jnp.where(core == 0, turned, scaled).astype(jnp.bfloat16)
            vk = lax.ppermute(kv, "tensor", over_core)
            keys = jnp.where(core == 0, kv, vk)
            values = jnp.where(core == 0, vk, kv)
        else:
            query = rotate(scaled, cosine, sine).astype(jnp.bfloat16)
            outs.append(attend_head(query, keys, values, allowed, keep))
    return jnp.concatenate(outs, axis=1)


VMEM = pltpu.VMEM
PLANE = ((1, 1), (1, 0), (0, 1), (0, 0))
WHOLE = pl.BlockSpec(memory_space=VMEM)
SCALARS = pl.BlockSpec(memory_space=pltpu.SMEM)


def call(kernel, out_shape, limit=12, result=False, **kwargs):
    if not result:
        out_shape = jax.tree.map(lambda s: pltpu.VMEM(s.shape, s.dtype), out_shape)
    return pl.pallas_call(
        kernel,
        out_shape=out_shape,
        compiler_params=pltpu.CompilerParams(vmem_limit_bytes=limit * 2**20),
        cost_estimate=pl.CostEstimate(flops=1, bytes_accessed=1, transcendentals=0),
        **kwargs,
    )


def select_kernel(columns, part, rows_ref, *refs):
    out_refs, sems = refs[:len(columns)], refs[-1]
    rows = pl.ds(pl.multiple_of(lax.axis_index("groups") * part, HEAD), part)
    copies = []
    for starts, out_ref in zip(columns, out_refs):
        at = 0
        while at < len(starts):
            more = 1
            while at + more < len(starts) and starts[at + more] == starts[at] + more * HEAD:
                more += 1
            copies.append(pltpu.make_async_copy(
                rows_ref.at[0, rows, pl.ds(starts[at], more * HEAD)],
                out_ref.at[:, pl.ds(at * HEAD, more * HEAD)],
                sems.at[len(copies)],
            ))
            at += more
    for copy in copies:
        copy.start()
    for copy in copies:
        copy.wait()


def select(projection, part, columns):
    chunk = jax.ShapeDtypeStruct((part, len(columns[0]) * HEAD), projection.dtype)
    out_shape = (chunk,) * len(columns)
    return call(
        functools.partial(select_kernel, columns, part),
        out_shape,
        in_specs=[pl.BlockSpec(memory_space=pltpu.HBM)],
        out_specs=[WHOLE] * len(out_shape),
        scratch_shapes=[pltpu.SemaphoreType.DMA((len(columns) * len(columns[0]),))],
    )(pltpu.with_memory_space_constraint(projection, pltpu.HBM))


def gate_kernel(part, depth, hidden_ref, gain_ref, *refs):
    piece_refs, (sq_ref, slab_ref, row_ref, sems) = refs[:4], refs[4:]
    place = lax.axis_index("dp")
    x, z, y = place % 2, place // 2, lax.axis_index("groups")
    wide = 4 * part
    columns = [pl.ds(pl.multiple_of(lax.rem(z - k + depth, depth) * wide, HEAD), wide) for k in range(depth)]
    copies = [pltpu.make_async_copy(hidden_ref.at[:, c], slab_ref.at[k], sems.at[k]) for k, c in enumerate(columns)]
    for copy in copies:
        copy.start()
    row_ref[0, :] = gain_ref[...].astype(jnp.float32)
    tokens = hidden_ref.shape[0]
    height = 64
    for k, copy in enumerate(copies):
        copy.wait()
        for top in range(0, tokens, height):
            rows = slice(top, top + height)
            total = jnp.zeros((height, HEAD), jnp.float32)
            for piece_ref, (dx, dy) in zip(piece_refs, PLANE):
                start = ((x ^ dx) * 2 + (y ^ dy)) * part
                whole = slab_ref[k, rows, pl.ds(pl.multiple_of(start, HEAD), part)].astype(jnp.float32)
                at = lax.rem(z - k + depth, depth) * wide + start
                gain = row_ref[:, pl.ds(pl.multiple_of(at, HEAD), part)]
                piece_ref[k, rows] = (whole * gain).astype(jnp.bfloat16)
                square = whole * whole
                for j in range(0, part, HEAD):
                    total += square[:, j:j + HEAD]
            sq_ref[rows] = total if k == 0 else sq_ref[rows] + total


def gate(hidden_in, norm_gain, part, depth):
    tokens = hidden_in.shape[0]
    piece = jax.ShapeDtypeStruct((depth, tokens, part), jnp.bfloat16)
    return call(
        functools.partial(gate_kernel, part, depth),
        (piece,) * 4 + (jax.ShapeDtypeStruct((tokens, HEAD), jnp.float32),),
        in_specs=[pl.BlockSpec(memory_space=pltpu.HBM), WHOLE],
        out_specs=[WHOLE] * 5,
        scratch_shapes=[
            pltpu.VMEM((depth, tokens, 4 * part), jnp.bfloat16),
            pltpu.VMEM((1, norm_gain.shape[0]), jnp.float32),
            pltpu.SemaphoreType.DMA((depth,)),
        ],
    )(pltpu.with_memory_space_constraint(hidden_in, pltpu.HBM), norm_gain)


def matmul_kernel(firsts, n_acts, n_more, sent, *refs):
    is_first = lax.axis_index("tensor") == 0
    acts, refs = refs[:n_acts], refs[n_acts:]
    slots, refs = refs[:len(firsts)], refs[len(firsts):]
    more, out_refs = refs[:n_more], refs[n_more:]
    more = [(ref, i) for ref in more for i in range(ref.shape[0])]
    right = [slot[...] for slot in slots]
    wide = 2 * HEAD
    for p in range(n_acts):
        total = jnp.dot(acts[p][firsts[0]], right[0], preferred_element_type=jnp.float32)
        for k in range(1, len(firsts)):
            total += jnp.dot(acts[p][firsts[k]], right[k], preferred_element_type=jnp.float32)
        if more:
            ref, i = more[p]
            total += ref[i]
        if not sent:
            out_refs[0][p] = total
            continue
        theirs_refs, mine_ref = out_refs[:-1], out_refs[-1]
        n_blocks = mine_ref.shape[1]
        per = n_acts * n_blocks // sent
        for g in range(n_blocks):
            low = total[:, g * wide:g * wide + HEAD]
            high = total[:, g * wide + HEAD:(g + 1) * wide]
            spot = p * n_blocks + g
            theirs_refs[spot // per][spot % per] = jnp.where(is_first, high, low).astype(jnp.bfloat16)
            mine_ref[p, g] = jnp.where(is_first, low, high)


def matmul(acts, slots, firsts, so_far=(), sent=0):
    n_blocks = slots[0].shape[1] // (2 * HEAD)
    tokens = acts[0].shape[1]
    args = [*acts, *slots, *so_far]
    if sent:
        out_shape = (jax.ShapeDtypeStruct((len(acts) * n_blocks // sent, tokens, HEAD), jnp.bfloat16),) * sent
        out_shape += (jax.ShapeDtypeStruct((len(acts), n_blocks, tokens, HEAD), jnp.float32),)
    else:
        out_shape = (jax.ShapeDtypeStruct((len(acts), tokens, n_blocks * 2 * HEAD), jnp.float32),)
    outs = call(
        functools.partial(matmul_kernel, firsts, len(acts), len(so_far), sent),
        out_shape,
        in_specs=[WHOLE] * len(args),
        out_specs=[WHOLE] * len(out_shape),
    )(*args)
    return outs if sent else outs[0]


def join_kernel(n_came, first, mine_ref, *refs):
    came_refs, out_refs = refs[:n_came], refs[n_came:]
    n_blocks = mine_ref.shape[1]
    per = len(out_refs) * n_blocks // n_came
    for p, out_ref in enumerate(out_refs):
        for g in range(n_blocks):
            spot = p * n_blocks + g
            came = came_refs[spot // per][spot % per].astype(jnp.float32)
            out_ref[g] = (mine_ref[first + p, g] + came).astype(out_ref.dtype)


def join(mine, came, types, first=0):
    return call(
        functools.partial(join_kernel, len(came), first),
        tuple(jax.ShapeDtypeStruct(mine.shape[1:], t) for t in types),
        in_specs=[WHOLE] * (1 + len(came)),
        out_specs=[WHOLE] * len(types),
    )(mine, *came)


def tables_kernel(lengths_ref, _, cosine_ref, sine_ref, allowed_ref, keep_ref):
    at = lax.broadcasted_iota(jnp.int32, cosine_ref.shape, 0)
    lane = lax.broadcasted_iota(jnp.int32, cosine_ref.shape, 1)
    pair = lax.rem(lane, HEAD // 2).astype(jnp.float32)
    angle = at.astype(jnp.float32) * jnp.exp(pair * (-2.0 * math.log(ROPE_BASE) / HEAD))
    cosine_ref[...] = jnp.cos(angle)
    sine_ref[...] = jnp.where(lane < HEAD // 2, -jnp.sin(angle), jnp.sin(angle))
    prompt = lengths_ref[0, 0]
    total_len = prompt + lengths_ref[0, 1]
    keep_ref[...] = ((at >= prompt - 1) & (at < total_len - 1)).astype(jnp.float32)
    query_at = lax.broadcasted_iota(jnp.int32, allowed_ref.shape, 0)
    key_at = lax.broadcasted_iota(jnp.int32, allowed_ref.shape, 1)
    allowed_ref[...] = ((key_at <= query_at) & (key_at < total_len)).astype(jnp.float32)


def tables(tokens, lengths, later_than):
    table = jax.ShapeDtypeStruct((tokens, HEAD), jnp.float32)
    allowed = jax.ShapeDtypeStruct((tokens, tokens), jnp.float32)
    return call(
        tables_kernel,
        (table, table, allowed, table),
        in_specs=[SCALARS, pl.BlockSpec(memory_space=pl.ANY)],
        out_specs=[WHOLE] * 4,
    )(lengths, later_than)


def scale_kernel(own_ref, other_ref, out_ref):
    squares = jnp.sum(own_ref[...] + other_ref[...], axis=1, keepdims=True)
    out_ref[...] = jnp.broadcast_to(lax.rsqrt(squares / D + EPSILON), out_ref.shape)


def inv_rms(own, other):
    return call(
        scale_kernel,
        jax.ShapeDtypeStruct(own.shape, jnp.float32),
        in_specs=[WHOLE] * 2,
        out_specs=WHOLE,
    )(own, other)


def summed(refs, index, scale_ref):
    total = refs[0][index]
    for ref in refs[1:]:
        total += ref[index].astype(jnp.float32)
    return total * scale_ref[...]


def turned(block, cosine_ref, sine_ref):
    half = HEAD // 2
    other = jnp.concatenate([block[:, half:], block[:, :half]], axis=1)
    return block * cosine_ref[...] + other * sine_ref[...]


def kv_kernel(own, r0, r1, r2, scale_ref, cosine_ref, sine_ref, out_ref):
    block = summed((own, r0, r1, r2), 0, scale_ref)
    spun = turned(block, cosine_ref, sine_ref)
    out_ref[...] = jnp.where(lax.axis_index("tensor") == 0, spun, block).astype(jnp.bfloat16)


def heads_kernel(first, n_parts, *refs):
    parts, refs = refs[:n_parts], refs[n_parts:]
    scale_ref, cosine_ref, sine_ref, allowed_ref, keep_ref, mine_ref, other_ref, *rest = refs
    earlier_refs, out_ref, scratch = rest[:-1], rest[-1], None
    if len(rest) > 1:
        earlier_ref, out_ref, scratch, sems = rest
        earlier_refs = [earlier_ref]
    copies = []

    def put(source, at):
        copies.append(pltpu.make_async_copy(source, out_ref.at[:, pl.ds(at, source.shape[1])], sems.at[len(copies)]))
        copies[-1].start()

    is_key = lax.axis_index("tensor") == 0
    mine, other = mine_ref[...], other_ref[...]
    keys = jnp.where(is_key, mine, other)
    values = jnp.where(is_key, other, mine)
    before = 0
    for earlier_ref in earlier_refs:
        put(earlier_ref, before)
        before += earlier_ref.shape[1]
    for i in range(first, parts[0].shape[0]):
        query = turned(summed(parts, i, scale_ref), cosine_ref, sine_ref).astype(jnp.bfloat16)
        scores = lax.dot_general(
            query, keys, (((1,), (1,)), ((), ())), preferred_element_type=jnp.float32
        ) * HEAD ** (-0.5)
        scores = jnp.where(allowed_ref[...] > 0.0, scores, -1e30)
        expo = jnp.exp(scores - jnp.max(scores, axis=-1, keepdims=True))
        attn = (expo / jnp.sum(expo, axis=-1, keepdims=True)).astype(jnp.bfloat16)
        mixed = jnp.dot(attn, values, preferred_element_type=jnp.float32)
        done = (mixed * keep_ref[...]).astype(jnp.bfloat16)
        if scratch is None:
            out_ref[:, (i - first) * HEAD:(i - first + 1) * HEAD] = done
        else:
            scratch[i - first] = done
            put(scratch.at[i - first], before + (i - first) * HEAD)
    for copy in copies:
        copy.wait()


def heads(parts, first, scale, tabled, mine, other, *earlier):
    args = [*parts, scale, *tabled, mine, other, *earlier]
    tokens = mine.shape[0]
    count = parts[0].shape[0] - first
    out_shape = jax.ShapeDtypeStruct((tokens, count * HEAD + sum(e.shape[1] for e in earlier)), jnp.bfloat16)
    scratch = [pltpu.VMEM((count, tokens, HEAD), jnp.bfloat16), pltpu.SemaphoreType.DMA((count + len(earlier),))]
    return call(
        functools.partial(heads_kernel, first, len(parts)),
        out_shape,
        result=bool(earlier),
        in_specs=[WHOLE] * len(args),
        out_specs=pl.BlockSpec(memory_space=pltpu.HBM) if earlier else WHOLE,
        scratch_shapes=scratch if earlier else [],
    )(*args)


def staged(hidden_in, norm_gain, projection, lengths):
    groups = lax.axis_size("groups")
    dp = lax.axis_size("dp")
    tensor = lax.axis_size("tensor")
    depth = dp // 2
    tokens = hidden_in.shape[0]
    part = projection.shape[1] // groups
    heads_local = QHEADS // tensor

    ring = [(i, (i + 2) % dp) for i in range(dp)]
    over_x = swap(dp)
    over_y = swap(groups)
    over_core = swap(tensor)
    across = [(g * dp + i, (g ^ 1) * dp + (i ^ 1)) for g in range(groups) for i in range(dp)]

    def to_core(a):
        return lax.ppermute(a, "tensor", over_core)

    def on_ring(a):
        return lax.ppermute(a, "dp", ring)

    def back(a):
        return lax.ppermute(a, "dp", [(j, i) for i, j in ring])

    def to_far(a):
        return lax.ppermute(a, ("groups", "dp"), across)

    def to_x(a):
        return lax.ppermute(a, "dp", over_x)

    def to_y(a):
        return lax.ppermute(a, "groups", over_y)

    def to_plane(three):
        return [to_far(three[0]), to_x(three[1]), to_y(three[2])]

    last = []

    def after(*values):
        held = lax.optimization_barrier(tuple(values) + tuple(last))[:len(values)]
        last[:] = held[:1]
        return held[0] if len(values) == 1 else held

    blocks = [[(QHEADS + c) * HEAD for c in range(tensor)]]
    blocks += [[(c * heads_local + i) * HEAD for c in range(tensor)] for i in range(heads_local)]
    columns = [blocks[0] + blocks[1], blocks[2] + blocks[3]]
    a0, = select(projection, part, columns[:1])
    a0 = after(a0)
    a1 = on_ring(a0)
    far, near_x, near_y, own, squares = after(*gate(after(hidden_in), norm_gain, part, depth))
    near_x = to_x(near_x)
    near_y = to_y(near_y)
    b0, = select(after(projection), part, columns[1:])
    b0, a0 = after(b0, a0)
    a3 = back(a0)
    other_squares = to_core(squares)
    tabled = after(*tables(tokens, lengths, after(squares)))
    scale = after(inv_rms(squares, after(other_squares)))

    a1, b0, far = after(a1, b0, far)
    b1 = on_ring(b0)
    far = to_far(far)
    a3, a1 = after(a3, a1)
    a2 = on_ring(a1)
    near_y = after(near_y)
    near_x = after(near_x)
    b1 = after(b1)
    b2 = on_ring(b1)
    early = (near_x, near_y, own)
    front = after(matmul(early, (a0, a1, a3), (0, 1, 3)))
    a2, b0 = after(a2, b0)
    b3 = back(b0)
    set_a = (a0, a1, a2, a3)

    *theirs, mine = after(*matmul(early, (a2,), (2,), (front,), sent=2))
    swapped = [to_core(t) for t in theirs]
    far = after(far)
    sums_x, sums_y, sums = after(*join(mine, after(*swapped), (jnp.bfloat16, jnp.bfloat16, jnp.float32)))
    sums_x = to_x(sums_x)
    sums_y = to_y(sums_y)
    acts = (far, own, near_x, near_y)
    *theirs, mine = after(*matmul((far,), set_a, (0, 1, 2, 3), sent=1))
    swapped = [to_core(t) for t in theirs]
    b2 = after(b2)
    swapped = [after(t) for t in swapped]
    sums_far = after(*join(mine, swapped, (jnp.bfloat16,)))
    sums_far = to_far(sums_far)
    sums_y = after(sums_y)
    sums_x = after(sums_x)
    front = after(matmul(acts, (b0, b1, b2), (0, 1, 2)))

    b3 = after(b3)
    parts_a = after(sums, sums_far, sums_x, sums_y)
    *theirs, mine = after(*matmul(acts, (b3,), (3,), (front,), sent=2))
    swapped = [to_core(t) for t in theirs]
    kv = after(call(
        kv_kernel,
        jax.ShapeDtypeStruct((tokens, HEAD), jnp.bfloat16),
        in_specs=[WHOLE] * 7,
        out_specs=WHOLE,
    )(*parts_a, scale, *tabled[:2]))
    vk = to_core(kv)
    sums_far, sums = after(*join(mine, (after(swapped[0]),), (jnp.bfloat16, jnp.float32)))
    sums_far = to_far(sums_far)
    sums_x, sums_y = after(*join(mine, (after(swapped[1]),), (jnp.bfloat16, jnp.bfloat16), first=2))
    sums_x = to_x(sums_x)
    sums_y = to_y(sums_y)
    vk = after(vk)
    one = after(heads(parts_a, 1, scale, tabled, kv, vk))
    sums_far = after(sums_far)
    sums_x, sums_y = after(sums_x, sums_y)
    return heads((sums, sums_far, sums_x, sums_y), 0, scale, tabled, kv, vk, one)


def local(hidden_in, norm_gain, projection, lengths):
    part = projection.shape[1] // lax.axis_size("groups")
    if lax.axis_size("dp") == 8 and part % HEAD == 0:
        return staged(hidden_in, norm_gain, projection, lengths)
    return general(hidden_in, norm_gain, projection, lengths)


def solution(mesh):
    in_specs = (
        P(("groups", "dp"), "tensor"),
        P("tensor"),
        P("tensor", "dp", None),
        P(("groups", "dp"), None),
    )
    out_specs = P(("groups", "dp"), "tensor")
    return jax.shard_map(local, mesh=mesh, in_specs=in_specs, out_specs=out_specs, check_vma=False)
```

```python
import functools
import math

import jax
import jax.numpy as jnp
from jax import lax
from jax.experimental import pallas as pl
from jax.experimental.pallas import tpu as pltpu
from jax.sharding import PartitionSpec as P

D = 12288
HEAD = 128
QHEADS = 6
ROPE_BASE = 1000000.0
EPSILON = 1e-05


def angles(seq_len):
    half = HEAD // 2
    positions = jnp.arange(seq_len, dtype=jnp.int32)
    freq = ROPE_BASE ** (-(jnp.arange(half, dtype=jnp.float32) * 2.0 / HEAD))
    angle = positions.astype(jnp.float32)[:, None] * freq[None, :]
    return jnp.cos(angle), jnp.sin(angle)


def rotate(block, cosine, sine):
    half = HEAD // 2
    first = block[:, :half]
    second = block[:, half:]
    return jnp.concatenate([first * cosine - second * sine, second * cosine + first * sine], axis=-1)


def attend_head(query, keys, values, allowed, keep):
    scores = lax.dot_general(
        query, keys, (((1,), (1,)), ((), ())), preferred_element_type=jnp.float32
    ) * HEAD ** (-0.5)
    scores = jnp.where(allowed, scores, -1e30)
    largest = jnp.max(scores, axis=-1, keepdims=True)
    expo = jnp.exp(scores - largest)
    attn = (expo / jnp.sum(expo, axis=-1, keepdims=True)).astype(jnp.bfloat16)
    mixed = jnp.dot(attn, values, preferred_element_type=jnp.float32)
    return (mixed * keep).astype(jnp.bfloat16)


def swap(size):
    return [(i, i ^ 1) for i in range(size)]


def general(hidden_in, norm_gain, projection, lengths):
    groups = lax.axis_size("groups")
    dp = lax.axis_size("dp")
    tensor = lax.axis_size("tensor")
    y = lax.axis_index("groups")
    place = lax.axis_index("dp")
    core = lax.axis_index("tensor")
    x = place % 2
    z = place // 2
    depth = dp // 2
    tokens = hidden_in.shape[0]
    rows = projection.shape[1]
    part = rows // groups
    heads_local = QHEADS // tensor

    ring = [(i, (i + 2) % dp) for i in range(dp)]
    over_x = swap(dp)
    over_y = swap(groups)
    over_core = swap(tensor)
    across = [(g * dp + i, (g ^ 1) * dp + (i ^ 1)) for g in range(groups) for i in range(dp)]

    mine = lax.dynamic_slice_in_dim(projection[0], y * part, part, 0)

    def column(owner, index):
        start = (QHEADS + owner) * HEAD if index == 0 else (owner * heads_local + index - 1) * HEAD
        return lax.dynamic_slice_in_dim(mine, start, HEAD, 1)

    n_cols = heads_local + 1
    theirs = jnp.concatenate([column(1 - core, i) for i in range(n_cols)], axis=1)
    other = lax.ppermute(theirs, "tensor", over_core)
    weights = []
    for i in range(n_cols):
        slot = jnp.concatenate([column(core, i), other[:, i * HEAD:(i + 1) * HEAD]], axis=0)
        weights.append([slot])
    for _ in range(depth - 1):
        for i in range(n_cols):
            weights[i].append(lax.ppermute(weights[i][-1], "dp", ring))

    wide32 = hidden_in.astype(jnp.float32)
    gated = (wide32 * norm_gain.astype(jnp.float32)[None, :]).astype(jnp.bfloat16)
    local_sq = jnp.sum(wide32 * wide32, axis=1)
    total_sq = local_sq + lax.ppermute(local_sq, "tensor", over_core)
    inv_rms = lax.rsqrt(total_sq / D + EPSILON)[:, None]

    def piece(dx, dy):
        slabs = []
        for k in range(depth):
            shard = ((z - k + depth) % depth) * 2 + (x ^ dx)
            slabs.append(lax.dynamic_slice_in_dim(gated, shard * rows + (y ^ dy) * part, part, 1))
        return jnp.stack(slabs)

    sent = [piece(1, 1), piece(1, 0), piece(0, 1)]
    held = [
        lax.ppermute(sent[0], ("groups", "dp"), across),
        lax.ppermute(sent[1], "dp", over_x),
        lax.ppermute(sent[2], "groups", over_y),
        piece(0, 0),
    ]
    acts = []
    for h in held:
        acts.append(jnp.concatenate([h, lax.ppermute(h, "tensor", over_core)], axis=2))
    acts = jnp.concatenate(acts, axis=1)

    cosine, sine = angles(tokens)
    positions = jnp.arange(tokens, dtype=jnp.int32)
    prompt = lengths[0, 0]
    total_len = prompt + lengths[0, 1]
    allowed = (positions[None, :] <= positions[:, None]) & (positions[None, :] < total_len)
    keep = ((positions >= prompt - 1) & (positions < total_len - 1)).astype(jnp.float32)[:, None]

    outs = []
    keys = values = None
    for i in range(n_cols):
        partial = sum(
            jnp.dot(acts[k], weights[i][k], preferred_element_type=jnp.float32) for k in range(depth)
        )
        blocks = partial.reshape(4, tokens, HEAD)
        low = blocks[:3].astype(jnp.bfloat16)
        summed = blocks[3]
        summed = summed + lax.ppermute(low[0], ("groups", "dp"), across).astype(jnp.float32)
        summed = summed + lax.ppermute(low[1], "dp", over_x).astype(jnp.float32)
        summed = summed + lax.ppermute(low[2], "groups", over_y).astype(jnp.float32)
        scaled = summed * inv_rms
        if i == 0:
            turned = rotate(scaled, cosine, sine)
            kv = jnp.where(core == 0, turned, scaled).astype(jnp.bfloat16)
            vk = lax.ppermute(kv, "tensor", over_core)
            keys = jnp.where(core == 0, kv, vk)
            values = jnp.where(core == 0, vk, kv)
        else:
            query = rotate(scaled, cosine, sine).astype(jnp.bfloat16)
            outs.append(attend_head(query, keys, values, allowed, keep))
    return jnp.concatenate(outs, axis=1)


VMEM = pltpu.VMEM
PLANE = ((1, 1), (1, 0), (0, 1), (0, 0))
WHOLE = pl.BlockSpec(memory_space=VMEM)
SCALARS = pl.BlockSpec(memory_space=pltpu.SMEM)


def call(kernel, out_shape, limit=12, result=False, **kwargs):
    if not result:
        out_shape = jax.tree.map(lambda s: pltpu.VMEM(s.shape, s.dtype), out_shape)
    return pl.pallas_call(
        kernel,
        out_shape=out_shape,
        compiler_params=pltpu.CompilerParams(vmem_limit_bytes=limit * 2**20),
        cost_estimate=pl.CostEstimate(flops=1, bytes_accessed=1, transcendentals=0),
        **kwargs,
    )


def select_kernel(columns, part, rows_ref, *refs):
    out_refs, sems = refs[:len(columns)], refs[-1]
    rows = pl.ds(pl.multiple_of(lax.axis_index("groups") * part, HEAD), part)
    copies = []
    for starts, out_ref in zip(columns, out_refs):
        at = 0
        while at < len(starts):
            more = 1
            while at + more < len(starts) and starts[at + more] == starts[at] + more * HEAD:
                more += 1
            copies.append(pltpu.make_async_copy(
                rows_ref.at[0, rows, pl.ds(starts[at], more * HEAD)],
                out_ref.at[:, pl.ds(at * HEAD, more * HEAD)],
                sems.at[len(copies)],
            ))
            at += more
    for copy in copies:
        copy.start()
    for copy in copies:
        copy.wait()


def select(projection, part, columns):
    chunk = jax.ShapeDtypeStruct((part, len(columns[0]) * HEAD), projection.dtype)
    out_shape = (chunk,) * len(columns)
    return call(
        functools.partial(select_kernel, columns, part),
        out_shape,
        in_specs=[pl.BlockSpec(memory_space=pltpu.HBM)],
        out_specs=[WHOLE] * len(out_shape),
        scratch_shapes=[pltpu.SemaphoreType.DMA((len(columns) * len(columns[0]),))],
    )(pltpu.with_memory_space_constraint(projection, pltpu.HBM))


def gate_kernel(part, depth, hidden_ref, gain_ref, *refs):
    piece_refs, (sq_ref, slab_ref, row_ref, sems) = refs[:4], refs[4:]
    place = lax.axis_index("dp")
    x, z, y = place % 2, place // 2, lax.axis_index("groups")
    wide = 4 * part
    columns = [pl.ds(pl.multiple_of(lax.rem(z - k + depth, depth) * wide, HEAD), wide) for k in range(depth)]
    copies = [pltpu.make_async_copy(hidden_ref.at[:, c], slab_ref.at[k], sems.at[k]) for k, c in enumerate(columns)]
    for copy in copies:
        copy.start()
    row_ref[0, :] = gain_ref[...].astype(jnp.float32)
    tokens = hidden_ref.shape[0]
    height = 64
    for k, copy in enumerate(copies):
        copy.wait()
        for top in range(0, tokens, height):
            rows = slice(top, top + height)
            total = jnp.zeros((height, HEAD), jnp.float32)
            for piece_ref, (dx, dy) in zip(piece_refs, PLANE):
                start = ((x ^ dx) * 2 + (y ^ dy)) * part
                whole = slab_ref[k, rows, pl.ds(pl.multiple_of(start, HEAD), part)].astype(jnp.float32)
                at = lax.rem(z - k + depth, depth) * wide + start
                gain = row_ref[:, pl.ds(pl.multiple_of(at, HEAD), part)]
                piece_ref[k, rows] = (whole * gain).astype(jnp.bfloat16)
                square = whole * whole
                for j in range(0, part, HEAD):
                    total += square[:, j:j + HEAD]
            sq_ref[rows] = total if k == 0 else sq_ref[rows] + total


def gate(hidden_in, norm_gain, part, depth):
    tokens = hidden_in.shape[0]
    piece = jax.ShapeDtypeStruct((depth, tokens, part), jnp.bfloat16)
    return call(
        functools.partial(gate_kernel, part, depth),
        (piece,) * 4 + (jax.ShapeDtypeStruct((tokens, HEAD), jnp.float32),),
        in_specs=[pl.BlockSpec(memory_space=pltpu.HBM), WHOLE],
        out_specs=[WHOLE] * 5,
        scratch_shapes=[
            pltpu.VMEM((depth, tokens, 4 * part), jnp.bfloat16),
            pltpu.VMEM((1, norm_gain.shape[0]), jnp.float32),
            pltpu.SemaphoreType.DMA((depth,)),
        ],
    )(pltpu.with_memory_space_constraint(hidden_in, pltpu.HBM), norm_gain)


def matmul_kernel(firsts, n_acts, n_more, sent, *refs):
    is_first = lax.axis_index("tensor") == 0
    acts, refs = refs[:n_acts], refs[n_acts:]
    slots, refs = refs[:len(firsts)], refs[len(firsts):]
    more, out_refs = refs[:n_more], refs[n_more:]
    more = [(ref, i) for ref in more for i in range(ref.shape[0])]
    right = [slot[...] for slot in slots]
    wide = 2 * HEAD
    for p in range(n_acts):
        total = jnp.dot(acts[p][firsts[0]], right[0], preferred_element_type=jnp.float32)
        for k in range(1, len(firsts)):
            total += jnp.dot(acts[p][firsts[k]], right[k], preferred_element_type=jnp.float32)
        if more:
            ref, i = more[p]
            total += ref[i]
        if not sent:
            out_refs[0][p] = total
            continue
        theirs_refs, mine_ref = out_refs[:-1], out_refs[-1]
        n_blocks = mine_ref.shape[1]
        per = n_acts * n_blocks // sent
        for g in range(n_blocks):
            low = total[:, g * wide:g * wide + HEAD]
            high = total[:, g * wide + HEAD:(g + 1) * wide]
            spot = p * n_blocks + g
            theirs_refs[spot // per][spot % per] = jnp.where(is_first, high, low).astype(jnp.bfloat16)
            mine_ref[p, g] = jnp.where(is_first, low, high)


def matmul(acts, slots, firsts, so_far=(), sent=0):
    n_blocks = slots[0].shape[1] // (2 * HEAD)
    tokens = acts[0].shape[1]
    args = [*acts, *slots, *so_far]
    if sent:
        out_shape = (jax.ShapeDtypeStruct((len(acts) * n_blocks // sent, tokens, HEAD), jnp.bfloat16),) * sent
        out_shape += (jax.ShapeDtypeStruct((len(acts), n_blocks, tokens, HEAD), jnp.float32),)
    else:
        out_shape = (jax.ShapeDtypeStruct((len(acts), tokens, n_blocks * 2 * HEAD), jnp.float32),)
    outs = call(
        functools.partial(matmul_kernel, firsts, len(acts), len(so_far), sent),
        out_shape,
        in_specs=[WHOLE] * len(args),
        out_specs=[WHOLE] * len(out_shape),
    )(*args)
    return outs if sent else outs[0]


def join_kernel(n_came, first, mine_ref, *refs):
    came_refs, out_refs = refs[:n_came], refs[n_came:]
    n_blocks = mine_ref.shape[1]
    per = len(out_refs) * n_blocks // n_came
    for p, out_ref in enumerate(out_refs):
        for g in range(n_blocks):
            spot = p * n_blocks + g
            came = came_refs[spot // per][spot % per].astype(jnp.float32)
            out_ref[g] = (mine_ref[first + p, g] + came).astype(out_ref.dtype)


def join(mine, came, types, first=0):
    return call(
        functools.partial(join_kernel, len(came), first),
        tuple(jax.ShapeDtypeStruct(mine.shape[1:], t) for t in types),
        in_specs=[WHOLE] * (1 + len(came)),
        out_specs=[WHOLE] * len(types),
    )(mine, *came)


def tables_kernel(lengths_ref, _, cosine_ref, sine_ref, allowed_ref, keep_ref):
    at = lax.broadcasted_iota(jnp.int32, cosine_ref.shape, 0)
    lane = lax.broadcasted_iota(jnp.int32, cosine_ref.shape, 1)
    pair = lax.rem(lane, HEAD // 2).astype(jnp.float32)
    angle = at.astype(jnp.float32) * jnp.exp(pair * (-2.0 * math.log(ROPE_BASE) / HEAD))
    cosine_ref[...] = jnp.cos(angle)
    sine_ref[...] = jnp.where(lane < HEAD // 2, -jnp.sin(angle), jnp.sin(angle))
    prompt = lengths_ref[0, 0]
    total_len = prompt + lengths_ref[0, 1]
    keep_ref[...] = ((at >= prompt - 1) & (at < total_len - 1)).astype(jnp.float32)
    query_at = lax.broadcasted_iota(jnp.int32, allowed_ref.shape, 0)
    key_at = lax.broadcasted_iota(jnp.int32, allowed_ref.shape, 1)
    allowed_ref[...] = ((key_at <= query_at) & (key_at < total_len)).astype(jnp.float32)


def tables(tokens, lengths, later_than):
    table = jax.ShapeDtypeStruct((tokens, HEAD), jnp.float32)
    allowed = jax.ShapeDtypeStruct((tokens, tokens), jnp.float32)
    return call(
        tables_kernel,
        (table, table, allowed, table),
        in_specs=[SCALARS, pl.BlockSpec(memory_space=pl.ANY)],
        out_specs=[WHOLE] * 4,
    )(lengths, later_than)


def scale_kernel(own_ref, other_ref, out_ref):
    squares = jnp.sum(own_ref[...] + other_ref[...], axis=1, keepdims=True)
    out_ref[...] = jnp.broadcast_to(lax.rsqrt(squares / D + EPSILON), out_ref.shape)


def inv_rms(own, other):
    return call(
        scale_kernel,
        jax.ShapeDtypeStruct(own.shape, jnp.float32),
        in_specs=[WHOLE] * 2,
        out_specs=WHOLE,
    )(own, other)


def summed(refs, index, scale_ref):
    total = refs[0][index]
    for ref in refs[1:]:
        total += ref[index].astype(jnp.float32)
    return total * scale_ref[...]


def turned(block, cosine_ref, sine_ref):
    half = HEAD // 2
    other = jnp.concatenate([block[:, half:], block[:, :half]], axis=1)
    return block * cosine_ref[...] + other * sine_ref[...]


def kv_kernel(own, r0, r1, r2, scale_ref, cosine_ref, sine_ref, out_ref):
    block = summed((own, r0, r1, r2), 0, scale_ref)
    spun = turned(block, cosine_ref, sine_ref)
    out_ref[...] = jnp.where(lax.axis_index("tensor") == 0, spun, block).astype(jnp.bfloat16)


def heads_kernel(first, n_parts, *refs):
    parts, refs = refs[:n_parts], refs[n_parts:]
    scale_ref, cosine_ref, sine_ref, allowed_ref, keep_ref, mine_ref, other_ref, *rest = refs
    earlier_refs, out_ref, scratch = rest[:-1], rest[-1], None
    if len(rest) > 1:
        earlier_ref, out_ref, scratch, sems = rest
        earlier_refs = [earlier_ref]
    copies = []

    def put(source, at):
        copies.append(pltpu.make_async_copy(source, out_ref.at[:, pl.ds(at, source.shape[1])], sems.at[len(copies)]))
        copies[-1].start()

    is_key = lax.axis_index("tensor") == 0
    mine, other = mine_ref[...], other_ref[...]
    keys = jnp.where(is_key, mine, other)
    values = jnp.where(is_key, other, mine)
    before = 0
    for earlier_ref in earlier_refs:
        put(earlier_ref, before)
        before += earlier_ref.shape[1]
    tokens = mine.shape[0]
    count = parts[0].shape[0] - first
    query = [turned(summed(parts, first + i, scale_ref), cosine_ref, sine_ref).astype(jnp.bfloat16) for i in range(count)]
    scores = lax.dot_general(
        jnp.concatenate(query, axis=0), keys, (((1,), (1,)), ((), ())), preferred_element_type=jnp.float32
    ) * HEAD ** (-0.5)
    allowed = jnp.concatenate([allowed_ref[...] > 0.0] * count, axis=0)
    scores = jnp.where(allowed, scores, -1e30)
    expo = jnp.exp(scores - jnp.max(scores, axis=-1, keepdims=True))
    attn = (expo * (1.0 / jnp.sum(expo, axis=-1, keepdims=True))).astype(jnp.bfloat16)
    mixed = jnp.dot(attn, values, preferred_element_type=jnp.float32)
    for i in range(count):
        done = (mixed[i * tokens:(i + 1) * tokens] * keep_ref[...]).astype(jnp.bfloat16)
        if scratch is None:
            out_ref[:, i * HEAD:(i + 1) * HEAD] = done
        else:
            scratch[i] = done
            put(scratch.at[i], before + i * HEAD)
    for copy in copies:
        copy.wait()


def heads(parts, first, scale, tabled, mine, other, *earlier):
    args = [*parts, scale, *tabled, mine, other, *earlier]
    tokens = mine.shape[0]
    count = parts[0].shape[0] - first
    out_shape = jax.ShapeDtypeStruct((tokens, count * HEAD + sum(e.shape[1] for e in earlier)), jnp.bfloat16)
    scratch = [pltpu.VMEM((count, tokens, HEAD), jnp.bfloat16), pltpu.SemaphoreType.DMA((count + len(earlier),))]
    return call(
        functools.partial(heads_kernel, first, len(parts)),
        out_shape,
        result=bool(earlier),
        in_specs=[WHOLE] * len(args),
        out_specs=pl.BlockSpec(memory_space=pltpu.HBM) if earlier else WHOLE,
        scratch_shapes=scratch if earlier else [],
    )(*args)


def staged(hidden_in, norm_gain, projection, lengths):
    groups = lax.axis_size("groups")
    dp = lax.axis_size("dp")
    tensor = lax.axis_size("tensor")
    depth = dp // 2
    tokens = hidden_in.shape[0]
    part = projection.shape[1] // groups
    heads_local = QHEADS // tensor

    ring = [(i, (i + 2) % dp) for i in range(dp)]
    over_x = swap(dp)
    over_y = swap(groups)
    over_core = swap(tensor)
    across = [(g * dp + i, (g ^ 1) * dp + (i ^ 1)) for g in range(groups) for i in range(dp)]

    def to_core(a):
        return lax.ppermute(a, "tensor", over_core)

    def on_ring(a):
        return lax.ppermute(a, "dp", ring)

    def back(a):
        return lax.ppermute(a, "dp", [(j, i) for i, j in ring])

    def to_far(a):
        return lax.ppermute(a, ("groups", "dp"), across)

    def to_x(a):
        return lax.ppermute(a, "dp", over_x)

    def to_y(a):
        return lax.ppermute(a, "groups", over_y)

    def to_plane(three):
        return [to_far(three[0]), to_x(three[1]), to_y(three[2])]

    last = []

    def after(*values):
        held = lax.optimization_barrier(tuple(values) + tuple(last))[:len(values)]
        last[:] = held[:1]
        return held[0] if len(values) == 1 else held

    blocks = [[(QHEADS + c) * HEAD for c in range(tensor)]]
    blocks += [[(c * heads_local + i) * HEAD for c in range(tensor)] for i in range(heads_local)]
    columns = [blocks[0] + blocks[1], blocks[2] + blocks[3]]
    a0, = select(projection, part, columns[:1])
    a0 = after(a0)
    a1 = on_ring(a0)
    far, near_x, near_y, own, squares = after(*gate(after(hidden_in), norm_gain, part, depth))
    near_x = to_x(near_x)
    near_y = to_y(near_y)
    b0, = select(after(projection), part, columns[1:])
    b0, a0 = after(b0, a0)
    a3 = back(a0)
    other_squares = to_core(squares)
    tabled = after(*tables(tokens, lengths, after(squares)))
    scale = after(inv_rms(squares, after(other_squares)))

    a1, b0, far = after(a1, b0, far)
    b1 = on_ring(b0)
    far = to_far(far)
    a3, a1 = after(a3, a1)
    a2 = on_ring(a1)
    near_y = after(near_y)
    near_x = after(near_x)
    b1 = after(b1)
    b2 = on_ring(b1)
    early = (near_x, near_y, own)
    front = after(matmul(early, (a0, a1, a3), (0, 1, 3)))
    a2 = after(a2)
    set_a = (a0, a1, a2, a3)

    *theirs, mine = after(*matmul(early, (a2,), (2,), (front,), sent=2))
    swapped = [to_core(t) for t in theirs]
    far, b0 = after(far, b0)
    b3 = back(b0)
    sums_x, sums_y, sums = after(*join(mine, after(*swapped), (jnp.bfloat16, jnp.bfloat16, jnp.float32)))
    sums_x = to_x(sums_x)
    sums_y = to_y(sums_y)
    acts = (far, own, near_x, near_y)
    *theirs, mine = after(*matmul((far,), set_a, (0, 1, 2, 3), sent=1))
    swapped = [to_core(t) for t in theirs]
    b2 = after(b2)
    swapped = [after(t) for t in swapped]
    sums_far = after(*join(mine, swapped, (jnp.bfloat16,)))
    sums_far = to_far(sums_far)
    sums_y = after(sums_y)
    sums_x = after(sums_x)
    front = after(matmul(acts, (b0, b1, b2), (0, 1, 2)))

    b3 = after(b3)
    parts_a = after(sums, sums_far, sums_x, sums_y)
    *theirs, mine = after(*matmul(acts, (b3,), (3,), (front,), sent=2))
    swapped = [to_core(t) for t in theirs]
    kv = after(call(
        kv_kernel,
        jax.ShapeDtypeStruct((tokens, HEAD), jnp.bfloat16),
        in_specs=[WHOLE] * 7,
        out_specs=WHOLE,
    )(*parts_a, scale, *tabled[:2]))
    vk = to_core(kv)
    sums_far, sums = after(*join(mine, (after(swapped[0]),), (jnp.bfloat16, jnp.float32)))
    sums_far = to_far(sums_far)
    sums_x, sums_y = after(*join(mine, (after(swapped[1]),), (jnp.bfloat16, jnp.bfloat16), first=2))
    sums_x = to_x(sums_x)
    sums_y = to_y(sums_y)
    vk = after(vk)
    one = after(heads(parts_a, 1, scale, tabled, kv, vk))
    sums_far = after(sums_far)
    sums_x, sums_y = after(sums_x, sums_y)
    return heads((sums, sums_far, sums_x, sums_y), 0, scale, tabled, kv, vk, one)


def local(hidden_in, norm_gain, projection, lengths):
    part = projection.shape[1] // lax.axis_size("groups")
    if lax.axis_size("dp") == 8 and part % HEAD == 0:
        return staged(hidden_in, norm_gain, projection, lengths)
    return general(hidden_in, norm_gain, projection, lengths)


def solution(mesh):
    in_specs = (
        P(("groups", "dp"), "tensor"),
        P("tensor"),
        P("tensor", "dp", None),
        P(("groups", "dp"), None),
    )
    out_specs = P(("groups", "dp"), "tensor")
    return jax.shard_map(local, mesh=mesh, in_specs=in_specs, out_specs=out_specs, check_vma=False)
```

```python
import functools
import math

import jax
import jax.numpy as jnp
from jax import lax
from jax.experimental import pallas as pl
from jax.experimental.pallas import tpu as pltpu
from jax.sharding import PartitionSpec as P

D = 12288
HEAD = 128
QHEADS = 6
ROPE_BASE = 1000000.0
EPSILON = 1e-05


def angles(seq_len):
    half = HEAD // 2
    positions = jnp.arange(seq_len, dtype=jnp.int32)
    freq = ROPE_BASE ** (-(jnp.arange(half, dtype=jnp.float32) * 2.0 / HEAD))
    angle = positions.astype(jnp.float32)[:, None] * freq[None, :]
    return jnp.cos(angle), jnp.sin(angle)


def rotate(block, cosine, sine):
    half = HEAD // 2
    first = block[:, :half]
    second = block[:, half:]
    return jnp.concatenate([first * cosine - second * sine, second * cosine + first * sine], axis=-1)


def attend_head(query, keys, values, allowed, keep):
    scores = lax.dot_general(
        query, keys, (((1,), (1,)), ((), ())), preferred_element_type=jnp.float32
    ) * HEAD ** (-0.5)
    scores = jnp.where(allowed, scores, -1e30)
    largest = jnp.max(scores, axis=-1, keepdims=True)
    expo = jnp.exp(scores - largest)
    attn = (expo / jnp.sum(expo, axis=-1, keepdims=True)).astype(jnp.bfloat16)
    mixed = jnp.dot(attn, values, preferred_element_type=jnp.float32)
    return (mixed * keep).astype(jnp.bfloat16)


def swap(size):
    return [(i, i ^ 1) for i in range(size)]


def general(hidden_in, norm_gain, projection, lengths):
    groups = lax.axis_size("groups")
    dp = lax.axis_size("dp")
    tensor = lax.axis_size("tensor")
    y = lax.axis_index("groups")
    place = lax.axis_index("dp")
    core = lax.axis_index("tensor")
    x = place % 2
    z = place // 2
    depth = dp // 2
    tokens = hidden_in.shape[0]
    rows = projection.shape[1]
    part = rows // groups
    heads_local = QHEADS // tensor

    ring = [(i, (i + 2) % dp) for i in range(dp)]
    over_x = swap(dp)
    over_y = swap(groups)
    over_core = swap(tensor)
    across = [(g * dp + i, (g ^ 1) * dp + (i ^ 1)) for g in range(groups) for i in range(dp)]

    mine = lax.dynamic_slice_in_dim(projection[0], y * part, part, 0)

    def column(owner, index):
        start = (QHEADS + owner) * HEAD if index == 0 else (owner * heads_local + index - 1) * HEAD
        return lax.dynamic_slice_in_dim(mine, start, HEAD, 1)

    n_cols = heads_local + 1
    theirs = jnp.concatenate([column(1 - core, i) for i in range(n_cols)], axis=1)
    other = lax.ppermute(theirs, "tensor", over_core)
    weights = []
    for i in range(n_cols):
        slot = jnp.concatenate([column(core, i), other[:, i * HEAD:(i + 1) * HEAD]], axis=0)
        weights.append([slot])
    for _ in range(depth - 1):
        for i in range(n_cols):
            weights[i].append(lax.ppermute(weights[i][-1], "dp", ring))

    wide32 = hidden_in.astype(jnp.float32)
    gated = (wide32 * norm_gain.astype(jnp.float32)[None, :]).astype(jnp.bfloat16)
    local_sq = jnp.sum(wide32 * wide32, axis=1)
    total_sq = local_sq + lax.ppermute(local_sq, "tensor", over_core)
    inv_rms = lax.rsqrt(total_sq / D + EPSILON)[:, None]

    def piece(dx, dy):
        slabs = []
        for k in range(depth):
            shard = ((z - k + depth) % depth) * 2 + (x ^ dx)
            slabs.append(lax.dynamic_slice_in_dim(gated, shard * rows + (y ^ dy) * part, part, 1))
        return jnp.stack(slabs)

    sent = [piece(1, 1), piece(1, 0), piece(0, 1)]
    held = [
        lax.ppermute(sent[0], ("groups", "dp"), across),
        lax.ppermute(sent[1], "dp", over_x),
        lax.ppermute(sent[2], "groups", over_y),
        piece(0, 0),
    ]
    acts = []
    for h in held:
        acts.append(jnp.concatenate([h, lax.ppermute(h, "tensor", over_core)], axis=2))
    acts = jnp.concatenate(acts, axis=1)

    cosine, sine = angles(tokens)
    positions = jnp.arange(tokens, dtype=jnp.int32)
    prompt = lengths[0, 0]
    total_len = prompt + lengths[0, 1]
    allowed = (positions[None, :] <= positions[:, None]) & (positions[None, :] < total_len)
    keep = ((positions >= prompt - 1) & (positions < total_len - 1)).astype(jnp.float32)[:, None]

    outs = []
    keys = values = None
    for i in range(n_cols):
        partial = sum(
            jnp.dot(acts[k], weights[i][k], preferred_element_type=jnp.float32) for k in range(depth)
        )
        blocks = partial.reshape(4, tokens, HEAD)
        low = blocks[:3].astype(jnp.bfloat16)
        summed = blocks[3]
        summed = summed + lax.ppermute(low[0], ("groups", "dp"), across).astype(jnp.float32)
        summed = summed + lax.ppermute(low[1], "dp", over_x).astype(jnp.float32)
        summed = summed + lax.ppermute(low[2], "groups", over_y).astype(jnp.float32)
        scaled = summed * inv_rms
        if i == 0:
            turned = rotate(scaled, cosine, sine)
            kv = jnp.where(core == 0, turned, scaled).astype(jnp.bfloat16)
            vk = lax.ppermute(kv, "tensor", over_core)
            keys = jnp.where(core == 0, kv, vk)
            values = jnp.where(core == 0, vk, kv)
        else:
            query = rotate(scaled, cosine, sine).astype(jnp.bfloat16)
            outs.append(attend_head(query, keys, values, allowed, keep))
    return jnp.concatenate(outs, axis=1)


VMEM = pltpu.VMEM
PLANE = ((1, 1), (1, 0), (0, 1), (0, 0))
WHOLE = pl.BlockSpec(memory_space=VMEM)
SCALARS = pl.BlockSpec(memory_space=pltpu.SMEM)


def call(kernel, out_shape, limit=12, result=False, **kwargs):
    if not result:
        out_shape = jax.tree.map(lambda s: pltpu.VMEM(s.shape, s.dtype), out_shape)
    return pl.pallas_call(
        kernel,
        out_shape=out_shape,
        compiler_params=pltpu.CompilerParams(vmem_limit_bytes=limit * 2**20),
        cost_estimate=pl.CostEstimate(flops=1, bytes_accessed=1, transcendentals=0),
        **kwargs,
    )


def select_kernel(columns, part, rows_ref, *refs):
    out_refs, sems = refs[:len(columns)], refs[-1]
    rows = pl.ds(pl.multiple_of(lax.axis_index("groups") * part, HEAD), part)
    copies = []
    for starts, out_ref in zip(columns, out_refs):
        at = 0
        while at < len(starts):
            more = 1
            while at + more < len(starts) and starts[at + more] == starts[at] + more * HEAD:
                more += 1
            copies.append(pltpu.make_async_copy(
                rows_ref.at[0, rows, pl.ds(starts[at], more * HEAD)],
                out_ref.at[:, pl.ds(at * HEAD, more * HEAD)],
                sems.at[len(copies)],
            ))
            at += more
    for copy in copies:
        copy.start()
    for copy in copies:
        copy.wait()


def select(projection, part, columns):
    chunk = jax.ShapeDtypeStruct((part, len(columns[0]) * HEAD), projection.dtype)
    out_shape = (chunk,) * len(columns)
    return call(
        functools.partial(select_kernel, columns, part),
        out_shape,
        in_specs=[pl.BlockSpec(memory_space=pltpu.HBM)],
        out_specs=[WHOLE] * len(out_shape),
        scratch_shapes=[pltpu.SemaphoreType.DMA((len(columns) * len(columns[0]),))],
    )(pltpu.with_memory_space_constraint(projection, pltpu.HBM))


def gate_kernel(part, depth, hidden_ref, gain_ref, *refs):
    piece_refs, (sq_ref, slab_ref, flat_ref, row_ref, sems) = refs[:4], refs[4:]
    place = lax.axis_index("dp")
    x, z, y = place % 2, place // 2, lax.axis_index("groups")
    wide = 4 * part
    columns = [pl.ds(pl.multiple_of(lax.rem(z - k + depth, depth) * wide, HEAD), wide) for k in range(depth)]
    copies = [pltpu.make_async_copy(hidden_ref.at[:, c], slab_ref.at[k], sems.at[k]) for k, c in enumerate(columns)]
    gain_copy = pltpu.make_async_copy(gain_ref, flat_ref, sems.at[depth])
    gain_copy.start()
    for copy in copies:
        copy.start()
    gain_copy.wait()
    row_ref[0, :] = flat_ref[...].astype(jnp.float32)
    tokens = hidden_ref.shape[0]
    height = 64
    for k, copy in enumerate(copies):
        copy.wait()
        for top in range(0, tokens, height):
            rows = slice(top, top + height)
            total = jnp.zeros((height, HEAD), jnp.float32)
            for piece_ref, (dx, dy) in zip(piece_refs, PLANE):
                start = ((x ^ dx) * 2 + (y ^ dy)) * part
                whole = slab_ref[k, rows, pl.ds(pl.multiple_of(start, HEAD), part)].astype(jnp.float32)
                at = lax.rem(z - k + depth, depth) * wide + start
                gain = row_ref[:, pl.ds(pl.multiple_of(at, HEAD), part)]
                piece_ref[k, rows] = (whole * gain).astype(jnp.bfloat16)
                square = whole * whole
                for j in range(0, part, HEAD):
                    total += square[:, j:j + HEAD]
            sq_ref[rows] = total if k == 0 else sq_ref[rows] + total


def gate(hidden_in, norm_gain, part, depth):
    tokens = hidden_in.shape[0]
    piece = jax.ShapeDtypeStruct((depth, tokens, part), jnp.bfloat16)
    return call(
        functools.partial(gate_kernel, part, depth),
        (piece,) * 4 + (jax.ShapeDtypeStruct((tokens, HEAD), jnp.float32),),
        in_specs=[pl.BlockSpec(memory_space=pltpu.HBM)] * 2,
        out_specs=[WHOLE] * 5,
        scratch_shapes=[
            pltpu.VMEM((depth, tokens, 4 * part), jnp.bfloat16),
            pltpu.VMEM(norm_gain.shape, norm_gain.dtype),
            pltpu.VMEM((1, norm_gain.shape[0]), jnp.float32),
            pltpu.SemaphoreType.DMA((depth + 1,)),
        ],
    )(*(pltpu.with_memory_space_constraint(a, pltpu.HBM) for a in (hidden_in, norm_gain)))


def matmul_kernel(firsts, n_acts, n_more, sent, *refs):
    is_first = lax.axis_index("tensor") == 0
    acts, refs = refs[:n_acts], refs[n_acts:]
    slots, refs = refs[:len(firsts)], refs[len(firsts):]
    more, out_refs = refs[:n_more], refs[n_more:]
    more = [(ref, i) for ref in more for i in range(ref.shape[0])]
    right = [slot[...] for slot in slots]
    wide = 2 * HEAD
    for p in range(n_acts):
        total = jnp.dot(acts[p][firsts[0]], right[0], preferred_element_type=jnp.float32)
        for k in range(1, len(firsts)):
            total += jnp.dot(acts[p][firsts[k]], right[k], preferred_element_type=jnp.float32)
        if more:
            ref, i = more[p]
            total += ref[i]
        if not sent:
            out_refs[0][p] = total
            continue
        theirs_refs, mine_ref = out_refs[:-1], out_refs[-1]
        n_blocks = mine_ref.shape[1]
        per = n_acts * n_blocks // sent
        for g in range(n_blocks):
            low = total[:, g * wide:g * wide + HEAD]
            high = total[:, g * wide + HEAD:(g + 1) * wide]
            spot = p * n_blocks + g
            theirs_refs[spot // per][spot % per] = jnp.where(is_first, high, low).astype(jnp.bfloat16)
            mine_ref[p, g] = jnp.where(is_first, low, high)


def matmul(acts, slots, firsts, so_far=(), sent=0):
    n_blocks = slots[0].shape[1] // (2 * HEAD)
    tokens = acts[0].shape[1]
    args = [*acts, *slots, *so_far]
    if sent:
        out_shape = (jax.ShapeDtypeStruct((len(acts) * n_blocks // sent, tokens, HEAD), jnp.bfloat16),) * sent
        out_shape += (jax.ShapeDtypeStruct((len(acts), n_blocks, tokens, HEAD), jnp.float32),)
    else:
        out_shape = (jax.ShapeDtypeStruct((len(acts), tokens, n_blocks * 2 * HEAD), jnp.float32),)
    outs = call(
        functools.partial(matmul_kernel, firsts, len(acts), len(so_far), sent),
        out_shape,
        in_specs=[WHOLE] * len(args),
        out_specs=[WHOLE] * len(out_shape),
    )(*args)
    return outs if sent else outs[0]


def join_kernel(n_came, first, mine_ref, *refs):
    came_refs, out_refs = refs[:n_came], refs[n_came:]
    n_blocks = mine_ref.shape[1]
    per = len(out_refs) * n_blocks // n_came
    for p, out_ref in enumerate(out_refs):
        for g in range(n_blocks):
            spot = p * n_blocks + g
            came = came_refs[spot // per][spot % per].astype(jnp.float32)
            out_ref[g] = (mine_ref[first + p, g] + came).astype(out_ref.dtype)


def join(mine, came, types, first=0):
    return call(
        functools.partial(join_kernel, len(came), first),
        tuple(jax.ShapeDtypeStruct(mine.shape[1:], t) for t in types),
        in_specs=[WHOLE] * (1 + len(came)),
        out_specs=[WHOLE] * len(types),
    )(mine, *came)


def tables_kernel(lengths_ref, _, cosine_ref, sine_ref, allowed_ref, keep_ref):
    at = lax.broadcasted_iota(jnp.int32, cosine_ref.shape, 0)
    lane = lax.broadcasted_iota(jnp.int32, cosine_ref.shape, 1)
    pair = lax.rem(lane, HEAD // 2).astype(jnp.float32)
    angle = at.astype(jnp.float32) * jnp.exp(pair * (-2.0 * math.log(ROPE_BASE) / HEAD))
    cosine_ref[...] = jnp.cos(angle)
    sine_ref[...] = jnp.where(lane < HEAD // 2, -jnp.sin(angle), jnp.sin(angle))
    prompt = lengths_ref[0, 0]
    total_len = prompt + lengths_ref[0, 1]
    keep_ref[...] = ((at >= prompt - 1) & (at < total_len - 1)).astype(jnp.float32)
    query_at = lax.broadcasted_iota(jnp.int32, allowed_ref.shape, 0)
    key_at = lax.broadcasted_iota(jnp.int32, allowed_ref.shape, 1)
    allowed_ref[...] = ((key_at <= query_at) & (key_at < total_len)).astype(jnp.float32)


def tables(tokens, lengths, later_than):
    table = jax.ShapeDtypeStruct((tokens, HEAD), jnp.float32)
    allowed = jax.ShapeDtypeStruct((tokens, tokens), jnp.float32)
    return call(
        tables_kernel,
        (table, table, allowed, table),
        in_specs=[SCALARS, pl.BlockSpec(memory_space=pl.ANY)],
        out_specs=[WHOLE] * 4,
    )(lengths, later_than)


def scale_kernel(own_ref, other_ref, out_ref):
    squares = jnp.sum(own_ref[...] + other_ref[...], axis=1, keepdims=True)
    out_ref[...] = jnp.broadcast_to(lax.rsqrt(squares / D + EPSILON), out_ref.shape)


def inv_rms(own, other):
    return call(
        scale_kernel,
        jax.ShapeDtypeStruct(own.shape, jnp.float32),
        in_specs=[WHOLE] * 2,
        out_specs=WHOLE,
    )(own, other)


def summed(refs, index, scale_ref):
    total = refs[0][index]
    for ref in refs[1:]:
        total += ref[index].astype(jnp.float32)
    return total * scale_ref[...]


def turned(block, cosine_ref, sine_ref):
    half = HEAD // 2
    other = jnp.concatenate([block[:, half:], block[:, :half]], axis=1)
    return block * cosine_ref[...] + other * sine_ref[...]


def kv_kernel(own, r0, r1, r2, scale_ref, cosine_ref, sine_ref, out_ref):
    block = summed((own, r0, r1, r2), 0, scale_ref)
    spun = turned(block, cosine_ref, sine_ref)
    out_ref[...] = jnp.where(lax.axis_index("tensor") == 0, spun, block).astype(jnp.bfloat16)


def heads_kernel(first, n_parts, *refs):
    parts, refs = refs[:n_parts], refs[n_parts:]
    scale_ref, cosine_ref, sine_ref, allowed_ref, keep_ref, mine_ref, other_ref, *rest = refs
    earlier_refs, out_ref, scratch = rest[:-1], rest[-1], None
    if len(rest) > 1:
        earlier_ref, out_ref, scratch, sems = rest
        earlier_refs = [earlier_ref]
    copies = []

    def put(source, at):
        copies.append(pltpu.make_async_copy(source, out_ref.at[:, pl.ds(at, source.shape[1])], sems.at[len(copies)]))
        copies[-1].start()

    is_key = lax.axis_index("tensor") == 0
    mine, other = mine_ref[...], other_ref[...]
    keys = jnp.where(is_key, mine, other)
    values = jnp.where(is_key, other, mine)
    before = 0
    for earlier_ref in earlier_refs:
        put(earlier_ref, before)
        before += earlier_ref.shape[1]
    tokens = mine.shape[0]
    count = parts[0].shape[0] - first
    query = [turned(summed(parts, first + i, scale_ref), cosine_ref, sine_ref).astype(jnp.bfloat16) for i in range(count)]
    scores = lax.dot_general(
        jnp.concatenate(query, axis=0), keys, (((1,), (1,)), ((), ())), preferred_element_type=jnp.float32
    ) * HEAD ** (-0.5)
    allowed = jnp.concatenate([allowed_ref[...] > 0.0] * count, axis=0)
    scores = jnp.where(allowed, scores, -1e30)
    expo = jnp.exp(scores - jnp.max(scores, axis=-1, keepdims=True))
    attn = (expo * (1.0 / jnp.sum(expo, axis=-1, keepdims=True))).astype(jnp.bfloat16)
    mixed = jnp.dot(attn, values, preferred_element_type=jnp.float32)
    for i in range(count):
        done = (mixed[i * tokens:(i + 1) * tokens] * keep_ref[...]).astype(jnp.bfloat16)
        if scratch is None:
            out_ref[:, i * HEAD:(i + 1) * HEAD] = done
        else:
            scratch[i] = done
            put(scratch.at[i], before + i * HEAD)
    for copy in copies:
        copy.wait()


def heads(parts, first, scale, tabled, mine, other, *earlier):
    args = [*parts, scale, *tabled, mine, other, *earlier]
    tokens = mine.shape[0]
    count = parts[0].shape[0] - first
    out_shape = jax.ShapeDtypeStruct((tokens, count * HEAD + sum(e.shape[1] for e in earlier)), jnp.bfloat16)
    scratch = [pltpu.VMEM((count, tokens, HEAD), jnp.bfloat16), pltpu.SemaphoreType.DMA((count + len(earlier),))]
    return call(
        functools.partial(heads_kernel, first, len(parts)),
        out_shape,
        result=bool(earlier),
        in_specs=[WHOLE] * len(args),
        out_specs=pl.BlockSpec(memory_space=pltpu.HBM) if earlier else WHOLE,
        scratch_shapes=scratch if earlier else [],
    )(*args)


def staged(hidden_in, norm_gain, projection, lengths):
    groups = lax.axis_size("groups")
    dp = lax.axis_size("dp")
    tensor = lax.axis_size("tensor")
    depth = dp // 2
    tokens = hidden_in.shape[0]
    part = projection.shape[1] // groups
    heads_local = QHEADS // tensor

    ring = [(i, (i + 2) % dp) for i in range(dp)]
    over_x = swap(dp)
    over_y = swap(groups)
    over_core = swap(tensor)
    across = [(g * dp + i, (g ^ 1) * dp + (i ^ 1)) for g in range(groups) for i in range(dp)]

    def to_core(a):
        return lax.ppermute(a, "tensor", over_core)

    def on_ring(a):
        return lax.ppermute(a, "dp", ring)

    def back(a):
        return lax.ppermute(a, "dp", [(j, i) for i, j in ring])

    def to_far(a):
        return lax.ppermute(a, ("groups", "dp"), across)

    def to_x(a):
        return lax.ppermute(a, "dp", over_x)

    def to_y(a):
        return lax.ppermute(a, "groups", over_y)

    def to_plane(three):
        return [to_far(three[0]), to_x(three[1]), to_y(three[2])]

    last = []

    def after(*values):
        held = lax.optimization_barrier(tuple(values) + tuple(last))[:len(values)]
        last[:] = held[:1]
        return held[0] if len(values) == 1 else held

    blocks = [[(QHEADS + c) * HEAD for c in range(tensor)]]
    blocks += [[(c * heads_local + i) * HEAD for c in range(tensor)] for i in range(heads_local)]
    columns = [blocks[0] + blocks[1], blocks[2] + blocks[3]]
    a0, = select(projection, part, columns[:1])
    a0 = after(a0)
    a1 = on_ring(a0)
    far, near_x, near_y, own, squares = after(*gate(after(hidden_in), norm_gain, part, depth))
    near_x = to_x(near_x)
    near_y = to_y(near_y)
    b0, = select(after(projection), part, columns[1:])
    b0, a0 = after(b0, a0)
    a3 = back(a0)
    other_squares = to_core(squares)
    tabled = after(*tables(tokens, lengths, after(squares)))
    scale = after(inv_rms(squares, after(other_squares)))

    a1, b0, far = after(a1, b0, far)
    b1 = on_ring(b0)
    far = to_far(far)
    a3, a1 = after(a3, a1)
    a2 = on_ring(a1)
    near_y = after(near_y)
    near_x = after(near_x)
    b1 = after(b1)
    b2 = on_ring(b1)
    early = (near_x, near_y, own)
    front = after(matmul(early, (a0, a1, a3), (0, 1, 3)))
    a2 = after(a2)
    set_a = (a0, a1, a2, a3)

    *theirs, mine = after(*matmul(early, (a2,), (2,), (front,), sent=2))
    swapped = [to_core(t) for t in theirs]
    far, b0 = after(far, b0)
    b3 = back(b0)
    sums_x, sums_y, sums = after(*join(mine, after(*swapped), (jnp.bfloat16, jnp.bfloat16, jnp.float32)))
    sums_x = to_x(sums_x)
    sums_y = to_y(sums_y)
    acts = (far, own, near_x, near_y)
    *theirs, mine = after(*matmul((far,), set_a, (0, 1, 2, 3), sent=1))
    swapped = [to_core(t) for t in theirs]
    b2 = after(b2)
    swapped = [after(t) for t in swapped]
    sums_far = after(*join(mine, swapped, (jnp.bfloat16,)))
    sums_far = to_far(sums_far)
    sums_y = after(sums_y)
    sums_x = after(sums_x)
    front = after(matmul(acts, (b0, b1, b2), (0, 1, 2)))

    b3 = after(b3)
    parts_a = after(sums, sums_far, sums_x, sums_y)
    *theirs, mine = after(*matmul(acts, (b3,), (3,), (front,), sent=2))
    swapped = [to_core(t) for t in theirs]
    kv = after(call(
        kv_kernel,
        jax.ShapeDtypeStruct((tokens, HEAD), jnp.bfloat16),
        in_specs=[WHOLE] * 7,
        out_specs=WHOLE,
    )(*parts_a, scale, *tabled[:2]))
    vk = to_core(kv)
    sums_far, sums = after(*join(mine, (after(swapped[0]),), (jnp.bfloat16, jnp.float32)))
    sums_far = to_far(sums_far)
    sums_x, sums_y = after(*join(mine, (after(swapped[1]),), (jnp.bfloat16, jnp.bfloat16), first=2))
    sums_x = to_x(sums_x)
    sums_y = to_y(sums_y)
    vk = after(vk)
    one = after(heads(parts_a, 1, scale, tabled, kv, vk))
    sums_far = after(sums_far)
    sums_x, sums_y = after(sums_x, sums_y)
    return heads((sums, sums_far, sums_x, sums_y), 0, scale, tabled, kv, vk, one)


def local(hidden_in, norm_gain, projection, lengths):
    part = projection.shape[1] // lax.axis_size("groups")
    if lax.axis_size("dp") == 8 and part % HEAD == 0:
        return staged(hidden_in, norm_gain, projection, lengths)
    return general(hidden_in, norm_gain, projection, lengths)


def solution(mesh):
    in_specs = (
        P(("groups", "dp"), "tensor"),
        P("tensor"),
        P("tensor", "dp", None),
        P(("groups", "dp"), None),
    )
    out_specs = P(("groups", "dp"), "tensor")
    return jax.shard_map(local, mesh=mesh, in_specs=in_specs, out_specs=out_specs, check_vma=False)
```

```python
import functools
import math

import jax
import jax.numpy as jnp
from jax import lax
from jax.experimental import pallas as pl
from jax.experimental.pallas import tpu as pltpu
from jax.sharding import PartitionSpec as P

D = 12288
HEAD = 128
QHEADS = 6
ROPE_BASE = 1000000.0
EPSILON = 1e-05


def angles(seq_len):
    half = HEAD // 2
    positions = jnp.arange(seq_len, dtype=jnp.int32)
    freq = ROPE_BASE ** (-(jnp.arange(half, dtype=jnp.float32) * 2.0 / HEAD))
    angle = positions.astype(jnp.float32)[:, None] * freq[None, :]
    return jnp.cos(angle), jnp.sin(angle)


def rotate(block, cosine, sine):
    half = HEAD // 2
    first = block[:, :half]
    second = block[:, half:]
    return jnp.concatenate([first * cosine - second * sine, second * cosine + first * sine], axis=-1)


def attend_head(query, keys, values, allowed, keep):
    scores = lax.dot_general(
        query, keys, (((1,), (1,)), ((), ())), preferred_element_type=jnp.float32
    ) * HEAD ** (-0.5)
    scores = jnp.where(allowed, scores, -1e30)
    largest = jnp.max(scores, axis=-1, keepdims=True)
    expo = jnp.exp(scores - largest)
    attn = (expo / jnp.sum(expo, axis=-1, keepdims=True)).astype(jnp.bfloat16)
    mixed = jnp.dot(attn, values, preferred_element_type=jnp.float32)
    return (mixed * keep).astype(jnp.bfloat16)


def swap(size):
    return [(i, i ^ 1) for i in range(size)]


def general(hidden_in, norm_gain, projection, lengths):
    groups = lax.axis_size("groups")
    dp = lax.axis_size("dp")
    tensor = lax.axis_size("tensor")
    y = lax.axis_index("groups")
    place = lax.axis_index("dp")
    core = lax.axis_index("tensor")
    x = place % 2
    z = place // 2
    depth = dp // 2
    tokens = hidden_in.shape[0]
    rows = projection.shape[1]
    part = rows // groups
    heads_local = QHEADS // tensor

    ring = [(i, (i + 2) % dp) for i in range(dp)]
    over_x = swap(dp)
    over_y = swap(groups)
    over_core = swap(tensor)
    across = [(g * dp + i, (g ^ 1) * dp + (i ^ 1)) for g in range(groups) for i in range(dp)]

    mine = lax.dynamic_slice_in_dim(projection[0], y * part, part, 0)

    def column(owner, index):
        start = (QHEADS + owner) * HEAD if index == 0 else (owner * heads_local + index - 1) * HEAD
        return lax.dynamic_slice_in_dim(mine, start, HEAD, 1)

    n_cols = heads_local + 1
    theirs = jnp.concatenate([column(1 - core, i) for i in range(n_cols)], axis=1)
    other = lax.ppermute(theirs, "tensor", over_core)
    weights = []
    for i in range(n_cols):
        slot = jnp.concatenate([column(core, i), other[:, i * HEAD:(i + 1) * HEAD]], axis=0)
        weights.append([slot])
    for _ in range(depth - 1):
        for i in range(n_cols):
            weights[i].append(lax.ppermute(weights[i][-1], "dp", ring))

    wide32 = hidden_in.astype(jnp.float32)
    gated = (wide32 * norm_gain.astype(jnp.float32)[None, :]).astype(jnp.bfloat16)
    local_sq = jnp.sum(wide32 * wide32, axis=1)
    total_sq = local_sq + lax.ppermute(local_sq, "tensor", over_core)
    inv_rms = lax.rsqrt(total_sq / D + EPSILON)[:, None]

    def piece(dx, dy):
        slabs = []
        for k in range(depth):
            shard = ((z - k + depth) % depth) * 2 + (x ^ dx)
            slabs.append(lax.dynamic_slice_in_dim(gated, shard * rows + (y ^ dy) * part, part, 1))
        return jnp.stack(slabs)

    sent = [piece(1, 1), piece(1, 0), piece(0, 1)]
    held = [
        lax.ppermute(sent[0], ("groups", "dp"), across),
        lax.ppermute(sent[1], "dp", over_x),
        lax.ppermute(sent[2], "groups", over_y),
        piece(0, 0),
    ]
    acts = []
    for h in held:
        acts.append(jnp.concatenate([h, lax.ppermute(h, "tensor", over_core)], axis=2))
    acts = jnp.concatenate(acts, axis=1)

    cosine, sine = angles(tokens)
    positions = jnp.arange(tokens, dtype=jnp.int32)
    prompt = lengths[0, 0]
    total_len = prompt + lengths[0, 1]
    allowed = (positions[None, :] <= positions[:, None]) & (positions[None, :] < total_len)
    keep = ((positions >= prompt - 1) & (positions < total_len - 1)).astype(jnp.float32)[:, None]

    outs = []
    keys = values = None
    for i in range(n_cols):
        partial = sum(
            jnp.dot(acts[k], weights[i][k], preferred_element_type=jnp.float32) for k in range(depth)
        )
        blocks = partial.reshape(4, tokens, HEAD)
        low = blocks[:3].astype(jnp.bfloat16)
        summed = blocks[3]
        summed = summed + lax.ppermute(low[0], ("groups", "dp"), across).astype(jnp.float32)
        summed = summed + lax.ppermute(low[1], "dp", over_x).astype(jnp.float32)
        summed = summed + lax.ppermute(low[2], "groups", over_y).astype(jnp.float32)
        scaled = summed * inv_rms
        if i == 0:
            turned = rotate(scaled, cosine, sine)
            kv = jnp.where(core == 0, turned, scaled).astype(jnp.bfloat16)
            vk = lax.ppermute(kv, "tensor", over_core)
            keys = jnp.where(core == 0, kv, vk)
            values = jnp.where(core == 0, vk, kv)
        else:
            query = rotate(scaled, cosine, sine).astype(jnp.bfloat16)
            outs.append(attend_head(query, keys, values, allowed, keep))
    return jnp.concatenate(outs, axis=1)


VMEM = pltpu.VMEM
PLANE = ((1, 1), (1, 0), (0, 1), (0, 0))
WHOLE = pl.BlockSpec(memory_space=VMEM)
SCALARS = pl.BlockSpec(memory_space=pltpu.SMEM)


def call(kernel, out_shape, limit=12, result=False, **kwargs):
    if not result:
        out_shape = jax.tree.map(lambda s: pltpu.VMEM(s.shape, s.dtype), out_shape)
    return pl.pallas_call(
        kernel,
        out_shape=out_shape,
        compiler_params=pltpu.CompilerParams(vmem_limit_bytes=limit * 2**20),
        cost_estimate=pl.CostEstimate(flops=1, bytes_accessed=1, transcendentals=0),
        **kwargs,
    )


def split_kernel(columns, rows_ref, *out_refs):
    for starts, out_ref in zip(columns, out_refs):
        for i, start in enumerate(starts):
            out_ref[:, i * HEAD:(i + 1) * HEAD] = rows_ref[:, start:start + HEAD]


def split(rows, columns):
    return call(
        functools.partial(split_kernel, columns),
        tuple(jax.ShapeDtypeStruct((rows.shape[0], len(c) * HEAD), rows.dtype) for c in columns),
        in_specs=[WHOLE],
        out_specs=[WHOLE] * len(columns),
    )(rows)


def gate_kernel(part, depth, hidden_ref, gain_ref, *refs):
    piece_refs, (sq_ref, slab_ref, flat_ref, row_ref, sems) = refs[:4], refs[4:]
    place = lax.axis_index("dp")
    x, z, y = place % 2, place // 2, lax.axis_index("groups")
    wide = 4 * part
    columns = [pl.ds(pl.multiple_of(lax.rem(z - k + depth, depth) * wide, HEAD), wide) for k in range(depth)]
    copies = [pltpu.make_async_copy(hidden_ref.at[:, c], slab_ref.at[k], sems.at[k]) for k, c in enumerate(columns)]
    gain_copy = pltpu.make_async_copy(gain_ref, flat_ref, sems.at[depth])
    gain_copy.start()
    for copy in copies:
        copy.start()
    gain_copy.wait()
    row_ref[0, :] = flat_ref[...].astype(jnp.float32)
    tokens = hidden_ref.shape[0]
    height = 64
    for k, copy in enumerate(copies):
        copy.wait()
        for top in range(0, tokens, height):
            rows = slice(top, top + height)
            total = jnp.zeros((height, HEAD), jnp.float32)
            for piece_ref, (dx, dy) in zip(piece_refs, PLANE):
                start = ((x ^ dx) * 2 + (y ^ dy)) * part
                whole = slab_ref[k, rows, pl.ds(pl.multiple_of(start, HEAD), part)].astype(jnp.float32)
                at = lax.rem(z - k + depth, depth) * wide + start
                gain = row_ref[:, pl.ds(pl.multiple_of(at, HEAD), part)]
                piece_ref[k, rows] = (whole * gain).astype(jnp.bfloat16)
                square = whole * whole
                for j in range(0, part, HEAD):
                    total += square[:, j:j + HEAD]
            sq_ref[rows] = total if k == 0 else sq_ref[rows] + total


def gate(hidden_in, norm_gain, part, depth):
    tokens = hidden_in.shape[0]
    piece = jax.ShapeDtypeStruct((depth, tokens, part), jnp.bfloat16)
    return call(
        functools.partial(gate_kernel, part, depth),
        (piece,) * 4 + (jax.ShapeDtypeStruct((tokens, HEAD), jnp.float32),),
        in_specs=[pl.BlockSpec(memory_space=pltpu.HBM)] * 2,
        out_specs=[WHOLE] * 5,
        scratch_shapes=[
            pltpu.VMEM((depth, tokens, 4 * part), jnp.bfloat16),
            pltpu.VMEM(norm_gain.shape, norm_gain.dtype),
            pltpu.VMEM((1, norm_gain.shape[0]), jnp.float32),
            pltpu.SemaphoreType.DMA((depth + 1,)),
        ],
    )(*(pltpu.with_memory_space_constraint(a, pltpu.HBM) for a in (hidden_in, norm_gain)))


def matmul_kernel(firsts, n_acts, n_more, sent, paired, *refs):
    is_first = lax.axis_index("tensor") == 0
    acts, refs = refs[:n_acts], refs[n_acts:]
    slots, refs = refs[:len(firsts)], refs[len(firsts):]
    more, out_refs = refs[:n_more], refs[n_more:]
    more = [(ref, i) for ref in more for i in range(ref.shape[0])]
    right = [slot[...] for slot in slots]
    wide = 2 * HEAD
    for p in range(n_acts):
        total = jnp.dot(acts[p][firsts[0]], right[0], preferred_element_type=jnp.float32)
        for k in range(1, len(firsts)):
            total += jnp.dot(acts[p][firsts[k]], right[k], preferred_element_type=jnp.float32)
        if more:
            ref, i = more[p]
            total += ref[i]
        if not sent:
            out_refs[0][p] = total
            continue
        theirs_refs, mine_ref = out_refs[:-1], out_refs[-1]
        n_blocks = mine_ref.shape[1]
        per = n_acts * n_blocks // sent
        for g in range(n_blocks):
            at, apart = (g * wide, HEAD) if paired else (g * HEAD, n_blocks * HEAD)
            low = total[:, at:at + HEAD]
            high = total[:, at + apart:at + apart + HEAD]
            spot = p * n_blocks + g
            theirs_refs[spot // per][spot % per] = jnp.where(is_first, high, low).astype(jnp.bfloat16)
            mine_ref[p, g] = jnp.where(is_first, low, high)


def matmul(acts, slots, firsts, so_far=(), sent=0, paired=True):
    n_blocks = slots[0].shape[1] // (2 * HEAD)
    tokens = acts[0].shape[1]
    args = [*acts, *slots, *so_far]
    if sent:
        out_shape = (jax.ShapeDtypeStruct((len(acts) * n_blocks // sent, tokens, HEAD), jnp.bfloat16),) * sent
        out_shape += (jax.ShapeDtypeStruct((len(acts), n_blocks, tokens, HEAD), jnp.float32),)
    else:
        out_shape = (jax.ShapeDtypeStruct((len(acts), tokens, n_blocks * 2 * HEAD), jnp.float32),)
    outs = call(
        functools.partial(matmul_kernel, firsts, len(acts), len(so_far), sent, paired),
        out_shape,
        in_specs=[WHOLE] * len(args),
        out_specs=[WHOLE] * len(out_shape),
    )(*args)
    return outs if sent else outs[0]


def join_kernel(n_came, first, mine_ref, *refs):
    came_refs, out_refs = refs[:n_came], refs[n_came:]
    n_blocks = mine_ref.shape[1]
    per = len(out_refs) * n_blocks // n_came
    for p, out_ref in enumerate(out_refs):
        for g in range(n_blocks):
            spot = p * n_blocks + g
            came = came_refs[spot // per][spot % per].astype(jnp.float32)
            out_ref[g] = (mine_ref[first + p, g] + came).astype(out_ref.dtype)


def join(mine, came, types, first=0):
    return call(
        functools.partial(join_kernel, len(came), first),
        tuple(jax.ShapeDtypeStruct(mine.shape[1:], t) for t in types),
        in_specs=[WHOLE] * (1 + len(came)),
        out_specs=[WHOLE] * len(types),
    )(mine, *came)


def tables_kernel(lengths_ref, _, cosine_ref, sine_ref, allowed_ref, keep_ref):
    at = lax.broadcasted_iota(jnp.int32, cosine_ref.shape, 0)
    lane = lax.broadcasted_iota(jnp.int32, cosine_ref.shape, 1)
    pair = lax.rem(lane, HEAD // 2).astype(jnp.float32)
    angle = at.astype(jnp.float32) * jnp.exp(pair * (-2.0 * math.log(ROPE_BASE) / HEAD))
    cosine_ref[...] = jnp.cos(angle)
    sine_ref[...] = jnp.where(lane < HEAD // 2, -jnp.sin(angle), jnp.sin(angle))
    prompt = lengths_ref[0, 0]
    total_len = prompt + lengths_ref[0, 1]
    keep_ref[...] = ((at >= prompt - 1) & (at < total_len - 1)).astype(jnp.float32)
    query_at = lax.broadcasted_iota(jnp.int32, allowed_ref.shape, 0)
    key_at = lax.broadcasted_iota(jnp.int32, allowed_ref.shape, 1)
    allowed_ref[...] = ((key_at <= query_at) & (key_at < total_len)).astype(jnp.float32)


def tables(tokens, lengths, later_than):
    table = jax.ShapeDtypeStruct((tokens, HEAD), jnp.float32)
    allowed = jax.ShapeDtypeStruct((tokens, tokens), jnp.float32)
    return call(
        tables_kernel,
        (table, table, allowed, table),
        in_specs=[SCALARS, pl.BlockSpec(memory_space=pl.ANY)],
        out_specs=[WHOLE] * 4,
    )(lengths, later_than)


def scale_kernel(own_ref, other_ref, out_ref):
    squares = jnp.sum(own_ref[...] + other_ref[...], axis=1, keepdims=True)
    out_ref[...] = jnp.broadcast_to(lax.rsqrt(squares / D + EPSILON), out_ref.shape)


def inv_rms(own, other):
    return call(
        scale_kernel,
        jax.ShapeDtypeStruct(own.shape, jnp.float32),
        in_specs=[WHOLE] * 2,
        out_specs=WHOLE,
    )(own, other)


def summed(refs, index, scale_ref):
    total = refs[0][index]
    for ref in refs[1:]:
        total += ref[index].astype(jnp.float32)
    return total * scale_ref[...]


def turned(block, cosine_ref, sine_ref):
    half = HEAD // 2
    other = jnp.concatenate([block[:, half:], block[:, :half]], axis=1)
    return block * cosine_ref[...] + other * sine_ref[...]


def kv_kernel(own, r0, r1, r2, scale_ref, cosine_ref, sine_ref, out_ref):
    block = summed((own, r0, r1, r2), 0, scale_ref)
    spun = turned(block, cosine_ref, sine_ref)
    out_ref[...] = jnp.where(lax.axis_index("tensor") == 0, spun, block).astype(jnp.bfloat16)


def heads_kernel(first, n_parts, *refs):
    parts, refs = refs[:n_parts], refs[n_parts:]
    scale_ref, cosine_ref, sine_ref, allowed_ref, keep_ref, mine_ref, other_ref, *rest = refs
    earlier_refs, out_ref, scratch = rest[:-1], rest[-1], None
    if len(rest) > 1:
        earlier_ref, out_ref, scratch, sems = rest
        earlier_refs = [earlier_ref]
    copies = []

    def put(source, at):
        where = pl.ds(pl.multiple_of(at, HEAD), HEAD)
        copies.append(pltpu.make_async_copy(source, out_ref.at[:, where], sems.at[len(copies)]))
        copies[-1].start()

    is_key = lax.axis_index("tensor") == 0
    mine, other = mine_ref[...], other_ref[...]
    keys = jnp.where(is_key, mine, other)
    values = jnp.where(is_key, other, mine)
    count = parts[0].shape[0] - first
    before = jnp.where(is_key, HEAD, 0)
    for earlier_ref in earlier_refs:
        put(earlier_ref, jnp.where(is_key, 0, count * HEAD))
    tokens = mine.shape[0]
    query = [turned(summed(parts, first + i, scale_ref), cosine_ref, sine_ref).astype(jnp.bfloat16) for i in range(count)]
    scores = lax.dot_general(
        jnp.concatenate(query, axis=0), keys, (((1,), (1,)), ((), ())), preferred_element_type=jnp.float32
    ) * HEAD ** (-0.5)
    allowed = jnp.concatenate([allowed_ref[...] > 0.0] * count, axis=0)
    scores = jnp.where(allowed, scores, -1e30)
    expo = jnp.exp(scores - jnp.max(scores, axis=-1, keepdims=True))
    attn = (expo * (1.0 / jnp.sum(expo, axis=-1, keepdims=True))).astype(jnp.bfloat16)
    mixed = jnp.dot(attn, values, preferred_element_type=jnp.float32)
    for i in range(count):
        done = (mixed[i * tokens:(i + 1) * tokens] * keep_ref[...]).astype(jnp.bfloat16)
        if scratch is None:
            out_ref[:, i * HEAD:(i + 1) * HEAD] = done
        else:
            scratch[i] = done
            put(scratch.at[i], before + i * HEAD)
    for copy in copies:
        copy.wait()


def heads(parts, first, scale, tabled, mine, other, *earlier):
    args = [*parts, scale, *tabled, mine, other, *earlier]
    tokens = mine.shape[0]
    count = parts[0].shape[0] - first
    out_shape = jax.ShapeDtypeStruct((tokens, count * HEAD + sum(e.shape[1] for e in earlier)), jnp.bfloat16)
    scratch = [pltpu.VMEM((count, tokens, HEAD), jnp.bfloat16), pltpu.SemaphoreType.DMA((count + len(earlier),))]
    return call(
        functools.partial(heads_kernel, first, len(parts)),
        out_shape,
        result=bool(earlier),
        in_specs=[WHOLE] * len(args),
        out_specs=pl.BlockSpec(memory_space=pltpu.HBM) if earlier else WHOLE,
        scratch_shapes=scratch if earlier else [],
    )(*args)


def staged(hidden_in, norm_gain, projection, lengths):
    groups = lax.axis_size("groups")
    dp = lax.axis_size("dp")
    tensor = lax.axis_size("tensor")
    depth = dp // 2
    tokens = hidden_in.shape[0]
    part = projection.shape[1] // groups
    heads_local = QHEADS // tensor

    ring = [(i, (i + 2) % dp) for i in range(dp)]
    over_x = swap(dp)
    over_y = swap(groups)
    over_core = swap(tensor)
    across = [(g * dp + i, (g ^ 1) * dp + (i ^ 1)) for g in range(groups) for i in range(dp)]

    def to_core(a):
        return lax.ppermute(a, "tensor", over_core)

    def on_ring(a):
        return lax.ppermute(a, "dp", ring)

    def back(a):
        return lax.ppermute(a, "dp", [(j, i) for i, j in ring])

    def to_far(a):
        return lax.ppermute(a, ("groups", "dp"), across)

    def to_x(a):
        return lax.ppermute(a, "dp", over_x)

    def to_y(a):
        return lax.ppermute(a, "groups", over_y)

    def to_plane(three):
        return [to_far(three[0]), to_x(three[1]), to_y(three[2])]

    last = []

    def after(*values):
        held = lax.optimization_barrier(tuple(values) + tuple(last))[:len(values)]
        last[:] = held[:1]
        return held[0] if len(values) == 1 else held

    columns_a = [(QHEADS + c) * HEAD for c in range(tensor)] + [0, (QHEADS - 1) * HEAD]
    columns_b = [i * HEAD for i in range(1, QHEADS - 1)]
    start = (0, lax.axis_index("groups") * part, 0)
    rows = lax.dynamic_slice(projection, start, (1, part, projection.shape[2]))[0]
    b0, a0 = split(rows, (columns_b, columns_a))
    b1 = on_ring(b0)
    far, near_x, near_y, own, squares = after(*gate(hidden_in, norm_gain, part, depth))
    near_x = to_x(near_x)
    near_y = to_y(near_y)
    a0 = after(a0)
    a1 = on_ring(a0)
    other_squares = to_core(squares)
    tabled = after(*tables(tokens, lengths, after(squares)))
    scale = after(inv_rms(squares, after(other_squares)))

    b1, a0, far = after(b1, a0, far)
    a3 = back(a0)
    far = to_far(far)
    a1 = after(a1)
    a2 = on_ring(a1)
    b0 = after(b0)
    near_y = after(near_y)
    near_x = after(near_x)
    a3, b1 = after(a3, b1)
    b2 = on_ring(b1)
    early = (near_x, near_y, own)
    front = after(matmul(early, (a0, a1, a3), (0, 1, 3)))
    a2 = after(a2)
    set_a = (a0, a1, a2, a3)

    *theirs, mine = after(*matmul(early, (a2,), (2,), (front,), sent=2))
    swapped = [to_core(t) for t in theirs]
    far, b0 = after(far, b0)
    b3 = back(b0)
    sums_x, sums_y, sums = after(*join(mine, after(*swapped), (jnp.bfloat16, jnp.bfloat16, jnp.float32)))
    sums_x = to_x(sums_x)
    sums_y = to_y(sums_y)
    acts = (far, own, near_x, near_y)
    *theirs, mine = after(*matmul((far,), set_a, (0, 1, 2, 3), sent=1))
    swapped = [to_core(t) for t in theirs]
    b2 = after(b2)
    swapped = [after(t) for t in swapped]
    sums_far = after(*join(mine, swapped, (jnp.bfloat16,)))
    sums_far = to_far(sums_far)
    sums_y = after(sums_y)
    sums_x = after(sums_x)
    front = after(matmul(acts, (b0, b1, b2), (0, 1, 2)))

    b3 = after(b3)
    parts_a = after(sums, sums_far, sums_x, sums_y)
    *theirs, mine = after(*matmul(acts, (b3,), (3,), (front,), sent=2, paired=False))
    swapped = [to_core(t) for t in theirs]
    kv = after(call(
        kv_kernel,
        jax.ShapeDtypeStruct((tokens, HEAD), jnp.bfloat16),
        in_specs=[WHOLE] * 7,
        out_specs=WHOLE,
    )(*parts_a, scale, *tabled[:2]))
    vk = to_core(kv)
    sums_far, sums = after(*join(mine, (after(swapped[0]),), (jnp.bfloat16, jnp.float32)))
    sums_far = to_far(sums_far)
    sums_x, sums_y = after(*join(mine, (after(swapped[1]),), (jnp.bfloat16, jnp.bfloat16), first=2))
    sums_x = to_x(sums_x)
    sums_y = to_y(sums_y)
    vk = after(vk)
    one = after(heads(parts_a, 1, scale, tabled, kv, vk))
    sums_far = after(sums_far)
    sums_x, sums_y = after(sums_x, sums_y)
    return heads((sums, sums_far, sums_x, sums_y), 0, scale, tabled, kv, vk, one)


def local(hidden_in, norm_gain, projection, lengths):
    part = projection.shape[1] // lax.axis_size("groups")
    if lax.axis_size("dp") == 8 and part % HEAD == 0:
        return staged(hidden_in, norm_gain, projection, lengths)
    return general(hidden_in, norm_gain, projection, lengths)


def solution(mesh):
    in_specs = (
        P(("groups", "dp"), "tensor"),
        P("tensor"),
        P("tensor", "dp", None),
        P(("groups", "dp"), None),
    )
    out_specs = P(("groups", "dp"), "tensor")
    return jax.shard_map(local, mesh=mesh, in_specs=in_specs, out_specs=out_specs, check_vma=False)
```

```python
import functools
import math

import jax
import jax.numpy as jnp
from jax import lax
from jax.experimental import pallas as pl
from jax.experimental.pallas import tpu as pltpu
from jax.sharding import PartitionSpec as P

D = 12288
HEAD = 128
QHEADS = 6
ROPE_BASE = 1000000.0
EPSILON = 1e-05


def angles(seq_len):
    half = HEAD // 2
    positions = jnp.arange(seq_len, dtype=jnp.int32)
    freq = ROPE_BASE ** (-(jnp.arange(half, dtype=jnp.float32) * 2.0 / HEAD))
    angle = positions.astype(jnp.float32)[:, None] * freq[None, :]
    return jnp.cos(angle), jnp.sin(angle)


def rotate(block, cosine, sine):
    half = HEAD // 2
    first = block[:, :half]
    second = block[:, half:]
    return jnp.concatenate([first * cosine - second * sine, second * cosine + first * sine], axis=-1)


def attend_head(query, keys, values, allowed, keep):
    scores = lax.dot_general(
        query, keys, (((1,), (1,)), ((), ())), preferred_element_type=jnp.float32
    ) * HEAD ** (-0.5)
    scores = jnp.where(allowed, scores, -1e30)
    largest = jnp.max(scores, axis=-1, keepdims=True)
    expo = jnp.exp(scores - largest)
    attn = (expo / jnp.sum(expo, axis=-1, keepdims=True)).astype(jnp.bfloat16)
    mixed = jnp.dot(attn, values, preferred_element_type=jnp.float32)
    return (mixed * keep).astype(jnp.bfloat16)


def swap(size):
    return [(i, i ^ 1) for i in range(size)]


def general(hidden_in, norm_gain, projection, lengths):
    groups = lax.axis_size("groups")
    dp = lax.axis_size("dp")
    tensor = lax.axis_size("tensor")
    y = lax.axis_index("groups")
    place = lax.axis_index("dp")
    core = lax.axis_index("tensor")
    x = place % 2
    z = place // 2
    depth = dp // 2
    tokens = hidden_in.shape[0]
    rows = projection.shape[1]
    part = rows // groups
    heads_local = QHEADS // tensor

    ring = [(i, (i + 2) % dp) for i in range(dp)]
    over_x = swap(dp)
    over_y = swap(groups)
    over_core = swap(tensor)
    across = [(g * dp + i, (g ^ 1) * dp + (i ^ 1)) for g in range(groups) for i in range(dp)]

    mine = lax.dynamic_slice_in_dim(projection[0], y * part, part, 0)

    def column(owner, index):
        start = (QHEADS + owner) * HEAD if index == 0 else (owner * heads_local + index - 1) * HEAD
        return lax.dynamic_slice_in_dim(mine, start, HEAD, 1)

    n_cols = heads_local + 1
    theirs = jnp.concatenate([column(1 - core, i) for i in range(n_cols)], axis=1)
    other = lax.ppermute(theirs, "tensor", over_core)
    weights = []
    for i in range(n_cols):
        slot = jnp.concatenate([column(core, i), other[:, i * HEAD:(i + 1) * HEAD]], axis=0)
        weights.append([slot])
    for _ in range(depth - 1):
        for i in range(n_cols):
            weights[i].append(lax.ppermute(weights[i][-1], "dp", ring))

    wide32 = hidden_in.astype(jnp.float32)
    gated = (wide32 * norm_gain.astype(jnp.float32)[None, :]).astype(jnp.bfloat16)
    local_sq = jnp.sum(wide32 * wide32, axis=1)
    total_sq = local_sq + lax.ppermute(local_sq, "tensor", over_core)
    inv_rms = lax.rsqrt(total_sq / D + EPSILON)[:, None]

    def piece(dx, dy):
        slabs = []
        for k in range(depth):
            shard = ((z - k + depth) % depth) * 2 + (x ^ dx)
            slabs.append(lax.dynamic_slice_in_dim(gated, shard * rows + (y ^ dy) * part, part, 1))
        return jnp.stack(slabs)

    sent = [piece(1, 1), piece(1, 0), piece(0, 1)]
    held = [
        lax.ppermute(sent[0], ("groups", "dp"), across),
        lax.ppermute(sent[1], "dp", over_x),
        lax.ppermute(sent[2], "groups", over_y),
        piece(0, 0),
    ]
    acts = []
    for h in held:
        acts.append(jnp.concatenate([h, lax.ppermute(h, "tensor", over_core)], axis=2))
    acts = jnp.concatenate(acts, axis=1)

    cosine, sine = angles(tokens)
    positions = jnp.arange(tokens, dtype=jnp.int32)
    prompt = lengths[0, 0]
    total_len = prompt + lengths[0, 1]
    allowed = (positions[None, :] <= positions[:, None]) & (positions[None, :] < total_len)
    keep = ((positions >= prompt - 1) & (positions < total_len - 1)).astype(jnp.float32)[:, None]

    outs = []
    keys = values = None
    for i in range(n_cols):
        partial = sum(
            jnp.dot(acts[k], weights[i][k], preferred_element_type=jnp.float32) for k in range(depth)
        )
        blocks = partial.reshape(4, tokens, HEAD)
        low = blocks[:3].astype(jnp.bfloat16)
        summed = blocks[3]
        summed = summed + lax.ppermute(low[0], ("groups", "dp"), across).astype(jnp.float32)
        summed = summed + lax.ppermute(low[1], "dp", over_x).astype(jnp.float32)
        summed = summed + lax.ppermute(low[2], "groups", over_y).astype(jnp.float32)
        scaled = summed * inv_rms
        if i == 0:
            turned = rotate(scaled, cosine, sine)
            kv = jnp.where(core == 0, turned, scaled).astype(jnp.bfloat16)
            vk = lax.ppermute(kv, "tensor", over_core)
            keys = jnp.where(core == 0, kv, vk)
            values = jnp.where(core == 0, vk, kv)
        else:
            query = rotate(scaled, cosine, sine).astype(jnp.bfloat16)
            outs.append(attend_head(query, keys, values, allowed, keep))
    return jnp.concatenate(outs, axis=1)


VMEM = pltpu.VMEM
PLANE = ((1, 1), (1, 0), (0, 1), (0, 0))
WHOLE = pl.BlockSpec(memory_space=VMEM)
SCALARS = pl.BlockSpec(memory_space=pltpu.SMEM)


def call(kernel, out_shape, limit=12, result=False, **kwargs):
    if not result:
        out_shape = jax.tree.map(lambda s: pltpu.VMEM(s.shape, s.dtype), out_shape)
    return pl.pallas_call(
        kernel,
        out_shape=out_shape,
        compiler_params=pltpu.CompilerParams(vmem_limit_bytes=limit * 2**20),
        cost_estimate=pl.CostEstimate(flops=1, bytes_accessed=1, transcendentals=0),
        **kwargs,
    )


def select_kernel(columns, part, rows_ref, *refs):
    out_refs, sems = refs[:len(columns)], refs[-1]
    rows = pl.ds(pl.multiple_of(lax.axis_index("groups") * part, HEAD), part)
    copies = []
    for starts, out_ref in zip(columns, out_refs):
        at = 0
        while at < len(starts):
            more = 1
            while at + more < len(starts) and starts[at + more] == starts[at] + more * HEAD:
                more += 1
            copies.append(pltpu.make_async_copy(
                rows_ref.at[0, rows, pl.ds(starts[at], more * HEAD)],
                out_ref.at[:, pl.ds(at * HEAD, more * HEAD)],
                sems.at[len(copies)],
            ))
            at += more
    for copy in copies:
        copy.start()
    for copy in copies:
        copy.wait()


def select(projection, part, columns):
    chunk = jax.ShapeDtypeStruct((part, len(columns[0]) * HEAD), projection.dtype)
    out_shape = (chunk,) * len(columns)
    return call(
        functools.partial(select_kernel, columns, part),
        out_shape,
        in_specs=[pl.BlockSpec(memory_space=pltpu.HBM)],
        out_specs=[WHOLE] * len(out_shape),
        scratch_shapes=[pltpu.SemaphoreType.DMA((len(columns) * len(columns[0]),))],
    )(projection)


def gate_kernel(part, depth, hidden_ref, gain_ref, *refs):
    piece_refs, (sq_ref, slab_ref, flat_ref, row_ref, sems) = refs[:4], refs[4:]
    place = lax.axis_index("dp")
    x, z, y = place % 2, place // 2, lax.axis_index("groups")
    wide = 4 * part
    columns = [pl.ds(pl.multiple_of(lax.rem(z - k + depth, depth) * wide, HEAD), wide) for k in range(depth)]
    copies = [pltpu.make_async_copy(hidden_ref.at[:, c], slab_ref.at[k], sems.at[k]) for k, c in enumerate(columns)]
    gain_copy = pltpu.make_async_copy(gain_ref, flat_ref, sems.at[depth])
    gain_copy.start()
    for copy in copies:
        copy.start()
    gain_copy.wait()
    row_ref[0, :] = flat_ref[...].astype(jnp.float32)
    tokens = hidden_ref.shape[0]
    height = 64
    for k, copy in enumerate(copies):
        copy.wait()
        for top in range(0, tokens, height):
            rows = slice(top, top + height)
            total = jnp.zeros((height, HEAD), jnp.float32)
            for piece_ref, (dx, dy) in zip(piece_refs, PLANE):
                start = ((x ^ dx) * 2 + (y ^ dy)) * part
                whole = slab_ref[k, rows, pl.ds(pl.multiple_of(start, HEAD), part)].astype(jnp.float32)
                at = lax.rem(z - k + depth, depth) * wide + start
                gain = row_ref[:, pl.ds(pl.multiple_of(at, HEAD), part)]
                piece_ref[k, rows] = (whole * gain).astype(jnp.bfloat16)
                square = whole * whole
                for j in range(0, part, HEAD):
                    total += square[:, j:j + HEAD]
            sq_ref[rows] = total if k == 0 else sq_ref[rows] + total


def gate(hidden_in, norm_gain, part, depth):
    tokens = hidden_in.shape[0]
    piece = jax.ShapeDtypeStruct((depth, tokens, part), jnp.bfloat16)
    return call(
        functools.partial(gate_kernel, part, depth),
        (piece,) * 4 + (jax.ShapeDtypeStruct((tokens, HEAD), jnp.float32),),
        in_specs=[pl.BlockSpec(memory_space=pltpu.HBM)] * 2,
        out_specs=[WHOLE] * 5,
        scratch_shapes=[
            pltpu.VMEM((depth, tokens, 4 * part), jnp.bfloat16),
            pltpu.VMEM(norm_gain.shape, norm_gain.dtype),
            pltpu.VMEM((1, norm_gain.shape[0]), jnp.float32),
            pltpu.SemaphoreType.DMA((depth + 1,)),
        ],
    )(*(pltpu.with_memory_space_constraint(a, pltpu.HBM) for a in (hidden_in, norm_gain)))


def matmul_kernel(firsts, n_acts, n_more, sent, paired, *refs):
    is_first = lax.axis_index("tensor") == 0
    acts, refs = refs[:n_acts], refs[n_acts:]
    slots, refs = refs[:len(firsts)], refs[len(firsts):]
    more, out_refs = refs[:n_more], refs[n_more:]
    more = [(ref, i) for ref in more for i in range(ref.shape[0])]
    right = [slot[...] for slot in slots]
    wide = 2 * HEAD
    for p in range(n_acts):
        total = jnp.dot(acts[p][firsts[0]], right[0], preferred_element_type=jnp.float32)
        for k in range(1, len(firsts)):
            total += jnp.dot(acts[p][firsts[k]], right[k], preferred_element_type=jnp.float32)
        if more:
            ref, i = more[p]
            total += ref[i]
        if not sent:
            out_refs[0][p] = total
            continue
        theirs_refs, mine_ref = out_refs[:-1], out_refs[-1]
        n_blocks = mine_ref.shape[1]
        per = n_acts * n_blocks // sent
        for g in range(n_blocks):
            at, apart = (g * wide, HEAD) if paired else (g * HEAD, n_blocks * HEAD)
            low = total[:, at:at + HEAD]
            high = total[:, at + apart:at + apart + HEAD]
            spot = p * n_blocks + g
            theirs_refs[spot // per][spot % per] = jnp.where(is_first, high, low).astype(jnp.bfloat16)
            mine_ref[p, g] = jnp.where(is_first, low, high)


def matmul(acts, slots, firsts, so_far=(), sent=0, paired=True):
    n_blocks = slots[0].shape[1] // (2 * HEAD)
    tokens = acts[0].shape[1]
    args = [*acts, *slots, *so_far]
    if sent:
        out_shape = (jax.ShapeDtypeStruct((len(acts) * n_blocks // sent, tokens, HEAD), jnp.bfloat16),) * sent
        out_shape += (jax.ShapeDtypeStruct((len(acts), n_blocks, tokens, HEAD), jnp.float32),)
    else:
        out_shape = (jax.ShapeDtypeStruct((len(acts), tokens, n_blocks * 2 * HEAD), jnp.float32),)
    outs = call(
        functools.partial(matmul_kernel, firsts, len(acts), len(so_far), sent, paired),
        out_shape,
        in_specs=[WHOLE] * len(args),
        out_specs=[WHOLE] * len(out_shape),
    )(*args)
    return outs if sent else outs[0]


def join_kernel(n_came, first, mine_ref, *refs):
    came_refs, out_refs = refs[:n_came], refs[n_came:]
    n_blocks = mine_ref.shape[1]
    per = len(out_refs) * n_blocks // n_came
    for p, out_ref in enumerate(out_refs):
        for g in range(n_blocks):
            spot = p * n_blocks + g
            came = came_refs[spot // per][spot % per].astype(jnp.float32)
            out_ref[g] = (mine_ref[first + p, g] + came).astype(out_ref.dtype)


def join(mine, came, types, first=0):
    return call(
        functools.partial(join_kernel, len(came), first),
        tuple(jax.ShapeDtypeStruct(mine.shape[1:], t) for t in types),
        in_specs=[WHOLE] * (1 + len(came)),
        out_specs=[WHOLE] * len(types),
    )(mine, *came)


def tables_kernel(lengths_ref, _, cosine_ref, sine_ref, allowed_ref, keep_ref):
    at = lax.broadcasted_iota(jnp.int32, cosine_ref.shape, 0)
    lane = lax.broadcasted_iota(jnp.int32, cosine_ref.shape, 1)
    pair = lax.rem(lane, HEAD // 2).astype(jnp.float32)
    angle = at.astype(jnp.float32) * jnp.exp(pair * (-2.0 * math.log(ROPE_BASE) / HEAD))
    cosine_ref[...] = jnp.cos(angle)
    sine_ref[...] = jnp.where(lane < HEAD // 2, -jnp.sin(angle), jnp.sin(angle))
    prompt = lengths_ref[0, 0]
    total_len = prompt + lengths_ref[0, 1]
    keep_ref[...] = ((at >= prompt - 1) & (at < total_len - 1)).astype(jnp.float32)
    query_at = lax.broadcasted_iota(jnp.int32, allowed_ref.shape, 0)
    key_at = lax.broadcasted_iota(jnp.int32, allowed_ref.shape, 1)
    allowed_ref[...] = ((key_at <= query_at) & (key_at < total_len)).astype(jnp.float32)


def tables(tokens, lengths, later_than):
    table = jax.ShapeDtypeStruct((tokens, HEAD), jnp.float32)
    allowed = jax.ShapeDtypeStruct((tokens, tokens), jnp.float32)
    return call(
        tables_kernel,
        (table, table, allowed, table),
        in_specs=[SCALARS, pl.BlockSpec(memory_space=pl.ANY)],
        out_specs=[WHOLE] * 4,
    )(lengths, later_than)


def scale_kernel(own_ref, other_ref, out_ref):
    squares = jnp.sum(own_ref[...] + other_ref[...], axis=1, keepdims=True)
    out_ref[...] = jnp.broadcast_to(lax.rsqrt(squares / D + EPSILON), out_ref.shape)


def inv_rms(own, other):
    return call(
        scale_kernel,
        jax.ShapeDtypeStruct(own.shape, jnp.float32),
        in_specs=[WHOLE] * 2,
        out_specs=WHOLE,
    )(own, other)


def summed(refs, index, scale_ref):
    total = refs[0][index]
    for ref in refs[1:]:
        total += ref[index].astype(jnp.float32)
    return total * scale_ref[...]


def turned(block, cosine_ref, sine_ref):
    half = HEAD // 2
    other = jnp.concatenate([block[:, half:], block[:, :half]], axis=1)
    return block * cosine_ref[...] + other * sine_ref[...]


def kv_kernel(own, r0, r1, r2, scale_ref, cosine_ref, sine_ref, out_ref):
    block = summed((own, r0, r1, r2), 0, scale_ref)
    spun = turned(block, cosine_ref, sine_ref)
    out_ref[...] = jnp.where(lax.axis_index("tensor") == 0, spun, block).astype(jnp.bfloat16)


def heads_kernel(first, n_parts, *refs):
    parts, refs = refs[:n_parts], refs[n_parts:]
    scale_ref, cosine_ref, sine_ref, allowed_ref, keep_ref, mine_ref, other_ref, *rest = refs
    earlier_refs, out_ref, scratch = rest[:-1], rest[-1], None
    if len(rest) > 1:
        earlier_ref, out_ref, scratch, sems = rest
        earlier_refs = [earlier_ref]
    copies = []

    def put(source, at):
        where = pl.ds(pl.multiple_of(at, HEAD), HEAD)
        copies.append(pltpu.make_async_copy(source, out_ref.at[:, where], sems.at[len(copies)]))
        copies[-1].start()

    is_key = lax.axis_index("tensor") == 0
    mine, other = mine_ref[...], other_ref[...]
    keys = jnp.where(is_key, mine, other)
    values = jnp.where(is_key, other, mine)
    count = parts[0].shape[0] - first
    before = jnp.where(is_key, HEAD, 0)
    for earlier_ref in earlier_refs:
        put(earlier_ref, jnp.where(is_key, 0, count * HEAD))
    tokens = mine.shape[0]
    query = [turned(summed(parts, first + i, scale_ref), cosine_ref, sine_ref).astype(jnp.bfloat16) for i in range(count)]
    scores = lax.dot_general(
        jnp.concatenate(query, axis=0), keys, (((1,), (1,)), ((), ())), preferred_element_type=jnp.float32
    ) * HEAD ** (-0.5)
    allowed = jnp.concatenate([allowed_ref[...] > 0.0] * count, axis=0)
    scores = jnp.where(allowed, scores, -1e30)
    expo = jnp.exp(scores - jnp.max(scores, axis=-1, keepdims=True))
    attn = (expo * (1.0 / jnp.sum(expo, axis=-1, keepdims=True))).astype(jnp.bfloat16)
    mixed = jnp.dot(attn, values, preferred_element_type=jnp.float32)
    for i in range(count):
        done = (mixed[i * tokens:(i + 1) * tokens] * keep_ref[...]).astype(jnp.bfloat16)
        if scratch is None:
            out_ref[:, i * HEAD:(i + 1) * HEAD] = done
        else:
            scratch[i] = done
            put(scratch.at[i], before + i * HEAD)
    for copy in copies:
        copy.wait()


def heads(parts, first, scale, tabled, mine, other, *earlier):
    args = [*parts, scale, *tabled, mine, other, *earlier]
    tokens = mine.shape[0]
    count = parts[0].shape[0] - first
    out_shape = jax.ShapeDtypeStruct((tokens, count * HEAD + sum(e.shape[1] for e in earlier)), jnp.bfloat16)
    scratch = [pltpu.VMEM((count, tokens, HEAD), jnp.bfloat16), pltpu.SemaphoreType.DMA((count + len(earlier),))]
    return call(
        functools.partial(heads_kernel, first, len(parts)),
        out_shape,
        result=bool(earlier),
        in_specs=[WHOLE] * len(args),
        out_specs=pl.BlockSpec(memory_space=pltpu.HBM) if earlier else WHOLE,
        scratch_shapes=scratch if earlier else [],
    )(*args)


def staged(hidden_in, norm_gain, projection, lengths):
    groups = lax.axis_size("groups")
    dp = lax.axis_size("dp")
    tensor = lax.axis_size("tensor")
    depth = dp // 2
    tokens = hidden_in.shape[0]
    part = projection.shape[1] // groups
    heads_local = QHEADS // tensor

    ring = [(i, (i + 2) % dp) for i in range(dp)]
    over_x = swap(dp)
    over_y = swap(groups)
    over_core = swap(tensor)
    across = [(g * dp + i, (g ^ 1) * dp + (i ^ 1)) for g in range(groups) for i in range(dp)]

    def to_core(a):
        return lax.ppermute(a, "tensor", over_core)

    def on_ring(a):
        return lax.ppermute(a, "dp", ring)

    def back(a):
        return lax.ppermute(a, "dp", [(j, i) for i, j in ring])

    def to_far(a):
        return lax.ppermute(a, ("groups", "dp"), across)

    def to_x(a):
        return lax.ppermute(a, "dp", over_x)

    def to_y(a):
        return lax.ppermute(a, "groups", over_y)

    def to_plane(three):
        return [to_far(three[0]), to_x(three[1]), to_y(three[2])]

    last = []

    def after(*values):
        held = lax.optimization_barrier(tuple(values) + tuple(last))[:len(values)]
        last[:] = held[:1]
        return held[0] if len(values) == 1 else held

    columns = [(QHEADS + c) * HEAD for c in range(tensor)] + [0, (QHEADS - 1) * HEAD]

    def rows_b(projection):
        flat = projection.reshape(projection.shape[1:])
        start = (lax.axis_index("groups") * part, HEAD)
        return lax.dynamic_slice(flat, start, (part, 2 * (heads_local - 1) * HEAD))

    b1 = on_ring(rows_b(projection))
    far, near_x, near_y, own, squares = after(*gate(hidden_in, norm_gain, part, depth))
    near_x = to_x(near_x)
    near_y = to_y(near_y)
    a0, = select(after(projection), part, [columns])
    a0 = after(a0)
    a1 = on_ring(a0)
    other_squares = to_core(squares)
    tabled = after(*tables(tokens, lengths, after(squares)))
    scale = after(inv_rms(squares, after(other_squares)))

    b1, a0, far = after(b1, a0, far)
    a3 = back(a0)
    far = to_far(far)
    a1 = after(a1)
    a2 = on_ring(a1)
    b0 = after(rows_b(after(projection)))
    near_y = after(near_y)
    near_x = after(near_x)
    a3, b1 = after(a3, b1)
    b2 = on_ring(b1)
    early = (near_x, near_y, own)
    front = after(matmul(early, (a0, a1, a3), (0, 1, 3)))
    a2 = after(a2)
    set_a = (a0, a1, a2, a3)

    *theirs, mine = after(*matmul(early, (a2,), (2,), (front,), sent=2))
    swapped = [to_core(t) for t in theirs]
    far, b0 = after(far, b0)
    b3 = back(b0)
    sums_x, sums_y, sums = after(*join(mine, after(*swapped), (jnp.bfloat16, jnp.bfloat16, jnp.float32)))
    sums_x = to_x(sums_x)
    sums_y = to_y(sums_y)
    acts = (far, own, near_x, near_y)
    *theirs, mine = after(*matmul((far,), set_a, (0, 1, 2, 3), sent=1))
    swapped = [to_core(t) for t in theirs]
    b2 = after(b2)
    swapped = [after(t) for t in swapped]
    sums_far = after(*join(mine, swapped, (jnp.bfloat16,)))
    sums_far = to_far(sums_far)
    sums_y = after(sums_y)
    sums_x = after(sums_x)
    front = after(matmul(acts, (b0, b1, b2), (0, 1, 2)))

    b3 = after(b3)
    parts_a = after(sums, sums_far, sums_x, sums_y)
    *theirs, mine = after(*matmul(acts, (b3,), (3,), (front,), sent=2, paired=False))
    swapped = [to_core(t) for t in theirs]
    kv = after(call(
        kv_kernel,
        jax.ShapeDtypeStruct((tokens, HEAD), jnp.bfloat16),
        in_specs=[WHOLE] * 7,
        out_specs=WHOLE,
    )(*parts_a, scale, *tabled[:2]))
    vk = to_core(kv)
    sums_far, sums = after(*join(mine, (after(swapped[0]),), (jnp.bfloat16, jnp.float32)))
    sums_far = to_far(sums_far)
    sums_x, sums_y = after(*join(mine, (after(swapped[1]),), (jnp.bfloat16, jnp.bfloat16), first=2))
    sums_x = to_x(sums_x)
    sums_y = to_y(sums_y)
    vk = after(vk)
    one = after(heads(parts_a, 1, scale, tabled, kv, vk))
    sums_far = after(sums_far)
    sums_x, sums_y = after(sums_x, sums_y)
    return heads((sums, sums_far, sums_x, sums_y), 0, scale, tabled, kv, vk, one)


def local(hidden_in, norm_gain, projection, lengths):
    part = projection.shape[1] // lax.axis_size("groups")
    if lax.axis_size("dp") == 8 and part % HEAD == 0:
        return staged(hidden_in, norm_gain, projection, lengths)
    return general(hidden_in, norm_gain, projection, lengths)


def solution(mesh):
    in_specs = (
        P(("groups", "dp"), "tensor"),
        P("tensor"),
        P("tensor", "dp", None),
        P(("groups", "dp"), None),
    )
    out_specs = P(("groups", "dp"), "tensor")
    return jax.shard_map(local, mesh=mesh, in_specs=in_specs, out_specs=out_specs, check_vma=False)
```

```python
import functools
import math

import jax
import jax.numpy as jnp
from jax import lax
from jax.experimental import pallas as pl
from jax.experimental.pallas import tpu as pltpu
from jax.sharding import PartitionSpec as P

D = 12288
HEAD = 128
QHEADS = 6
ROPE_BASE = 1000000.0
EPSILON = 1e-05


def angles(seq_len):
    half = HEAD // 2
    positions = jnp.arange(seq_len, dtype=jnp.int32)
    freq = ROPE_BASE ** (-(jnp.arange(half, dtype=jnp.float32) * 2.0 / HEAD))
    angle = positions.astype(jnp.float32)[:, None] * freq[None, :]
    return jnp.cos(angle), jnp.sin(angle)


def rotate(block, cosine, sine):
    half = HEAD // 2
    first = block[:, :half]
    second = block[:, half:]
    return jnp.concatenate([first * cosine - second * sine, second * cosine + first * sine], axis=-1)


def attend_head(query, keys, values, allowed, keep):
    scores = lax.dot_general(
        query, keys, (((1,), (1,)), ((), ())), preferred_element_type=jnp.float32
    ) * HEAD ** (-0.5)
    scores = jnp.where(allowed, scores, -1e30)
    largest = jnp.max(scores, axis=-1, keepdims=True)
    expo = jnp.exp(scores - largest)
    attn = (expo / jnp.sum(expo, axis=-1, keepdims=True)).astype(jnp.bfloat16)
    mixed = jnp.dot(attn, values, preferred_element_type=jnp.float32)
    return (mixed * keep).astype(jnp.bfloat16)


def swap(size):
    return [(i, i ^ 1) for i in range(size)]


def general(hidden_in, norm_gain, projection, lengths):
    groups = lax.axis_size("groups")
    dp = lax.axis_size("dp")
    tensor = lax.axis_size("tensor")
    y = lax.axis_index("groups")
    place = lax.axis_index("dp")
    core = lax.axis_index("tensor")
    x = place % 2
    z = place // 2
    depth = dp // 2
    tokens = hidden_in.shape[0]
    rows = projection.shape[1]
    part = rows // groups
    heads_local = QHEADS // tensor

    ring = [(i, (i + 2) % dp) for i in range(dp)]
    over_x = swap(dp)
    over_y = swap(groups)
    over_core = swap(tensor)
    across = [(g * dp + i, (g ^ 1) * dp + (i ^ 1)) for g in range(groups) for i in range(dp)]

    mine = lax.dynamic_slice_in_dim(projection[0], y * part, part, 0)

    def column(owner, index):
        start = (QHEADS + owner) * HEAD if index == 0 else (owner * heads_local + index - 1) * HEAD
        return lax.dynamic_slice_in_dim(mine, start, HEAD, 1)

    n_cols = heads_local + 1
    theirs = jnp.concatenate([column(1 - core, i) for i in range(n_cols)], axis=1)
    other = lax.ppermute(theirs, "tensor", over_core)
    weights = []
    for i in range(n_cols):
        slot = jnp.concatenate([column(core, i), other[:, i * HEAD:(i + 1) * HEAD]], axis=0)
        weights.append([slot])
    for _ in range(depth - 1):
        for i in range(n_cols):
            weights[i].append(lax.ppermute(weights[i][-1], "dp", ring))

    wide32 = hidden_in.astype(jnp.float32)
    gated = (wide32 * norm_gain.astype(jnp.float32)[None, :]).astype(jnp.bfloat16)
    local_sq = jnp.sum(wide32 * wide32, axis=1)
    total_sq = local_sq + lax.ppermute(local_sq, "tensor", over_core)
    inv_rms = lax.rsqrt(total_sq / D + EPSILON)[:, None]

    def piece(dx, dy):
        slabs = []
        for k in range(depth):
            shard = ((z - k + depth) % depth) * 2 + (x ^ dx)
            slabs.append(lax.dynamic_slice_in_dim(gated, shard * rows + (y ^ dy) * part, part, 1))
        return jnp.stack(slabs)

    sent = [piece(1, 1), piece(1, 0), piece(0, 1)]
    held = [
        lax.ppermute(sent[0], ("groups", "dp"), across),
        lax.ppermute(sent[1], "dp", over_x),
        lax.ppermute(sent[2], "groups", over_y),
        piece(0, 0),
    ]
    acts = []
    for h in held:
        acts.append(jnp.concatenate([h, lax.ppermute(h, "tensor", over_core)], axis=2))
    acts = jnp.concatenate(acts, axis=1)

    cosine, sine = angles(tokens)
    positions = jnp.arange(tokens, dtype=jnp.int32)
    prompt = lengths[0, 0]
    total_len = prompt + lengths[0, 1]
    allowed = (positions[None, :] <= positions[:, None]) & (positions[None, :] < total_len)
    keep = ((positions >= prompt - 1) & (positions < total_len - 1)).astype(jnp.float32)[:, None]

    outs = []
    keys = values = None
    for i in range(n_cols):
        partial = sum(
            jnp.dot(acts[k], weights[i][k], preferred_element_type=jnp.float32) for k in range(depth)
        )
        blocks = partial.reshape(4, tokens, HEAD)
        low = blocks[:3].astype(jnp.bfloat16)
        summed = blocks[3]
        summed = summed + lax.ppermute(low[0], ("groups", "dp"), across).astype(jnp.float32)
        summed = summed + lax.ppermute(low[1], "dp", over_x).astype(jnp.float32)
        summed = summed + lax.ppermute(low[2], "groups", over_y).astype(jnp.float32)
        scaled = summed * inv_rms
        if i == 0:
            turned = rotate(scaled, cosine, sine)
            kv = jnp.where(core == 0, turned, scaled).astype(jnp.bfloat16)
            vk = lax.ppermute(kv, "tensor", over_core)
            keys = jnp.where(core == 0, kv, vk)
            values = jnp.where(core == 0, vk, kv)
        else:
            query = rotate(scaled, cosine, sine).astype(jnp.bfloat16)
            outs.append(attend_head(query, keys, values, allowed, keep))
    return jnp.concatenate(outs, axis=1)


VMEM = pltpu.VMEM
PLANE = ((1, 1), (1, 0), (0, 1), (0, 0))
WHOLE = pl.BlockSpec(memory_space=VMEM)
SCALARS = pl.BlockSpec(memory_space=pltpu.SMEM)


def call(kernel, out_shape, limit=12, result=False, **kwargs):
    if not result:
        out_shape = jax.tree.map(lambda s: pltpu.VMEM(s.shape, s.dtype), out_shape)
    return pl.pallas_call(
        kernel,
        out_shape=out_shape,
        compiler_params=pltpu.CompilerParams(vmem_limit_bytes=limit * 2**20),
        cost_estimate=pl.CostEstimate(flops=1, bytes_accessed=1, transcendentals=0),
        **kwargs,
    )


def select_kernel(columns, part, rows_ref, *refs):
    out_refs, sems = refs[:len(columns)], refs[-1]
    rows = pl.ds(pl.multiple_of(lax.axis_index("groups") * part, HEAD), part)
    copies = []
    for starts, out_ref in zip(columns, out_refs):
        at = 0
        while at < len(starts):
            more = 1
            while at + more < len(starts) and starts[at + more] == starts[at] + more * HEAD:
                more += 1
            copies.append(pltpu.make_async_copy(
                rows_ref.at[0, rows, pl.ds(starts[at], more * HEAD)],
                out_ref.at[:, pl.ds(at * HEAD, more * HEAD)],
                sems.at[len(copies)],
            ))
            at += more
    for copy in copies:
        copy.start()
    for copy in copies:
        copy.wait()


def select(projection, part, columns):
    chunk = jax.ShapeDtypeStruct((part, len(columns[0]) * HEAD), projection.dtype)
    out_shape = (chunk,) * len(columns)
    return call(
        functools.partial(select_kernel, columns, part),
        out_shape,
        in_specs=[pl.BlockSpec(memory_space=pltpu.HBM)],
        out_specs=[WHOLE] * len(out_shape),
        scratch_shapes=[pltpu.SemaphoreType.DMA((len(columns) * len(columns[0]),))],
    )(projection)


def gate_kernel(part, depth, hidden_ref, gain_ref, *refs):
    piece_refs, (sq_ref, slab_ref, flat_ref, row_ref, sems) = refs[:4], refs[4:]
    place = lax.axis_index("dp")
    x, z, y = place % 2, place // 2, lax.axis_index("groups")
    wide = 4 * part
    columns = [pl.ds(pl.multiple_of(lax.rem(z - k + depth, depth) * wide, HEAD), wide) for k in range(depth)]
    copies = [pltpu.make_async_copy(hidden_ref.at[:, c], slab_ref.at[k], sems.at[k]) for k, c in enumerate(columns)]
    gain_copy = pltpu.make_async_copy(gain_ref, flat_ref, sems.at[depth])
    gain_copy.start()
    for copy in copies:
        copy.start()
    gain_copy.wait()
    row_ref[0, :] = flat_ref[...].astype(jnp.float32)
    tokens = hidden_ref.shape[0]
    height = 64
    for k, copy in enumerate(copies):
        copy.wait()
        for top in range(0, tokens, height):
            rows = slice(top, top + height)
            total = jnp.zeros((height, HEAD), jnp.float32)
            for piece_ref, (dx, dy) in zip(piece_refs, PLANE):
                start = ((x ^ dx) * 2 + (y ^ dy)) * part
                whole = slab_ref[k, rows, pl.ds(pl.multiple_of(start, HEAD), part)].astype(jnp.float32)
                at = lax.rem(z - k + depth, depth) * wide + start
                gain = row_ref[:, pl.ds(pl.multiple_of(at, HEAD), part)]
                piece_ref[k, rows] = (whole * gain).astype(jnp.bfloat16)
                square = whole * whole
                for j in range(0, part, HEAD):
                    total += square[:, j:j + HEAD]
            sq_ref[rows] = total if k == 0 else sq_ref[rows] + total


def gate(hidden_in, norm_gain, part, depth):
    tokens = hidden_in.shape[0]
    piece = jax.ShapeDtypeStruct((depth, tokens, part), jnp.bfloat16)
    return call(
        functools.partial(gate_kernel, part, depth),
        (piece,) * 4 + (jax.ShapeDtypeStruct((tokens, HEAD), jnp.float32),),
        in_specs=[pl.BlockSpec(memory_space=pltpu.HBM)] * 2,
        out_specs=[WHOLE] * 5,
        scratch_shapes=[
            pltpu.VMEM((depth, tokens, 4 * part), jnp.bfloat16),
            pltpu.VMEM(norm_gain.shape, norm_gain.dtype),
            pltpu.VMEM((1, norm_gain.shape[0]), jnp.float32),
            pltpu.SemaphoreType.DMA((depth + 1,)),
        ],
    )(*(pltpu.with_memory_space_constraint(a, pltpu.HBM) for a in (hidden_in, norm_gain)))


def matmul_kernel(firsts, n_acts, n_more, sent, paired, *refs):
    is_first = lax.axis_index("tensor") == 0
    acts, refs = refs[:n_acts], refs[n_acts:]
    slots, refs = refs[:len(firsts)], refs[len(firsts):]
    more, out_refs = refs[:n_more], refs[n_more:]
    more = [(ref, i) for ref in more for i in range(ref.shape[0])]
    right = [slot[...] for slot in slots]
    wide = 2 * HEAD
    for p in range(n_acts):
        total = jnp.dot(acts[p][firsts[0]], right[0], preferred_element_type=jnp.float32)
        for k in range(1, len(firsts)):
            total += jnp.dot(acts[p][firsts[k]], right[k], preferred_element_type=jnp.float32)
        if more:
            ref, i = more[p]
            total += ref[i]
        if not sent:
            out_refs[0][p] = total
            continue
        theirs_refs, mine_ref = out_refs[:-1], out_refs[-1]
        n_blocks = mine_ref.shape[1]
        per = n_acts * n_blocks // sent
        for g in range(n_blocks):
            at, apart = (g * wide, HEAD) if paired else (g * HEAD, n_blocks * HEAD)
            low = total[:, at:at + HEAD]
            high = total[:, at + apart:at + apart + HEAD]
            spot = p * n_blocks + g
            theirs_refs[spot // per][spot % per] = jnp.where(is_first, high, low).astype(jnp.bfloat16)
            mine_ref[p, g] = jnp.where(is_first, low, high)


def matmul(acts, slots, firsts, so_far=(), sent=0, paired=True):
    n_blocks = slots[0].shape[1] // (2 * HEAD)
    tokens = acts[0].shape[1]
    args = [*acts, *slots, *so_far]
    if sent:
        out_shape = (jax.ShapeDtypeStruct((len(acts) * n_blocks // sent, tokens, HEAD), jnp.bfloat16),) * sent
        out_shape += (jax.ShapeDtypeStruct((len(acts), n_blocks, tokens, HEAD), jnp.float32),)
    else:
        out_shape = (jax.ShapeDtypeStruct((len(acts), tokens, n_blocks * 2 * HEAD), jnp.float32),)
    outs = call(
        functools.partial(matmul_kernel, firsts, len(acts), len(so_far), sent, paired),
        out_shape,
        in_specs=[WHOLE] * len(args),
        out_specs=[WHOLE] * len(out_shape),
    )(*args)
    return outs if sent else outs[0]


def half_kernel(first, swapped, n_acts, *refs):
    acts, (slot_ref, more_ref), out_refs = refs[:n_acts], refs[n_acts:n_acts + 2], refs[n_acts + 2:]
    core = lax.axis_index("tensor")
    width = slot_ref.shape[1] // 2
    where = pl.ds(pl.multiple_of((1 - core if swapped else core) * width, HEAD), width)
    right = slot_ref[:, where]
    n_blocks = width // HEAD
    per = n_acts * n_blocks // len(out_refs)
    for p in range(n_acts):
        total = jnp.dot(acts[p][first], right, preferred_element_type=jnp.float32) + more_ref[p, :, where]
        for g in range(n_blocks):
            spot = p * n_blocks + g
            out_ref = out_refs[spot // per]
            out_ref[spot % per] = total[:, g * HEAD:(g + 1) * HEAD].astype(out_ref.dtype)


def half_matmul(acts, slot, first, so_far, swapped, pieces, dtype):
    tokens, width = acts[0].shape[1], slot.shape[1] // 2
    args = [*acts, slot, so_far]
    rows = len(acts) * width // HEAD // pieces
    return call(
        functools.partial(half_kernel, first, swapped, len(acts)),
        (jax.ShapeDtypeStruct((rows, tokens, HEAD), dtype),) * pieces,
        in_specs=[WHOLE] * len(args),
        out_specs=[WHOLE] * pieces,
    )(*args)


def join_kernel(n_came, first, mine_ref, *refs):
    came_refs, out_refs = refs[:n_came], refs[n_came:]
    n_blocks = mine_ref.shape[1]
    per = len(out_refs) * n_blocks // n_came
    for p, out_ref in enumerate(out_refs):
        for g in range(n_blocks):
            spot = p * n_blocks + g
            came = came_refs[spot // per][spot % per].astype(jnp.float32)
            out_ref[g] = (mine_ref[first + p, g] + came).astype(out_ref.dtype)


def join(mine, came, types, first=0):
    return call(
        functools.partial(join_kernel, len(came), first),
        tuple(jax.ShapeDtypeStruct(mine.shape[1:], t) for t in types),
        in_specs=[WHOLE] * (1 + len(came)),
        out_specs=[WHOLE] * len(types),
    )(mine, *came)


def tables_kernel(lengths_ref, _, cosine_ref, sine_ref, allowed_ref, keep_ref):
    at = lax.broadcasted_iota(jnp.int32, cosine_ref.shape, 0)
    lane = lax.broadcasted_iota(jnp.int32, cosine_ref.shape, 1)
    pair = lax.rem(lane, HEAD // 2).astype(jnp.float32)
    angle = at.astype(jnp.float32) * jnp.exp(pair * (-2.0 * math.log(ROPE_BASE) / HEAD))
    cosine_ref[...] = jnp.cos(angle)
    sine_ref[...] = jnp.where(lane < HEAD // 2, -jnp.sin(angle), jnp.sin(angle))
    prompt = lengths_ref[0, 0]
    total_len = prompt + lengths_ref[0, 1]
    keep_ref[...] = ((at >= prompt - 1) & (at < total_len - 1)).astype(jnp.float32)
    query_at = lax.broadcasted_iota(jnp.int32, allowed_ref.shape, 0)
    key_at = lax.broadcasted_iota(jnp.int32, allowed_ref.shape, 1)
    allowed_ref[...] = ((key_at <= query_at) & (key_at < total_len)).astype(jnp.float32)


def tables(tokens, lengths, later_than):
    table = jax.ShapeDtypeStruct((tokens, HEAD), jnp.float32)
    allowed = jax.ShapeDtypeStruct((tokens, tokens), jnp.float32)
    return call(
        tables_kernel,
        (table, table, allowed, table),
        in_specs=[SCALARS, pl.BlockSpec(memory_space=pl.ANY)],
        out_specs=[WHOLE] * 4,
    )(lengths, later_than)


def scale_kernel(own_ref, other_ref, out_ref):
    squares = jnp.sum(own_ref[...] + other_ref[...], axis=1, keepdims=True)
    out_ref[...] = jnp.broadcast_to(lax.rsqrt(squares / D + EPSILON), out_ref.shape)


def inv_rms(own, other):
    return call(
        scale_kernel,
        jax.ShapeDtypeStruct(own.shape, jnp.float32),
        in_specs=[WHOLE] * 2,
        out_specs=WHOLE,
    )(own, other)


def summed(refs, index, scale_ref):
    total = refs[0][index]
    for ref in refs[1:]:
        total += ref[index].astype(jnp.float32)
    return total * scale_ref[...]


def turned(block, cosine_ref, sine_ref):
    half = HEAD // 2
    other = jnp.concatenate([block[:, half:], block[:, :half]], axis=1)
    return block * cosine_ref[...] + other * sine_ref[...]


def kv_kernel(own, r0, r1, r2, scale_ref, cosine_ref, sine_ref, out_ref):
    block = summed((own, r0, r1, r2), 0, scale_ref)
    spun = turned(block, cosine_ref, sine_ref)
    out_ref[...] = jnp.where(lax.axis_index("tensor") == 0, spun, block).astype(jnp.bfloat16)


def heads_kernel(first, n_parts, *refs):
    parts, refs = refs[:n_parts], refs[n_parts:]
    scale_ref, cosine_ref, sine_ref, allowed_ref, keep_ref, mine_ref, other_ref, *rest = refs
    earlier_refs, out_ref, scratch = rest[:-1], rest[-1], None
    if len(rest) > 1:
        earlier_ref, out_ref, scratch, sems = rest
        earlier_refs = [earlier_ref]
    copies = []

    def put(source, at):
        where = pl.ds(pl.multiple_of(at, HEAD), HEAD)
        copies.append(pltpu.make_async_copy(source, out_ref.at[:, where], sems.at[len(copies)]))
        copies[-1].start()

    is_key = lax.axis_index("tensor") == 0
    mine, other = mine_ref[...], other_ref[...]
    keys = jnp.where(is_key, mine, other)
    values = jnp.where(is_key, other, mine)
    count = parts[0].shape[0] - first
    before = jnp.where(is_key, HEAD, 0)
    for earlier_ref in earlier_refs:
        put(earlier_ref, jnp.where(is_key, 0, count * HEAD))
    tokens = mine.shape[0]
    query = [turned(summed(parts, first + i, scale_ref), cosine_ref, sine_ref).astype(jnp.bfloat16) for i in range(count)]
    scores = lax.dot_general(
        jnp.concatenate(query, axis=0), keys, (((1,), (1,)), ((), ())), preferred_element_type=jnp.float32
    ) * HEAD ** (-0.5)
    allowed = jnp.concatenate([allowed_ref[...] > 0.0] * count, axis=0)
    scores = jnp.where(allowed, scores, -1e30)
    expo = jnp.exp(scores - jnp.max(scores, axis=-1, keepdims=True))
    attn = (expo * (1.0 / jnp.sum(expo, axis=-1, keepdims=True))).astype(jnp.bfloat16)
    mixed = jnp.dot(attn, values, preferred_element_type=jnp.float32)
    for i in range(count):
        done = (mixed[i * tokens:(i + 1) * tokens] * keep_ref[...]).astype(jnp.bfloat16)
        if scratch is None:
            out_ref[:, i * HEAD:(i + 1) * HEAD] = done
        else:
            scratch[i] = done
            put(scratch.at[i], before + i * HEAD)
    for copy in copies:
        copy.wait()


def heads(parts, first, scale, tabled, mine, other, *earlier):
    args = [*parts, scale, *tabled, mine, other, *earlier]
    tokens = mine.shape[0]
    count = parts[0].shape[0] - first
    out_shape = jax.ShapeDtypeStruct((tokens, count * HEAD + sum(e.shape[1] for e in earlier)), jnp.bfloat16)
    scratch = [pltpu.VMEM((count, tokens, HEAD), jnp.bfloat16), pltpu.SemaphoreType.DMA((count + len(earlier),))]
    return call(
        functools.partial(heads_kernel, first, len(parts)),
        out_shape,
        result=bool(earlier),
        in_specs=[WHOLE] * len(args),
        out_specs=pl.BlockSpec(memory_space=pltpu.HBM) if earlier else WHOLE,
        scratch_shapes=scratch if earlier else [],
    )(*args)


def staged(hidden_in, norm_gain, projection, lengths):
    groups = lax.axis_size("groups")
    dp = lax.axis_size("dp")
    tensor = lax.axis_size("tensor")
    depth = dp // 2
    tokens = hidden_in.shape[0]
    part = projection.shape[1] // groups
    heads_local = QHEADS // tensor

    ring = [(i, (i + 2) % dp) for i in range(dp)]
    over_x = swap(dp)
    over_y = swap(groups)
    over_core = swap(tensor)
    across = [(g * dp + i, (g ^ 1) * dp + (i ^ 1)) for g in range(groups) for i in range(dp)]

    def to_core(a):
        return lax.ppermute(a, "tensor", over_core)

    def on_ring(a):
        return lax.ppermute(a, "dp", ring)

    def back(a):
        return lax.ppermute(a, "dp", [(j, i) for i, j in ring])

    def to_far(a):
        return lax.ppermute(a, ("groups", "dp"), across)

    def to_x(a):
        return lax.ppermute(a, "dp", over_x)

    def to_y(a):
        return lax.ppermute(a, "groups", over_y)

    def to_plane(three):
        return [to_far(three[0]), to_x(three[1]), to_y(three[2])]

    last = []

    def after(*values):
        held = lax.optimization_barrier(tuple(values) + tuple(last))[:len(values)]
        last[:] = held[:1]
        return held[0] if len(values) == 1 else held

    columns = [(QHEADS + c) * HEAD for c in range(tensor)] + [0, (QHEADS - 1) * HEAD]

    def rows_b(projection):
        flat = projection.reshape(projection.shape[1:])
        start = (lax.axis_index("groups") * part, HEAD)
        return lax.dynamic_slice(flat, start, (part, 2 * (heads_local - 1) * HEAD))

    b1 = on_ring(rows_b(projection))
    far, near_x, near_y, own, squares = after(*gate(hidden_in, norm_gain, part, depth))
    near_x = to_x(near_x)
    near_y = to_y(near_y)
    a0, = select(after(projection), part, [columns])
    a0 = after(a0)
    a1 = on_ring(a0)
    other_squares = to_core(squares)
    tabled = after(*tables(tokens, lengths, after(squares)))
    scale = after(inv_rms(squares, after(other_squares)))

    b1, a0, far = after(b1, a0, far)
    a3 = back(a0)
    far = to_far(far)
    a1 = after(a1)
    a2 = on_ring(a1)
    b0 = after(rows_b(after(projection)))
    near_y = after(near_y)
    near_x = after(near_x)
    a3, b1 = after(a3, b1)
    b2 = on_ring(b1)
    early = (near_x, near_y, own)
    front = after(matmul(early, (a0, a1, a3), (0, 1, 3)))
    a2 = after(a2)
    set_a = (a0, a1, a2, a3)

    *theirs, mine = after(*matmul(early, (a2,), (2,), (front,), sent=2))
    swapped = [to_core(t) for t in theirs]
    far, b0 = after(far, b0)
    b3 = back(b0)
    sums_x, sums_y, sums = after(*join(mine, after(*swapped), (jnp.bfloat16, jnp.bfloat16, jnp.float32)))
    sums_x = to_x(sums_x)
    sums_y = to_y(sums_y)
    acts = (far, own, near_x, near_y)
    *theirs, mine = after(*matmul((far,), set_a, (0, 1, 2, 3), sent=1))
    swapped = [to_core(t) for t in theirs]
    b2 = after(b2)
    swapped = [after(t) for t in swapped]
    sums_far = after(*join(mine, swapped, (jnp.bfloat16,)))
    sums_far = to_far(sums_far)
    sums_y = after(sums_y)
    sums_x = after(sums_x)
    front = after(matmul(acts, (b0, b1, b2), (0, 1, 2)))

    b3 = after(b3)
    parts_a = after(sums, sums_far, sums_x, sums_y)
    theirs = after(*half_matmul(acts, b3, 3, front, True, 2, jnp.bfloat16))
    swapped = [to_core(t) for t in theirs]
    mine, = half_matmul(acts, after(b3), 3, front, False, 1, jnp.float32)
    mine = mine.reshape(len(acts), -1, *mine.shape[1:])
    kv = after(call(
        kv_kernel,
        jax.ShapeDtypeStruct((tokens, HEAD), jnp.bfloat16),
        in_specs=[WHOLE] * 7,
        out_specs=WHOLE,
    )(*parts_a, scale, *tabled[:2]))
    vk = to_core(kv)
    sums_far, sums = after(*join(mine, (after(swapped[0]),), (jnp.bfloat16, jnp.float32)))
    sums_far = to_far(sums_far)
    sums_x, sums_y = after(*join(mine, (after(swapped[1]),), (jnp.bfloat16, jnp.bfloat16), first=2))
    sums_x = to_x(sums_x)
    sums_y = to_y(sums_y)
    vk = after(vk)
    one = after(heads(parts_a, 1, scale, tabled, kv, vk))
    sums_far = after(sums_far)
    sums_x, sums_y = after(sums_x, sums_y)
    return heads((sums, sums_far, sums_x, sums_y), 0, scale, tabled, kv, vk, one)


def local(hidden_in, norm_gain, projection, lengths):
    part = projection.shape[1] // lax.axis_size("groups")
    if lax.axis_size("dp") == 8 and part % HEAD == 0:
        return staged(hidden_in, norm_gain, projection, lengths)
    return general(hidden_in, norm_gain, projection, lengths)


def solution(mesh):
    in_specs = (
        P(("groups", "dp"), "tensor"),
        P("tensor"),
        P("tensor", "dp", None),
        P(("groups", "dp"), None),
    )
    out_specs = P(("groups", "dp"), "tensor")
    return jax.shard_map(local, mesh=mesh, in_specs=in_specs, out_specs=out_specs, check_vma=False)
```

```python
import functools
import math

import jax
import jax.numpy as jnp
from jax import lax
from jax.experimental import pallas as pl
from jax.experimental.pallas import tpu as pltpu
from jax.sharding import PartitionSpec as P

D = 12288
HEAD = 128
QHEADS = 6
ROPE_BASE = 1000000.0
EPSILON = 1e-05


def angles(seq_len):
    half = HEAD // 2
    positions = jnp.arange(seq_len, dtype=jnp.int32)
    freq = ROPE_BASE ** (-(jnp.arange(half, dtype=jnp.float32) * 2.0 / HEAD))
    angle = positions.astype(jnp.float32)[:, None] * freq[None, :]
    return jnp.cos(angle), jnp.sin(angle)


def rotate(block, cosine, sine):
    half = HEAD // 2
    first = block[:, :half]
    second = block[:, half:]
    return jnp.concatenate([first * cosine - second * sine, second * cosine + first * sine], axis=-1)


def attend_head(query, keys, values, allowed, keep):
    scores = lax.dot_general(
        query, keys, (((1,), (1,)), ((), ())), preferred_element_type=jnp.float32
    ) * HEAD ** (-0.5)
    scores = jnp.where(allowed, scores, -1e30)
    largest = jnp.max(scores, axis=-1, keepdims=True)
    expo = jnp.exp(scores - largest)
    attn = (expo / jnp.sum(expo, axis=-1, keepdims=True)).astype(jnp.bfloat16)
    mixed = jnp.dot(attn, values, preferred_element_type=jnp.float32)
    return (mixed * keep).astype(jnp.bfloat16)


def swap(size):
    return [(i, i ^ 1) for i in range(size)]


def general(hidden_in, norm_gain, projection, lengths):
    groups = lax.axis_size("groups")
    dp = lax.axis_size("dp")
    tensor = lax.axis_size("tensor")
    y = lax.axis_index("groups")
    place = lax.axis_index("dp")
    core = lax.axis_index("tensor")
    x = place % 2
    z = place // 2
    depth = dp // 2
    tokens = hidden_in.shape[0]
    rows = projection.shape[1]
    part = rows // groups
    heads_local = QHEADS // tensor

    ring = [(i, (i + 2) % dp) for i in range(dp)]
    over_x = swap(dp)
    over_y = swap(groups)
    over_core = swap(tensor)
    across = [(g * dp + i, (g ^ 1) * dp + (i ^ 1)) for g in range(groups) for i in range(dp)]

    mine = lax.dynamic_slice_in_dim(projection[0], y * part, part, 0)

    def column(owner, index):
        start = (QHEADS + owner) * HEAD if index == 0 else (owner * heads_local + index - 1) * HEAD
        return lax.dynamic_slice_in_dim(mine, start, HEAD, 1)

    n_cols = heads_local + 1
    theirs = jnp.concatenate([column(1 - core, i) for i in range(n_cols)], axis=1)
    other = lax.ppermute(theirs, "tensor", over_core)
    weights = []
    for i in range(n_cols):
        slot = jnp.concatenate([column(core, i), other[:, i * HEAD:(i + 1) * HEAD]], axis=0)
        weights.append([slot])
    for _ in range(depth - 1):
        for i in range(n_cols):
            weights[i].append(lax.ppermute(weights[i][-1], "dp", ring))

    wide32 = hidden_in.astype(jnp.float32)
    gated = (wide32 * norm_gain.astype(jnp.float32)[None, :]).astype(jnp.bfloat16)
    local_sq = jnp.sum(wide32 * wide32, axis=1)
    total_sq = local_sq + lax.ppermute(local_sq, "tensor", over_core)
    inv_rms = lax.rsqrt(total_sq / D + EPSILON)[:, None]

    def piece(dx, dy):
        slabs = []
        for k in range(depth):
            shard = ((z - k + depth) % depth) * 2 + (x ^ dx)
            slabs.append(lax.dynamic_slice_in_dim(gated, shard * rows + (y ^ dy) * part, part, 1))
        return jnp.stack(slabs)

    sent = [piece(1, 1), piece(1, 0), piece(0, 1)]
    held = [
        lax.ppermute(sent[0], ("groups", "dp"), across),
        lax.ppermute(sent[1], "dp", over_x),
        lax.ppermute(sent[2], "groups", over_y),
        piece(0, 0),
    ]
    acts = []
    for h in held:
        acts.append(jnp.concatenate([h, lax.ppermute(h, "tensor", over_core)], axis=2))
    acts = jnp.concatenate(acts, axis=1)

    cosine, sine = angles(tokens)
    positions = jnp.arange(tokens, dtype=jnp.int32)
    prompt = lengths[0, 0]
    total_len = prompt + lengths[0, 1]
    allowed = (positions[None, :] <= positions[:, None]) & (positions[None, :] < total_len)
    keep = ((positions >= prompt - 1) & (positions < total_len - 1)).astype(jnp.float32)[:, None]

    outs = []
    keys = values = None
    for i in range(n_cols):
        partial = sum(
            jnp.dot(acts[k], weights[i][k], preferred_element_type=jnp.float32) for k in range(depth)
        )
        blocks = partial.reshape(4, tokens, HEAD)
        low = blocks[:3].astype(jnp.bfloat16)
        summed = blocks[3]
        summed = summed + lax.ppermute(low[0], ("groups", "dp"), across).astype(jnp.float32)
        summed = summed + lax.ppermute(low[1], "dp", over_x).astype(jnp.float32)
        summed = summed + lax.ppermute(low[2], "groups", over_y).astype(jnp.float32)
        scaled = summed * inv_rms
        if i == 0:
            turned = rotate(scaled, cosine, sine)
            kv = jnp.where(core == 0, turned, scaled).astype(jnp.bfloat16)
            vk = lax.ppermute(kv, "tensor", over_core)
            keys = jnp.where(core == 0, kv, vk)
            values = jnp.where(core == 0, vk, kv)
        else:
            query = rotate(scaled, cosine, sine).astype(jnp.bfloat16)
            outs.append(attend_head(query, keys, values, allowed, keep))
    return jnp.concatenate(outs, axis=1)


VMEM = pltpu.VMEM
PLANE = ((1, 1), (1, 0), (0, 1), (0, 0))
WHOLE = pl.BlockSpec(memory_space=VMEM)
SCALARS = pl.BlockSpec(memory_space=pltpu.SMEM)


def call(kernel, out_shape, limit=12, result=False, **kwargs):
    if not result:
        out_shape = jax.tree.map(lambda s: pltpu.VMEM(s.shape, s.dtype), out_shape)
    return pl.pallas_call(
        kernel,
        out_shape=out_shape,
        compiler_params=pltpu.CompilerParams(vmem_limit_bytes=limit * 2**20),
        cost_estimate=pl.CostEstimate(flops=1, bytes_accessed=1, transcendentals=0),
        **kwargs,
    )


def select_kernel(columns, part, rows_ref, *refs):
    out_refs, sems = refs[:len(columns)], refs[-1]
    rows = pl.ds(pl.multiple_of(lax.axis_index("groups") * part, HEAD), part)
    copies = []
    for starts, out_ref in zip(columns, out_refs):
        at = 0
        while at < len(starts):
            more = 1
            while at + more < len(starts) and starts[at + more] == starts[at] + more * HEAD:
                more += 1
            copies.append(pltpu.make_async_copy(
                rows_ref.at[0, rows, pl.ds(starts[at], more * HEAD)],
                out_ref.at[:, pl.ds(at * HEAD, more * HEAD)],
                sems.at[len(copies)],
            ))
            at += more
    for copy in copies:
        copy.start()
    for copy in copies:
        copy.wait()


def select(projection, part, columns):
    chunk = jax.ShapeDtypeStruct((part, len(columns[0]) * HEAD), projection.dtype)
    out_shape = (chunk,) * len(columns)
    return call(
        functools.partial(select_kernel, columns, part),
        out_shape,
        in_specs=[pl.BlockSpec(memory_space=pltpu.HBM)],
        out_specs=[WHOLE] * len(out_shape),
        scratch_shapes=[pltpu.SemaphoreType.DMA((len(columns) * len(columns[0]),))],
    )(projection)


def gate_kernel(part, depth, hidden_ref, gain_ref, *refs):
    piece_refs, (sq_ref, slab_ref, flat_ref, row_ref, sems) = refs[:4], refs[4:]
    place = lax.axis_index("dp")
    x, z, y = place % 2, place // 2, lax.axis_index("groups")
    wide = 4 * part
    columns = [pl.ds(pl.multiple_of(lax.rem(z - k + depth, depth) * wide, HEAD), wide) for k in range(depth)]
    copies = [pltpu.make_async_copy(hidden_ref.at[:, c], slab_ref.at[k], sems.at[k]) for k, c in enumerate(columns)]
    gain_copy = pltpu.make_async_copy(gain_ref, flat_ref, sems.at[depth])
    gain_copy.start()
    for copy in copies:
        copy.start()
    gain_copy.wait()
    row_ref[0, :] = flat_ref[...].astype(jnp.float32)
    tokens = hidden_ref.shape[0]
    height = 64
    for k, copy in enumerate(copies):
        copy.wait()
        for top in range(0, tokens, height):
            rows = slice(top, top + height)
            total = jnp.zeros((height, HEAD), jnp.float32)
            for piece_ref, (dx, dy) in zip(piece_refs, PLANE):
                start = ((x ^ dx) * 2 + (y ^ dy)) * part
                whole = slab_ref[k, rows, pl.ds(pl.multiple_of(start, HEAD), part)].astype(jnp.float32)
                at = lax.rem(z - k + depth, depth) * wide + start
                gain = row_ref[:, pl.ds(pl.multiple_of(at, HEAD), part)]
                piece_ref[k, rows] = (whole * gain).astype(jnp.bfloat16)
                square = whole * whole
                for j in range(0, part, HEAD):
                    total += square[:, j:j + HEAD]
            sq_ref[rows] = total if k == 0 else sq_ref[rows] + total


def gate(hidden_in, norm_gain, part, depth):
    tokens = hidden_in.shape[0]
    piece = jax.ShapeDtypeStruct((depth, tokens, part), jnp.bfloat16)
    return call(
        functools.partial(gate_kernel, part, depth),
        (piece,) * 4 + (jax.ShapeDtypeStruct((tokens, HEAD), jnp.float32),),
        in_specs=[pl.BlockSpec(memory_space=pltpu.HBM)] * 2,
        out_specs=[WHOLE] * 5,
        scratch_shapes=[
            pltpu.VMEM((depth, tokens, 4 * part), jnp.bfloat16),
            pltpu.VMEM(norm_gain.shape, norm_gain.dtype),
            pltpu.VMEM((1, norm_gain.shape[0]), jnp.float32),
            pltpu.SemaphoreType.DMA((depth + 1,)),
        ],
    )(*(pltpu.with_memory_space_constraint(a, pltpu.HBM) for a in (hidden_in, norm_gain)))


def matmul_kernel(firsts, n_acts, n_more, sent, paired, *refs):
    is_first = lax.axis_index("tensor") == 0
    acts, refs = refs[:n_acts], refs[n_acts:]
    slots, refs = refs[:len(firsts)], refs[len(firsts):]
    more, out_refs = refs[:n_more], refs[n_more:]
    more = [(ref, i) for ref in more for i in range(ref.shape[0])]
    right = [slot[...] for slot in slots]
    wide = 2 * HEAD
    for p in range(n_acts):
        total = jnp.dot(acts[p][firsts[0]], right[0], preferred_element_type=jnp.float32)
        for k in range(1, len(firsts)):
            total += jnp.dot(acts[p][firsts[k]], right[k], preferred_element_type=jnp.float32)
        if more:
            ref, i = more[p]
            total += ref[i]
        if not sent:
            out_refs[0][p] = total
            continue
        theirs_refs, mine_ref = out_refs[:-1], out_refs[-1]
        n_blocks = mine_ref.shape[1]
        per = n_acts * n_blocks // sent
        for g in range(n_blocks):
            at, apart = (g * wide, HEAD) if paired else (g * HEAD, n_blocks * HEAD)
            low = total[:, at:at + HEAD]
            high = total[:, at + apart:at + apart + HEAD]
            spot = p * n_blocks + g
            theirs_refs[spot // per][spot % per] = jnp.where(is_first, high, low).astype(jnp.bfloat16)
            mine_ref[p, g] = jnp.where(is_first, low, high)


def matmul(acts, slots, firsts, so_far=(), sent=0, paired=True):
    n_blocks = slots[0].shape[1] // (2 * HEAD)
    tokens = acts[0].shape[1]
    args = [*acts, *slots, *so_far]
    if sent:
        out_shape = (jax.ShapeDtypeStruct((len(acts) * n_blocks // sent, tokens, HEAD), jnp.bfloat16),) * sent
        out_shape += (jax.ShapeDtypeStruct((len(acts), n_blocks, tokens, HEAD), jnp.float32),)
    else:
        out_shape = (jax.ShapeDtypeStruct((len(acts), tokens, n_blocks * 2 * HEAD), jnp.float32),)
    outs = call(
        functools.partial(matmul_kernel, firsts, len(acts), len(so_far), sent, paired),
        out_shape,
        in_specs=[WHOLE] * len(args),
        out_specs=[WHOLE] * len(out_shape),
    )(*args)
    return outs if sent else outs[0]


def half_kernel(first, swapped, n_acts, skip, *refs):
    acts, (slot_ref, more_ref), out_refs = refs[:n_acts], refs[n_acts:n_acts + 2], refs[n_acts + 2:]
    core = lax.axis_index("tensor")
    width = slot_ref.shape[1] // 2
    where = pl.ds(pl.multiple_of((1 - core if swapped else core) * width, HEAD), width)
    right = slot_ref[:, where]
    n_blocks = width // HEAD
    per = n_acts * n_blocks // len(out_refs)
    for p in range(n_acts):
        total = jnp.dot(acts[p][first], right, preferred_element_type=jnp.float32) + more_ref[skip + p, :, where]
        for g in range(n_blocks):
            spot = p * n_blocks + g
            out_ref = out_refs[spot // per]
            out_ref[spot % per] = total[:, g * HEAD:(g + 1) * HEAD].astype(out_ref.dtype)


def half_matmul(acts, slot, first, so_far, swapped, pieces, dtype, skip=0):
    tokens, width = acts[0].shape[1], slot.shape[1] // 2
    args = [*acts, slot, so_far]
    rows = len(acts) * width // HEAD // pieces
    return call(
        functools.partial(half_kernel, first, swapped, len(acts), skip),
        (jax.ShapeDtypeStruct((rows, tokens, HEAD), dtype),) * pieces,
        in_specs=[WHOLE] * len(args),
        out_specs=[WHOLE] * pieces,
    )(*args)


def join_kernel(n_came, first, mine_ref, *refs):
    came_refs, out_refs = refs[:n_came], refs[n_came:]
    n_blocks = mine_ref.shape[1]
    per = len(out_refs) * n_blocks // n_came
    for p, out_ref in enumerate(out_refs):
        for g in range(n_blocks):
            spot = p * n_blocks + g
            came = came_refs[spot // per][spot % per].astype(jnp.float32)
            out_ref[g] = (mine_ref[first + p, g] + came).astype(out_ref.dtype)


def join(mine, came, types, first=0):
    return call(
        functools.partial(join_kernel, len(came), first),
        tuple(jax.ShapeDtypeStruct(mine.shape[1:], t) for t in types),
        in_specs=[WHOLE] * (1 + len(came)),
        out_specs=[WHOLE] * len(types),
    )(mine, *came)


def tables_kernel(lengths_ref, _, cosine_ref, sine_ref, allowed_ref, keep_ref):
    at = lax.broadcasted_iota(jnp.int32, cosine_ref.shape, 0)
    lane = lax.broadcasted_iota(jnp.int32, cosine_ref.shape, 1)
    pair = lax.rem(lane, HEAD // 2).astype(jnp.float32)
    angle = at.astype(jnp.float32) * jnp.exp(pair * (-2.0 * math.log(ROPE_BASE) / HEAD))
    cosine_ref[...] = jnp.cos(angle)
    sine_ref[...] = jnp.where(lane < HEAD // 2, -jnp.sin(angle), jnp.sin(angle))
    prompt = lengths_ref[0, 0]
    total_len = prompt + lengths_ref[0, 1]
    keep_ref[...] = ((at >= prompt - 1) & (at < total_len - 1)).astype(jnp.float32)
    query_at = lax.broadcasted_iota(jnp.int32, allowed_ref.shape, 0)
    key_at = lax.broadcasted_iota(jnp.int32, allowed_ref.shape, 1)
    allowed_ref[...] = ((key_at <= query_at) & (key_at < total_len)).astype(jnp.float32)


def tables(tokens, lengths, later_than):
    table = jax.ShapeDtypeStruct((tokens, HEAD), jnp.float32)
    allowed = jax.ShapeDtypeStruct((tokens, tokens), jnp.float32)
    return call(
        tables_kernel,
        (table, table, allowed, table),
        in_specs=[SCALARS, pl.BlockSpec(memory_space=pl.ANY)],
        out_specs=[WHOLE] * 4,
    )(lengths, later_than)


def scale_kernel(own_ref, other_ref, out_ref):
    squares = jnp.sum(own_ref[...] + other_ref[...], axis=1, keepdims=True)
    out_ref[...] = jnp.broadcast_to(lax.rsqrt(squares / D + EPSILON), out_ref.shape)


def inv_rms(own, other):
    return call(
        scale_kernel,
        jax.ShapeDtypeStruct(own.shape, jnp.float32),
        in_specs=[WHOLE] * 2,
        out_specs=WHOLE,
    )(own, other)


def summed(refs, index, scale_ref):
    total = refs[0][index]
    for ref in refs[1:]:
        total += ref[index].astype(jnp.float32)
    return total * scale_ref[...]


def turned(block, cosine_ref, sine_ref):
    half = HEAD // 2
    other = jnp.concatenate([block[:, half:], block[:, :half]], axis=1)
    return block * cosine_ref[...] + other * sine_ref[...]


def kv_kernel(own, r0, r1, r2, scale_ref, cosine_ref, sine_ref, out_ref):
    block = summed((own, r0, r1, r2), 0, scale_ref)
    spun = turned(block, cosine_ref, sine_ref)
    out_ref[...] = jnp.where(lax.axis_index("tensor") == 0, spun, block).astype(jnp.bfloat16)


def heads_kernel(first, n_parts, *refs):
    parts, refs = refs[:n_parts], refs[n_parts:]
    scale_ref, cosine_ref, sine_ref, allowed_ref, keep_ref, mine_ref, other_ref, *rest = refs
    earlier_refs, out_ref, scratch = rest[:-1], rest[-1], None
    if len(rest) > 1:
        earlier_ref, out_ref, scratch, sems = rest
        earlier_refs = [earlier_ref]
    copies = []

    def put(source, at):
        where = pl.ds(pl.multiple_of(at, HEAD), HEAD)
        copies.append(pltpu.make_async_copy(source, out_ref.at[:, where], sems.at[len(copies)]))
        copies[-1].start()

    is_key = lax.axis_index("tensor") == 0
    mine, other = mine_ref[...], other_ref[...]
    keys = jnp.where(is_key, mine, other)
    values = jnp.where(is_key, other, mine)
    count = parts[0].shape[0] - first
    before = jnp.where(is_key, HEAD, 0)
    for earlier_ref in earlier_refs:
        put(earlier_ref, jnp.where(is_key, 0, count * HEAD))
    tokens = mine.shape[0]
    query = [turned(summed(parts, first + i, scale_ref), cosine_ref, sine_ref).astype(jnp.bfloat16) for i in range(count)]
    scores = lax.dot_general(
        jnp.concatenate(query, axis=0), keys, (((1,), (1,)), ((), ())), preferred_element_type=jnp.float32
    ) * HEAD ** (-0.5)
    allowed = jnp.concatenate([allowed_ref[...] > 0.0] * count, axis=0)
    scores = jnp.where(allowed, scores, -1e30)
    expo = jnp.exp(scores - jnp.max(scores, axis=-1, keepdims=True))
    attn = (expo * (1.0 / jnp.sum(expo, axis=-1, keepdims=True))).astype(jnp.bfloat16)
    mixed = jnp.dot(attn, values, preferred_element_type=jnp.float32)
    for i in range(count):
        done = (mixed[i * tokens:(i + 1) * tokens] * keep_ref[...]).astype(jnp.bfloat16)
        if scratch is None:
            out_ref[:, i * HEAD:(i + 1) * HEAD] = done
        else:
            scratch[i] = done
            put(scratch.at[i], before + i * HEAD)
    for copy in copies:
        copy.wait()


def heads(parts, first, scale, tabled, mine, other, *earlier):
    args = [*parts, scale, *tabled, mine, other, *earlier]
    tokens = mine.shape[0]
    count = parts[0].shape[0] - first
    out_shape = jax.ShapeDtypeStruct((tokens, count * HEAD + sum(e.shape[1] for e in earlier)), jnp.bfloat16)
    scratch = [pltpu.VMEM((count, tokens, HEAD), jnp.bfloat16), pltpu.SemaphoreType.DMA((count + len(earlier),))]
    return call(
        functools.partial(heads_kernel, first, len(parts)),
        out_shape,
        result=bool(earlier),
        in_specs=[WHOLE] * len(args),
        out_specs=pl.BlockSpec(memory_space=pltpu.HBM) if earlier else WHOLE,
        scratch_shapes=scratch if earlier else [],
    )(*args)


def staged(hidden_in, norm_gain, projection, lengths):
    groups = lax.axis_size("groups")
    dp = lax.axis_size("dp")
    tensor = lax.axis_size("tensor")
    depth = dp // 2
    tokens = hidden_in.shape[0]
    part = projection.shape[1] // groups
    heads_local = QHEADS // tensor

    ring = [(i, (i + 2) % dp) for i in range(dp)]
    over_x = swap(dp)
    over_y = swap(groups)
    over_core = swap(tensor)
    across = [(g * dp + i, (g ^ 1) * dp + (i ^ 1)) for g in range(groups) for i in range(dp)]

    def to_core(a):
        return lax.ppermute(a, "tensor", over_core)

    def on_ring(a):
        return lax.ppermute(a, "dp", ring)

    def back(a):
        return lax.ppermute(a, "dp", [(j, i) for i, j in ring])

    def to_far(a):
        return lax.ppermute(a, ("groups", "dp"), across)

    def to_x(a):
        return lax.ppermute(a, "dp", over_x)

    def to_y(a):
        return lax.ppermute(a, "groups", over_y)

    def to_plane(three):
        return [to_far(three[0]), to_x(three[1]), to_y(three[2])]

    last = []

    def after(*values):
        held = lax.optimization_barrier(tuple(values) + tuple(last))[:len(values)]
        last[:] = held[:1]
        return held[0] if len(values) == 1 else held

    columns = [(QHEADS + c) * HEAD for c in range(tensor)] + [0, (QHEADS - 1) * HEAD]

    def rows_b(projection):
        flat = projection.reshape(projection.shape[1:])
        start = (lax.axis_index("groups") * part, HEAD)
        return lax.dynamic_slice(flat, start, (part, 2 * (heads_local - 1) * HEAD))

    b1 = on_ring(rows_b(projection))
    far, near_x, near_y, own, squares = after(*gate(hidden_in, norm_gain, part, depth))
    near_x = to_x(near_x)
    near_y = to_y(near_y)
    a0, = select(after(projection), part, [columns])
    a0 = after(a0)
    a1 = on_ring(a0)
    other_squares = to_core(squares)
    tabled = after(*tables(tokens, lengths, after(squares)))
    scale = after(inv_rms(squares, after(other_squares)))

    b1, a0, far = after(b1, a0, far)
    a3 = back(a0)
    far = to_far(far)
    a1 = after(a1)
    a2 = on_ring(a1)
    b0 = after(rows_b(after(projection)))
    near_y = after(near_y)
    near_x = after(near_x)
    a3, b1 = after(a3, b1)
    b2 = on_ring(b1)
    early = (near_x, near_y, own)
    front = after(matmul(early, (a0, a1, a3), (0, 1, 3)))
    a2 = after(a2)
    set_a = (a0, a1, a2, a3)

    *theirs, mine = after(*matmul(early, (a2,), (2,), (front,), sent=2))
    swapped = [to_core(t) for t in theirs]
    far, b0 = after(far, b0)
    b3 = back(b0)
    sums_x, sums_y, sums = after(*join(mine, after(*swapped), (jnp.bfloat16, jnp.bfloat16, jnp.float32)))
    sums_x = to_x(sums_x)
    sums_y = to_y(sums_y)
    acts = (far, own, near_x, near_y)
    *theirs, mine = after(*matmul((far,), set_a, (0, 1, 2, 3), sent=1))
    swapped = [to_core(t) for t in theirs]
    b2 = after(b2)
    swapped = [after(t) for t in swapped]
    sums_far = after(*join(mine, swapped, (jnp.bfloat16,)))
    sums_far = to_far(sums_far)
    sums_y = after(sums_y)
    sums_x = after(sums_x)
    front = after(matmul(acts, (b0, b1, b2), (0, 1, 2)))

    b3 = after(b3)
    parts_a = after(sums, sums_far, sums_x, sums_y)
    theirs, = half_matmul(acts[:2], b3, 3, front, True, 1, jnp.bfloat16)
    theirs = after(theirs)
    swapped = [to_core(theirs)]
    theirs, = half_matmul(acts[2:], after(b3), 3, front, True, 1, jnp.bfloat16, 2)
    theirs = after(theirs)
    swapped.append(to_core(theirs))
    mine = []
    for skip in (0, 2):
        total, = half_matmul(acts[skip:skip + 2], after(b3), 3, front, False, 1, jnp.float32, skip)
        mine.append(total.reshape(2, -1, *total.shape[1:]))
    kv = after(call(
        kv_kernel,
        jax.ShapeDtypeStruct((tokens, HEAD), jnp.bfloat16),
        in_specs=[WHOLE] * 7,
        out_specs=WHOLE,
    )(*parts_a, scale, *tabled[:2]))
    vk = to_core(kv)
    sums_far, sums = after(*join(mine[0], (after(swapped[0]),), (jnp.bfloat16, jnp.float32)))
    sums_far = to_far(sums_far)
    sums_x, sums_y = after(*join(mine[1], (after(swapped[1]),), (jnp.bfloat16, jnp.bfloat16)))
    sums_x = to_x(sums_x)
    sums_y = to_y(sums_y)
    vk = after(vk)
    one = after(heads(parts_a, 1, scale, tabled, kv, vk))
    sums_far = after(sums_far)
    sums_x, sums_y = after(sums_x, sums_y)
    return heads((sums, sums_far, sums_x, sums_y), 0, scale, tabled, kv, vk, one)


def local(hidden_in, norm_gain, projection, lengths):
    part = projection.shape[1] // lax.axis_size("groups")
    if lax.axis_size("dp") == 8 and part % HEAD == 0:
        return staged(hidden_in, norm_gain, projection, lengths)
    return general(hidden_in, norm_gain, projection, lengths)


def solution(mesh):
    in_specs = (
        P(("groups", "dp"), "tensor"),
        P("tensor"),
        P("tensor", "dp", None),
        P(("groups", "dp"), None),
    )
    out_specs = P(("groups", "dp"), "tensor")
    return jax.shard_map(local, mesh=mesh, in_specs=in_specs, out_specs=out_specs, check_vma=False)
```

```python
import functools
import math

import jax
import jax.numpy as jnp
from jax import lax
from jax.experimental import pallas as pl
from jax.experimental.pallas import tpu as pltpu
from jax.sharding import PartitionSpec as P

D = 12288
HEAD = 128
QHEADS = 6
ROPE_BASE = 1000000.0
EPSILON = 1e-05


def angles(seq_len):
    half = HEAD // 2
    positions = jnp.arange(seq_len, dtype=jnp.int32)
    freq = ROPE_BASE ** (-(jnp.arange(half, dtype=jnp.float32) * 2.0 / HEAD))
    angle = positions.astype(jnp.float32)[:, None] * freq[None, :]
    return jnp.cos(angle), jnp.sin(angle)


def rotate(block, cosine, sine):
    half = HEAD // 2
    first = block[:, :half]
    second = block[:, half:]
    return jnp.concatenate([first * cosine - second * sine, second * cosine + first * sine], axis=-1)


def attend_head(query, keys, values, allowed, keep):
    scores = lax.dot_general(
        query, keys, (((1,), (1,)), ((), ())), preferred_element_type=jnp.float32
    ) * HEAD ** (-0.5)
    scores = jnp.where(allowed, scores, -1e30)
    largest = jnp.max(scores, axis=-1, keepdims=True)
    expo = jnp.exp(scores - largest)
    attn = (expo / jnp.sum(expo, axis=-1, keepdims=True)).astype(jnp.bfloat16)
    mixed = jnp.dot(attn, values, preferred_element_type=jnp.float32)
    return (mixed * keep).astype(jnp.bfloat16)


def swap(size):
    return [(i, i ^ 1) for i in range(size)]


def general(hidden_in, norm_gain, projection, lengths):
    groups = lax.axis_size("groups")
    dp = lax.axis_size("dp")
    tensor = lax.axis_size("tensor")
    y = lax.axis_index("groups")
    place = lax.axis_index("dp")
    core = lax.axis_index("tensor")
    x = place % 2
    z = place // 2
    depth = dp // 2
    tokens = hidden_in.shape[0]
    rows = projection.shape[1]
    part = rows // groups
    heads_local = QHEADS // tensor

    ring = [(i, (i + 2) % dp) for i in range(dp)]
    over_x = swap(dp)
    over_y = swap(groups)
    over_core = swap(tensor)
    across = [(g * dp + i, (g ^ 1) * dp + (i ^ 1)) for g in range(groups) for i in range(dp)]

    mine = lax.dynamic_slice_in_dim(projection[0], y * part, part, 0)

    def column(owner, index):
        start = (QHEADS + owner) * HEAD if index == 0 else (owner * heads_local + index - 1) * HEAD
        return lax.dynamic_slice_in_dim(mine, start, HEAD, 1)

    n_cols = heads_local + 1
    theirs = jnp.concatenate([column(1 - core, i) for i in range(n_cols)], axis=1)
    other = lax.ppermute(theirs, "tensor", over_core)
    weights = []
    for i in range(n_cols):
        slot = jnp.concatenate([column(core, i), other[:, i * HEAD:(i + 1) * HEAD]], axis=0)
        weights.append([slot])
    for _ in range(depth - 1):
        for i in range(n_cols):
            weights[i].append(lax.ppermute(weights[i][-1], "dp", ring))

    wide32 = hidden_in.astype(jnp.float32)
    gated = (wide32 * norm_gain.astype(jnp.float32)[None, :]).astype(jnp.bfloat16)
    local_sq = jnp.sum(wide32 * wide32, axis=1)
    total_sq = local_sq + lax.ppermute(local_sq, "tensor", over_core)
    inv_rms = lax.rsqrt(total_sq / D + EPSILON)[:, None]

    def piece(dx, dy):
        slabs = []
        for k in range(depth):
            shard = ((z - k + depth) % depth) * 2 + (x ^ dx)
            slabs.append(lax.dynamic_slice_in_dim(gated, shard * rows + (y ^ dy) * part, part, 1))
        return jnp.stack(slabs)

    sent = [piece(1, 1), piece(1, 0), piece(0, 1)]
    held = [
        lax.ppermute(sent[0], ("groups", "dp"), across),
        lax.ppermute(sent[1], "dp", over_x),
        lax.ppermute(sent[2], "groups", over_y),
        piece(0, 0),
    ]
    acts = []
    for h in held:
        acts.append(jnp.concatenate([h, lax.ppermute(h, "tensor", over_core)], axis=2))
    acts = jnp.concatenate(acts, axis=1)

    cosine, sine = angles(tokens)
    positions = jnp.arange(tokens, dtype=jnp.int32)
    prompt = lengths[0, 0]
    total_len = prompt + lengths[0, 1]
    allowed = (positions[None, :] <= positions[:, None]) & (positions[None, :] < total_len)
    keep = ((positions >= prompt - 1) & (positions < total_len - 1)).astype(jnp.float32)[:, None]

    outs = []
    keys = values = None
    for i in range(n_cols):
        partial = sum(
            jnp.dot(acts[k], weights[i][k], preferred_element_type=jnp.float32) for k in range(depth)
        )
        blocks = partial.reshape(4, tokens, HEAD)
        low = blocks[:3].astype(jnp.bfloat16)
        summed = blocks[3]
        summed = summed + lax.ppermute(low[0], ("groups", "dp"), across).astype(jnp.float32)
        summed = summed + lax.ppermute(low[1], "dp", over_x).astype(jnp.float32)
        summed = summed + lax.ppermute(low[2], "groups", over_y).astype(jnp.float32)
        scaled = summed * inv_rms
        if i == 0:
            turned = rotate(scaled, cosine, sine)
            kv = jnp.where(core == 0, turned, scaled).astype(jnp.bfloat16)
            vk = lax.ppermute(kv, "tensor", over_core)
            keys = jnp.where(core == 0, kv, vk)
            values = jnp.where(core == 0, vk, kv)
        else:
            query = rotate(scaled, cosine, sine).astype(jnp.bfloat16)
            outs.append(attend_head(query, keys, values, allowed, keep))
    return jnp.concatenate(outs, axis=1)


VMEM = pltpu.VMEM
PLANE = ((1, 1), (1, 0), (0, 1), (0, 0))
WHOLE = pl.BlockSpec(memory_space=VMEM)
SCALARS = pl.BlockSpec(memory_space=pltpu.SMEM)


def call(kernel, out_shape, limit=12, result=False, **kwargs):
    if not result:
        out_shape = jax.tree.map(lambda s: pltpu.VMEM(s.shape, s.dtype), out_shape)
    return pl.pallas_call(
        kernel,
        out_shape=out_shape,
        compiler_params=pltpu.CompilerParams(vmem_limit_bytes=limit * 2**20),
        cost_estimate=pl.CostEstimate(flops=1, bytes_accessed=1, transcendentals=0),
        **kwargs,
    )


def select_kernel(columns, part, rows_ref, *refs):
    out_refs, sems = refs[:len(columns)], refs[-1]
    rows = pl.ds(pl.multiple_of(lax.axis_index("groups") * part, HEAD), part)
    copies = []
    for starts, out_ref in zip(columns, out_refs):
        at = 0
        while at < len(starts):
            more = 1
            while at + more < len(starts) and starts[at + more] == starts[at] + more * HEAD:
                more += 1
            copies.append(pltpu.make_async_copy(
                rows_ref.at[0, rows, pl.ds(starts[at], more * HEAD)],
                out_ref.at[:, pl.ds(at * HEAD, more * HEAD)],
                sems.at[len(copies)],
            ))
            at += more
    for copy in copies:
        copy.start()
    for copy in copies:
        copy.wait()


def select(projection, part, columns):
    chunk = jax.ShapeDtypeStruct((part, len(columns[0]) * HEAD), projection.dtype)
    out_shape = (chunk,) * len(columns)
    return call(
        functools.partial(select_kernel, columns, part),
        out_shape,
        in_specs=[pl.BlockSpec(memory_space=pltpu.HBM)],
        out_specs=[WHOLE] * len(out_shape),
        scratch_shapes=[pltpu.SemaphoreType.DMA((len(columns) * len(columns[0]),))],
    )(projection)


def gate_kernel(part, depth, hidden_ref, gain_ref, *refs):
    piece_refs, (sq_ref, slab_ref, flat_ref, row_ref, sems) = refs[:4], refs[4:]
    place = lax.axis_index("dp")
    x, z, y = place % 2, place // 2, lax.axis_index("groups")
    wide = 4 * part
    columns = [pl.ds(pl.multiple_of(lax.rem(z - k + depth, depth) * wide, HEAD), wide) for k in range(depth)]
    copies = [pltpu.make_async_copy(hidden_ref.at[:, c], slab_ref.at[k], sems.at[k]) for k, c in enumerate(columns)]
    gain_copy = pltpu.make_async_copy(gain_ref, flat_ref, sems.at[depth])
    gain_copy.start()
    for copy in copies:
        copy.start()
    gain_copy.wait()
    row_ref[0, :] = flat_ref[...].astype(jnp.float32)
    tokens = hidden_ref.shape[0]
    height = 64
    for k, copy in enumerate(copies):
        copy.wait()
        for top in range(0, tokens, height):
            rows = slice(top, top + height)
            total = jnp.zeros((height, HEAD), jnp.float32)
            for piece_ref, (dx, dy) in zip(piece_refs, PLANE):
                start = ((x ^ dx) * 2 + (y ^ dy)) * part
                whole = slab_ref[k, rows, pl.ds(pl.multiple_of(start, HEAD), part)].astype(jnp.float32)
                at = lax.rem(z - k + depth, depth) * wide + start
                gain = row_ref[:, pl.ds(pl.multiple_of(at, HEAD), part)]
                piece_ref[k, rows] = (whole * gain).astype(jnp.bfloat16)
                square = whole * whole
                for j in range(0, part, HEAD):
                    total += square[:, j:j + HEAD]
            sq_ref[rows] = total if k == 0 else sq_ref[rows] + total


def gate(hidden_in, norm_gain, part, depth):
    tokens = hidden_in.shape[0]
    piece = jax.ShapeDtypeStruct((depth, tokens, part), jnp.bfloat16)
    return call(
        functools.partial(gate_kernel, part, depth),
        (piece,) * 4 + (jax.ShapeDtypeStruct((tokens, HEAD), jnp.float32),),
        in_specs=[pl.BlockSpec(memory_space=pltpu.HBM)] * 2,
        out_specs=[WHOLE] * 5,
        scratch_shapes=[
            pltpu.VMEM((depth, tokens, 4 * part), jnp.bfloat16),
            pltpu.VMEM(norm_gain.shape, norm_gain.dtype),
            pltpu.VMEM((1, norm_gain.shape[0]), jnp.float32),
            pltpu.SemaphoreType.DMA((depth + 1,)),
        ],
    )(*(pltpu.with_memory_space_constraint(a, pltpu.HBM) for a in (hidden_in, norm_gain)))


def matmul_kernel(firsts, n_acts, n_more, sent, paired, *refs):
    is_first = lax.axis_index("tensor") == 0
    acts, refs = refs[:n_acts], refs[n_acts:]
    slots, refs = refs[:len(firsts)], refs[len(firsts):]
    more, out_refs = refs[:n_more], refs[n_more:]
    more = [(ref, i) for ref in more for i in range(ref.shape[0])]
    right = [slot[...] for slot in slots]
    wide = 2 * HEAD
    for p in range(n_acts):
        total = jnp.dot(acts[p][firsts[0]], right[0], preferred_element_type=jnp.float32)
        for k in range(1, len(firsts)):
            total += jnp.dot(acts[p][firsts[k]], right[k], preferred_element_type=jnp.float32)
        if more:
            ref, i = more[p]
            total += ref[i]
        if not sent:
            out_refs[0][p] = total
            continue
        theirs_refs, mine_ref = out_refs[:-1], out_refs[-1]
        n_blocks = mine_ref.shape[1]
        per = n_acts * n_blocks // sent
        for g in range(n_blocks):
            at, apart = (g * wide, HEAD) if paired else (g * HEAD, n_blocks * HEAD)
            low = total[:, at:at + HEAD]
            high = total[:, at + apart:at + apart + HEAD]
            spot = p * n_blocks + g
            theirs_refs[spot // per][spot % per] = jnp.where(is_first, high, low).astype(jnp.bfloat16)
            mine_ref[p, g] = jnp.where(is_first, low, high)


def matmul(acts, slots, firsts, so_far=(), sent=0, paired=True):
    n_blocks = slots[0].shape[1] // (2 * HEAD)
    tokens = acts[0].shape[1]
    args = [*acts, *slots, *so_far]
    if sent:
        out_shape = (jax.ShapeDtypeStruct((len(acts) * n_blocks // sent, tokens, HEAD), jnp.bfloat16),) * sent
        out_shape += (jax.ShapeDtypeStruct((len(acts), n_blocks, tokens, HEAD), jnp.float32),)
    else:
        out_shape = (jax.ShapeDtypeStruct((len(acts), tokens, n_blocks * 2 * HEAD), jnp.float32),)
    outs = call(
        functools.partial(matmul_kernel, firsts, len(acts), len(so_far), sent, paired),
        out_shape,
        in_specs=[WHOLE] * len(args),
        out_specs=[WHOLE] * len(out_shape),
    )(*args)
    return outs if sent else outs[0]


def half_kernel(first, swapped, n_acts, skip, *refs):
    acts, (slot_ref, more_ref), out_refs = refs[:n_acts], refs[n_acts:n_acts + 2], refs[n_acts + 2:]
    core = lax.axis_index("tensor")
    width = slot_ref.shape[1] // 2
    where = pl.ds(pl.multiple_of((1 - core if swapped else core) * width, HEAD), width)
    right = slot_ref[:, where]
    n_blocks = width // HEAD
    per = n_acts * n_blocks // len(out_refs)
    for p in range(n_acts):
        total = jnp.dot(acts[p][first], right, preferred_element_type=jnp.float32) + more_ref[skip + p, :, where]
        for g in range(n_blocks):
            spot = p * n_blocks + g
            out_ref = out_refs[spot // per]
            out_ref[spot % per] = total[:, g * HEAD:(g + 1) * HEAD].astype(out_ref.dtype)


def half_matmul(acts, slot, first, so_far, swapped, pieces, dtype, skip=0):
    tokens, width = acts[0].shape[1], slot.shape[1] // 2
    args = [*acts, slot, so_far]
    rows = len(acts) * width // HEAD // pieces
    return call(
        functools.partial(half_kernel, first, swapped, len(acts), skip),
        (jax.ShapeDtypeStruct((rows, tokens, HEAD), dtype),) * pieces,
        in_specs=[WHOLE] * len(args),
        out_specs=[WHOLE] * pieces,
    )(*args)


def join_kernel(n_came, first, mine_ref, *refs):
    came_refs, out_refs = refs[:n_came], refs[n_came:]
    n_blocks = mine_ref.shape[1]
    per = len(out_refs) * n_blocks // n_came
    for p, out_ref in enumerate(out_refs):
        for g in range(n_blocks):
            spot = p * n_blocks + g
            came = came_refs[spot // per][spot % per].astype(jnp.float32)
            out_ref[g] = (mine_ref[first + p, g] + came).astype(out_ref.dtype)


def join(mine, came, types, first=0):
    return call(
        functools.partial(join_kernel, len(came), first),
        tuple(jax.ShapeDtypeStruct(mine.shape[1:], t) for t in types),
        in_specs=[WHOLE] * (1 + len(came)),
        out_specs=[WHOLE] * len(types),
    )(mine, *came)


def tables_kernel(lengths_ref, _, cosine_ref, sine_ref, allowed_ref, keep_ref):
    at = lax.broadcasted_iota(jnp.int32, cosine_ref.shape, 0)
    lane = lax.broadcasted_iota(jnp.int32, cosine_ref.shape, 1)
    pair = lax.rem(lane, HEAD // 2).astype(jnp.float32)
    angle = at.astype(jnp.float32) * jnp.exp(pair * (-2.0 * math.log(ROPE_BASE) / HEAD))
    cosine_ref[...] = jnp.cos(angle)
    sine_ref[...] = jnp.where(lane < HEAD // 2, -jnp.sin(angle), jnp.sin(angle))
    prompt = lengths_ref[0, 0]
    total_len = prompt + lengths_ref[0, 1]
    keep_ref[...] = ((at >= prompt - 1) & (at < total_len - 1)).astype(jnp.float32)
    query_at = lax.broadcasted_iota(jnp.int32, allowed_ref.shape, 0)
    key_at = lax.broadcasted_iota(jnp.int32, allowed_ref.shape, 1)
    allowed_ref[...] = ((key_at <= query_at) & (key_at < total_len)).astype(jnp.float32)


def tables(tokens, lengths, later_than):
    table = jax.ShapeDtypeStruct((tokens, HEAD), jnp.float32)
    allowed = jax.ShapeDtypeStruct((tokens, tokens), jnp.float32)
    return call(
        tables_kernel,
        (table, table, allowed, table),
        in_specs=[SCALARS, pl.BlockSpec(memory_space=pl.ANY)],
        out_specs=[WHOLE] * 4,
    )(lengths, later_than)


def scale_kernel(own_ref, other_ref, out_ref):
    squares = jnp.sum(own_ref[...] + other_ref[...], axis=1, keepdims=True)
    out_ref[...] = jnp.broadcast_to(lax.rsqrt(squares / D + EPSILON), out_ref.shape)


def inv_rms(own, other):
    return call(
        scale_kernel,
        jax.ShapeDtypeStruct(own.shape, jnp.float32),
        in_specs=[WHOLE] * 2,
        out_specs=WHOLE,
    )(own, other)


def summed(refs, index, scale_ref):
    total = refs[0][index]
    for ref in refs[1:]:
        total += ref[index].astype(jnp.float32)
    return total * scale_ref[...]


def turned(block, cosine_ref, sine_ref):
    half = HEAD // 2
    other = jnp.concatenate([block[:, half:], block[:, :half]], axis=1)
    return block * cosine_ref[...] + other * sine_ref[...]


def kv_kernel(own, r0, r1, r2, scale_ref, cosine_ref, sine_ref, out_ref):
    block = summed((own, r0, r1, r2), 0, scale_ref)
    spun = turned(block, cosine_ref, sine_ref)
    out_ref[...] = jnp.where(lax.axis_index("tensor") == 0, spun, block).astype(jnp.bfloat16)


def heads_kernel(first, n_parts, *refs):
    parts, refs = refs[:n_parts], refs[n_parts:]
    scale_ref, cosine_ref, sine_ref, allowed_ref, keep_ref, mine_ref, other_ref, *rest = refs
    earlier_refs, out_ref, scratch = rest[:-1], rest[-1], None
    if len(rest) > 1:
        earlier_ref, out_ref, scratch, sems = rest
        earlier_refs = [earlier_ref]
    copies = []

    def put(source, at):
        where = pl.ds(pl.multiple_of(at, HEAD), HEAD)
        copies.append(pltpu.make_async_copy(source, out_ref.at[:, where], sems.at[len(copies)]))
        copies[-1].start()

    is_key = lax.axis_index("tensor") == 0
    mine, other = mine_ref[...], other_ref[...]
    keys = jnp.where(is_key, mine, other)
    values = jnp.where(is_key, other, mine)
    count = parts[0].shape[0] - first
    before = jnp.where(is_key, HEAD, 0)
    for earlier_ref in earlier_refs:
        put(earlier_ref, jnp.where(is_key, 0, count * HEAD))
    tokens = mine.shape[0]
    query = [turned(summed(parts, first + i, scale_ref), cosine_ref, sine_ref).astype(jnp.bfloat16) for i in range(count)]
    scores = lax.dot_general(
        jnp.concatenate(query, axis=0), keys, (((1,), (1,)), ((), ())), preferred_element_type=jnp.float32
    ) * HEAD ** (-0.5)
    allowed = jnp.concatenate([allowed_ref[...] > 0.0] * count, axis=0)
    scores = jnp.where(allowed, scores, -1e30)
    expo = jnp.exp(scores - jnp.max(scores, axis=-1, keepdims=True))
    attn = (expo * (1.0 / jnp.sum(expo, axis=-1, keepdims=True))).astype(jnp.bfloat16)
    mixed = jnp.dot(attn, values, preferred_element_type=jnp.float32)
    for i in range(count):
        done = (mixed[i * tokens:(i + 1) * tokens] * keep_ref[...]).astype(jnp.bfloat16)
        if scratch is None:
            out_ref[:, i * HEAD:(i + 1) * HEAD] = done
        else:
            scratch[i] = done
            put(scratch.at[i], before + i * HEAD)
    for copy in copies:
        copy.wait()


def heads(parts, first, scale, tabled, mine, other, *earlier):
    args = [*parts, scale, *tabled, mine, other, *earlier]
    tokens = mine.shape[0]
    count = parts[0].shape[0] - first
    out_shape = jax.ShapeDtypeStruct((tokens, count * HEAD + sum(e.shape[1] for e in earlier)), jnp.bfloat16)
    scratch = [pltpu.VMEM((count, tokens, HEAD), jnp.bfloat16), pltpu.SemaphoreType.DMA((count + len(earlier),))]
    return call(
        functools.partial(heads_kernel, first, len(parts)),
        out_shape,
        result=bool(earlier),
        in_specs=[WHOLE] * len(args),
        out_specs=pl.BlockSpec(memory_space=pltpu.HBM) if earlier else WHOLE,
        scratch_shapes=scratch if earlier else [],
    )(*args)


def staged(hidden_in, norm_gain, projection, lengths):
    groups = lax.axis_size("groups")
    dp = lax.axis_size("dp")
    tensor = lax.axis_size("tensor")
    depth = dp // 2
    tokens = hidden_in.shape[0]
    part = projection.shape[1] // groups
    heads_local = QHEADS // tensor

    ring = [(i, (i + 2) % dp) for i in range(dp)]
    over_x = swap(dp)
    over_y = swap(groups)
    over_core = swap(tensor)
    across = [(g * dp + i, (g ^ 1) * dp + (i ^ 1)) for g in range(groups) for i in range(dp)]

    def to_core(a):
        return lax.ppermute(a, "tensor", over_core)

    def on_ring(a):
        return lax.ppermute(a, "dp", ring)

    def back(a):
        return lax.ppermute(a, "dp", [(j, i) for i, j in ring])

    def to_far(a):
        return lax.ppermute(a, ("groups", "dp"), across)

    def to_x(a):
        return lax.ppermute(a, "dp", over_x)

    def to_y(a):
        return lax.ppermute(a, "groups", over_y)

    def to_plane(three):
        return [to_far(three[0]), to_x(three[1]), to_y(three[2])]

    last = []

    def after(*values):
        held = lax.optimization_barrier(tuple(values) + tuple(last))[:len(values)]
        last[:] = held[:1]
        return held[0] if len(values) == 1 else held

    columns = [(QHEADS + c) * HEAD for c in range(tensor)] + [0, (QHEADS - 1) * HEAD]

    def rows_b(projection):
        flat = projection.reshape(projection.shape[1:])
        start = (lax.axis_index("groups") * part, HEAD)
        return lax.dynamic_slice(flat, start, (part, 2 * (heads_local - 1) * HEAD))

    b1 = on_ring(rows_b(projection))
    far, near_x, near_y, own, squares = after(*gate(hidden_in, norm_gain, part, depth))
    near_x = to_x(near_x)
    near_y = to_y(near_y)
    a0, = select(after(projection), part, [columns])
    a0 = after(a0)
    a1 = on_ring(a0)
    other_squares = to_core(squares)
    tabled = after(*tables(tokens, lengths, after(squares)))
    scale = after(inv_rms(squares, after(other_squares)))

    b1, a0, far = after(b1, a0, far)
    a3 = back(a0)
    far = to_far(far)
    a1 = after(a1)
    a2 = on_ring(a1)
    b0 = after(rows_b(after(projection)))
    near_y = after(near_y)
    near_x = after(near_x)
    a3, b1 = after(a3, b1)
    b2 = on_ring(b1)
    early = (near_x, near_y, own)
    front = after(matmul(early, (a0, a1, a3), (0, 1, 3)))
    a2 = after(a2)
    set_a = (a0, a1, a2, a3)

    *theirs, mine = after(*matmul(early, (a2,), (2,), (front,), sent=2))
    swapped = [to_core(t) for t in theirs]
    far, b0 = after(far, b0)
    b3 = back(b0)
    sums_x, sums_y, sums = after(*join(mine, after(*swapped), (jnp.bfloat16, jnp.bfloat16, jnp.float32)))
    sums_x = to_x(sums_x)
    sums_y = to_y(sums_y)
    acts = (far, own, near_x, near_y)
    *theirs, mine = after(*matmul((far,), set_a, (0, 1, 2, 3), sent=1))
    swapped = [to_core(t) for t in theirs]
    b2 = after(b2)
    swapped = [after(t) for t in swapped]
    sums_far = after(*join(mine, swapped, (jnp.bfloat16,)))
    sums_far = to_far(sums_far)
    sums_y = after(sums_y)
    sums_x = after(sums_x)
    front = after(matmul(acts, (b0, b1, b2), (0, 1, 2)))

    b3 = after(b3)
    parts_a = after(sums, sums_far, sums_x, sums_y)
    theirs, = half_matmul(acts[:2], b3, 3, front, True, 1, jnp.bfloat16)
    theirs = after(theirs)
    swapped = [to_core(theirs)]
    theirs, = half_matmul(acts[2:], after(b3), 3, front, True, 1, jnp.bfloat16, 2)
    theirs = after(theirs)
    swapped.append(to_core(theirs))
    mine = []
    for skip in (0, 2):
        total, = half_matmul(acts[skip:skip + 2], after(b3), 3, front, False, 1, jnp.float32, skip)
        mine.append(total.reshape(2, -1, *total.shape[1:]))
    sums_far, sums = after(*join(mine[0], (after(swapped[0]),), (jnp.bfloat16, jnp.float32)))
    sums_far = to_far(sums_far)
    kv = after(call(
        kv_kernel,
        jax.ShapeDtypeStruct((tokens, HEAD), jnp.bfloat16),
        in_specs=[WHOLE] * 7,
        out_specs=WHOLE,
    )(*parts_a, scale, *tabled[:2]))
    vk = to_core(kv)
    sums_x, sums_y = after(*join(mine[1], (after(swapped[1]),), (jnp.bfloat16, jnp.bfloat16)))
    sums_x = to_x(sums_x)
    sums_y = to_y(sums_y)
    vk = after(vk)
    one = after(heads(parts_a, 1, scale, tabled, kv, vk))
    sums_far = after(sums_far)
    sums_x, sums_y = after(sums_x, sums_y)
    return heads((sums, sums_far, sums_x, sums_y), 0, scale, tabled, kv, vk, one)


def local(hidden_in, norm_gain, projection, lengths):
    part = projection.shape[1] // lax.axis_size("groups")
    if lax.axis_size("dp") == 8 and part % HEAD == 0:
        return staged(hidden_in, norm_gain, projection, lengths)
    return general(hidden_in, norm_gain, projection, lengths)


def solution(mesh):
    in_specs = (
        P(("groups", "dp"), "tensor"),
        P("tensor"),
        P("tensor", "dp", None),
        P(("groups", "dp"), None),
    )
    out_specs = P(("groups", "dp"), "tensor")
    return jax.shard_map(local, mesh=mesh, in_specs=in_specs, out_specs=out_specs, check_vma=False)
```
